32 devices in a mesh: seq: 8 (over z, y), exp: 4 (over x, core).
Axes of the slice: x: 2, y: 2, z: 4, core: 2. Of those that a mesh axis runs over, the one named last changes fastest.
Arguments:
- residual_in: bfloat16 [4096, 2048], P(('seq', 'exp')), may hold values from -6 to 6
- query_input: bfloat16 [4096, 1024], P(('seq', 'exp')), may hold values from -6 to 6
- key_input: bfloat16 [4096, 1024], P(('seq', 'exp')), may hold values from -6 to 6
- value_input: bfloat16 [4096, 2048], P(('seq', 'exp')), may hold values from -6 to 6
- out_gate: bfloat16 [4096, 2048], P(('seq', 'exp')), may hold values from -6 to 6
- write_strength: float32 [4096, 16], P(('seq', 'exp')), may hold values from 0 to 2
- decay_rate: float32 [4096, 16], P(('seq', 'exp')), may hold values from 0 to 1
- head_gain: float32 [128], replicated, may hold values from 0.1 to 1.9
- out_proj: bfloat16 [2048, 2048], P(None, 'exp'), may hold values from -0.125 to 0.125
- post_gain: float32 [2048], replicated, may hold values from 0.1 to 1.9
- expert_ids: int32 [4096, 10], P(('seq', 'exp')), may hold values from 0 to 63, all different within a row; in each aligned block of 128 rows (0 to 127, 128 to 255, ...) at most 32 rows name the same one
- gate_weights: float32 [4096, 10], P(('seq', 'exp')), may hold values from 0.05 to 0.3
- expert_gate: bfloat16 [64, 2048, 512], P(('seq', 'exp')), may hold values from -0.125 to 0.125
- expert_up: bfloat16 [64, 2048, 512], P(('seq', 'exp')), may hold values from -0.125 to 0.125
- expert_down: bfloat16 [64, 512, 2048], P(('seq', 'exp')), may hold values from -0.25 to 0.25
Outputs:
- layer_out: bfloat16 [4096, 2048], P(('seq', 'exp'))
The draws below stay inside these ranges and needn't reach their ends.
Inputs may be any that keep to these rules, and one draw needn't show every extreme that they name: `expert_ids`: each row names 10 different experts. Within the rows of one device (aligned blocks of 128 rows) no expert is named more than 32 times, and in every draw some expert is named exactly 32 times within one device's rows.
All inputs are finite; a program needn't handle non-finite values.
Results may differ from the reference program's by a relative error of at most 0.011.
Values may be sent and summed in bfloat16 or wider, within the bound.
No kernel may reach another device: no remote copies, remote signals or barrier semaphores. Data moves between devices by JAX's collectives and lax.ppermute only.
A program may use at most 256 MiB of HBM per device.

```python
import math
from functools import partial
import jax
import jax.numpy as jnp
import numpy as np
from jax import lax

D = 2048
HK = 8
GROUP_VALUE_HEADS = 16
DK = 128
DV = 128
CH = 64
FFE = 512
TOP = 10
EXP_DEV = 2
TOK_DEV = 128
SEQUENCE_TOKENS = 4096
EXPERTS = 64
CAP = 32


def slow_heads(key):
    order_key, count_key = jax.random.split(jax.random.fold_in(key, 101))
    order = jax.random.permutation(order_key, GROUP_VALUE_HEADS)
    count = jax.random.randint(count_key, (), GROUP_VALUE_HEADS // 2, 3 * GROUP_VALUE_HEADS // 4 + 1)
    return order < count


def draw_decay_rate(key, part):
    slow = slow_heads(key)
    every_key = jax.random.split(jax.random.fold_in(key, 303), 6)
    slow_rate = jnp.exp(jax.random.uniform(every_key[0], (GROUP_VALUE_HEADS,), minval=math.log(0.03), maxval=math.log(0.3))) / SEQUENCE_TOKENS
    fast_rate = jnp.exp(jax.random.uniform(every_key[1], (GROUP_VALUE_HEADS,), minval=math.log(1.0 / 50.0), maxval=math.log(1.0 / 30.0)))
    starting_point = jnp.where(slow, slow_rate, fast_rate)
    device_multiplier = jnp.exp(jax.random.uniform(every_key[2], (SEQUENCE_TOKENS // TOK_DEV, GROUP_VALUE_HEADS), minval=math.log(0.5), maxval=math.log(2.0)))
    device_multiplier = jnp.repeat(device_multiplier, TOK_DEV, axis=0)
    coarse_guess = jnp.exp(jax.random.uniform(every_key[3], (SEQUENCE_TOKENS, GROUP_VALUE_HEADS), minval=math.log(0.5), maxval=math.log(2.0)))
    spots = jax.random.randint(every_key[4], (3,), 0, SEQUENCE_TOKENS)
    removed_part = jnp.any(jnp.arange(SEQUENCE_TOKENS)[:, None] == spots[None, :], axis=1)
    sudden_jump = jax.random.uniform(every_key[5], (SEQUENCE_TOKENS, GROUP_VALUE_HEADS), minval=0.22, maxval=0.4)
    return starting_point[None, :] * device_multiplier * coarse_guess + jnp.where(removed_part[:, None], sudden_jump, 0.0)


def draw_write_strength(key, part):
    slow = slow_heads(key)
    small_key, large_key = jax.random.split(jax.random.fold_in(key, 202))
    small = jnp.exp(jax.random.uniform(small_key, (SEQUENCE_TOKENS, GROUP_VALUE_HEADS), minval=math.log(0.25), maxval=math.log(1.0)))
    large = jax.random.uniform(large_key, (SEQUENCE_TOKENS, GROUP_VALUE_HEADS), minval=0.2, maxval=0.9)
    return jnp.where(slow[None, :], 2.0 - small * DK / SEQUENCE_TOKENS, large)


def block_levels(stream_key, dims, shards, smallest, top_value):
    def one(position, blocks):
        steps = jax.random.uniform(jax.random.fold_in(jax.random.fold_in(stream_key, 6), position), (blocks,), jnp.float32, smallest / len(shards), top_value / len(shards))
        return jnp.repeat(jnp.exp(steps), dims[position] // blocks).reshape((-1,) + (1,) * (len(dims) - position - 1))

    factor_of = one(*shards[0])
    for cut in shards[1:]:
        factor_of = factor_of * one(*cut)
    return factor_of


def deal_out(key, own, number, rows, amount, top, most, skew):
    order = jax.random.permutation(key, amount)
    crowded, usual = shares(amount, rows * top, most, skew, True), shares(amount, rows * top, most, skew, False)
    places = jnp.arange(amount)

    def named(lengths, turn):
        used = int((lengths > 0).sum())
        fixed = max(1, used // 4)
        shifted = fixed + (places - fixed + turn * (used - fixed)) % max(1, amount - fixed)
        return jnp.zeros((amount,), jnp.int32).at[order[jnp.where(places < fixed, places, shifted)]].set(jnp.asarray(lengths, jnp.int32))

    lengths = jnp.where(number % 4 == 0, named(crowded, number // 4), named(usual, number - number // 4 - 1))
    mixed = jax.random.permutation(jax.random.fold_in(own, 3), amount)
    donor, receiver = mixed[0:amount // 2 * 2:2], mixed[1:amount // 2 * 2:2]
    margin = jnp.minimum(lengths[donor] - 1, most - lengths[receiver]) // 2
    margin = jnp.where((donor == order[0]) | (receiver == order[0]) | (lengths[receiver] == 0), 0, jnp.maximum(margin, 0))
    shifted = jax.random.randint(jax.random.fold_in(own, 4), (amount // 2,), 0, 1 << 20) % (margin + 1)
    lengths = lengths.at[donor].add(-shifted).at[receiver].add(shifted)
    members = jnp.searchsorted(jnp.cumsum(lengths), jnp.arange(rows * top), side="right").astype(jnp.int32)
    table = members.reshape(top, rows).T
    table = table[jax.random.permutation(jax.random.fold_in(own, 1), rows)]
    turn = jax.random.randint(jax.random.fold_in(own, 2), (rows, 1), 0, top)
    return jnp.take_along_axis(table, (jnp.arange(top)[None, :] + turn) % top, axis=1)


def shares(amount, total, limit, slope, full):
    weights = [(1 << 20) // math.isqrt(grade ** slope) + 1 for grade in range(1, amount + 1)]
    largest = limit if full else min(limit, max(-(-total // amount), total * weights[0] // sum(weights)))
    least = 1 if total - largest >= amount - 1 else 0
    given, surplus = [largest] + [least] * (amount - 1), total - largest - least * (amount - 1)
    while surplus > 0:
        free = [i for i in range(1, amount) if given[i] < largest] or [i for i in range(1, amount) if given[i] < limit]
        mass, left = sum([weights[i] for i in free]), surplus
        for i in free:
            more = min(limit - given[i], max(1, left * weights[i] // mass), surplus)
            given[i] = given[i] + more
            surplus = surplus - more
    return np.array(given)


def bell_draw(key, extent, scale, bound, cuts=(), held_as=jnp.bfloat16):
    factor_of = block_levels(key, extent, cuts, -0.22, 0.18) if cuts else 1.0
    values = jax.random.normal(key, extent, jnp.float32) * scale * factor_of
    return jnp.minimum(jnp.maximum(values, -bound), bound).astype(held_as)


def setup_inputs(seed: int = 0) -> dict:
    keys = jax.random.split(jax.random.key(seed), 16)
    residual_in = bell_draw(keys[0], (SEQUENCE_TOKENS, D), 1.0, 6.0, ((0, 32),))
    query_input = bell_draw(keys[1], (SEQUENCE_TOKENS, HK * DK), 1.0, 6.0, ((0, 32),))
    key_input = bell_draw(keys[2], (SEQUENCE_TOKENS, HK * DK), 1.0, 6.0, ((0, 32),))
    value_input = bell_draw(keys[3], (SEQUENCE_TOKENS, GROUP_VALUE_HEADS * DV), 1.0, 6.0, ((0, 32),))
    out_gate = bell_draw(keys[4], (SEQUENCE_TOKENS, GROUP_VALUE_HEADS * DV), 1.0, 6.0, ((0, 32),))
    write_strength = draw_write_strength(jax.random.fold_in(keys[15], 71), 0)
    decay_rate = draw_decay_rate(jax.random.fold_in(keys[15], 71), 0)
    head_gain = jnp.clip(1.0 + 0.18 * jax.random.normal(keys[7], (DV,), jnp.float32), 0.1, 1.9)
    out_proj = bell_draw(keys[8], (GROUP_VALUE_HEADS * DV, D), (GROUP_VALUE_HEADS * DV) ** -0.5, 0.125, ((1, 4),))
    post_gain = jnp.clip(1.0 + 0.18 * jax.random.normal(keys[9], (D,), jnp.float32), 0.1, 1.9)
    expert_ids_keys = jax.random.split(jax.random.fold_in(keys[10], 1), SEQUENCE_TOKENS // TOK_DEV)
    expert_ids_turns = jax.random.permutation(jax.random.fold_in(keys[10], 3), SEQUENCE_TOKENS // TOK_DEV)
    expert_ids = jax.vmap(lambda own, number: deal_out(jax.random.fold_in(keys[10], 2), own, number, TOK_DEV, EXPERTS, TOP, CAP, 2))(expert_ids_keys, expert_ids_turns).reshape((SEQUENCE_TOKENS, TOP))
    gate_weights = jnp.clip(0.05 + 0.25 * jax.random.uniform(keys[11], (SEQUENCE_TOKENS, TOP), jnp.float32) ** block_levels(keys[11], (SEQUENCE_TOKENS, TOP), ((0, 32),), -0.2, 0.2), 0.05, 0.3)
    expert_gate = bell_draw(keys[12], (EXPERTS, D, FFE), D ** -0.5, 0.125, ((0, 32),))
    expert_up = bell_draw(keys[13], (EXPERTS, D, FFE), D ** -0.5, 0.125, ((0, 32),))
    expert_down = bell_draw(keys[14], (EXPERTS, FFE, D), FFE ** -0.5, 0.25, ((0, 32),))
    return {"residual_in": residual_in, "query_input": query_input, "key_input": key_input, "value_input": value_input, "out_gate": out_gate, "write_strength": write_strength, "decay_rate": decay_rate, "head_gain": head_gain, "out_proj": out_proj, "post_gain": post_gain, "expert_ids": expert_ids, "gate_weights": gate_weights, "expert_gate": expert_gate, "expert_up": expert_up, "expert_down": expert_down}


largest_value = lax.Precision.HIGHEST

def unit_rows(block):
    return block * lax.rsqrt(lax.optimization_barrier(jnp.sum(block * block, axis=-1, keepdims=True)) + 1e-06)

def block_terms(query_block, key_block, value_block, strength, rate):
    block_len = key_block.shape[1]
    width = key_block.shape[2]
    logs = jnp.cumsum(-rate, axis=1)
    log_gap = logs[:, :, None] - logs[:, None, :]
    row_ids = jnp.arange(block_len)[:, None]
    column_ids = jnp.arange(block_len)[None, :]
    inclusive = (row_ids >= column_ids)[None]
    strict = (row_ids > column_ids)[None]
    ratio = jnp.where(inclusive, jnp.exp(jnp.where(inclusive, log_gap, 0.0)), 0.0)
    key_gram = jnp.einsum('htd,hsd->hts', key_block, key_block, precision=largest_value)
    system = jnp.where(strict, ratio * key_gram, 0.0) * strength[:, :, None] + jnp.eye(block_len, dtype=jnp.float32)
    growth = jnp.exp(logs)
    newest_value = jax.scipy.linalg.solve_triangular(system, strength[:, :, None] * value_block, lower=True, unit_diagonal=True)
    key_matrix = jax.scipy.linalg.solve_triangular(system, (strength * growth)[:, :, None] * key_block, lower=True, unit_diagonal=True)
    mixed_query = ratio * jnp.einsum('htd,hsd->hts', query_block, key_block, precision=largest_value)
    faded_key = key_block * jnp.exp(logs[:, -1:] - logs)[:, :, None]
    transition_matrix = growth[:, -1][:, None, None] * jnp.eye(width, dtype=jnp.float32) - jnp.einsum('hck,hcj->hkj', faded_key, key_matrix, precision=largest_value)
    increment_term = jnp.einsum('btx,btw->bxw', faded_key, newest_value, precision=largest_value)
    return (query_block * growth[:, :, None], mixed_query, newest_value, key_matrix, transition_matrix, increment_term)

def block_output(passed_state, rescaled_query, mixed_query, newest_value, key_matrix):
    state_update = newest_value - jnp.einsum('lxw,lwp->lxp', key_matrix, passed_state, precision=largest_value)
    return jnp.einsum('lxw,lwp->lxp', rescaled_query, passed_state, precision=largest_value) + jnp.einsum('xib,xbp->xip', mixed_query, state_update, precision=largest_value)

def prepare(query_input, key_input, value_input, write_strength, decay_rate):
    tok_rows = key_input.shape[0]
    blocks_here = tok_rows // CH
    head_group = GROUP_VALUE_HEADS // HK
    query_unit = unit_rows(query_input.reshape(tok_rows, HK, DK).astype(jnp.float32)) * DK ** (-0.5)
    key_unit = unit_rows(key_input.reshape(tok_rows, HK, DK).astype(jnp.float32))
    query_unit = jnp.repeat(query_unit, head_group, axis=1)
    key_unit = jnp.repeat(key_unit, head_group, axis=1)
    value_heads = value_input.reshape(tok_rows, GROUP_VALUE_HEADS, DV).astype(jnp.float32)

    def blocked(array):
        shaped = array.reshape((blocks_here, CH) + array.shape[1:])
        return jnp.swapaxes(shaped, 1, 2)
    return jax.vmap(block_terms)(blocked(query_unit), blocked(key_unit), blocked(value_heads), blocked(write_strength), blocked(decay_rate))

def finish_core(outputs, out_gate, head_gain):
    tok_rows = out_gate.shape[0]
    recurrent = jnp.swapaxes(outputs, 1, 2).reshape(tok_rows, GROUP_VALUE_HEADS, DV)
    inv_rms = lax.rsqrt(lax.optimization_barrier(jnp.mean(recurrent * recurrent, axis=2, keepdims=True)) + 1e-06)
    gate_act = jax.nn.silu(out_gate.reshape(tok_rows, GROUP_VALUE_HEADS, DV).astype(jnp.float32))
    return (recurrent * inv_rms * head_gain * gate_act).astype(jnp.bfloat16).reshape(tok_rows, GROUP_VALUE_HEADS * DV)

def post_norm(hidden_state, post_gain):
    widened = hidden_state.astype(jnp.float32)
    return (widened * lax.rsqrt(lax.optimization_barrier(jnp.mean(widened * widened, axis=1, keepdims=True)) + 1e-06) * post_gain).astype(jnp.bfloat16)

def slot_index(expert_ids, experts, capacity):
    flat_ids = expert_ids.reshape(-1)
    onehot = (flat_ids[:, None] == jnp.arange(experts, dtype=jnp.int32)[None, :]).astype(jnp.int32)
    before = jnp.cumsum(onehot, axis=0) - onehot
    return (flat_ids * capacity + lax.optimization_barrier(jnp.sum(before * onehot, axis=1))).astype(jnp.int32)

def expert_rows(block, weight_gate, weight_up, weight_down):
    gate_part = jnp.dot(block.astype(jnp.float32), weight_gate.astype(jnp.float32), preferred_element_type=jnp.float32)
    up_part = jnp.dot(block.astype(jnp.float32), weight_up.astype(jnp.float32), preferred_element_type=jnp.float32)
    inner = (jax.nn.silu(gate_part) * up_part).astype(jnp.bfloat16)
    return jnp.dot(inner.astype(jnp.float32), weight_down.astype(jnp.float32), preferred_element_type=jnp.float32).astype(jnp.bfloat16)

def reference(residual_in, query_input, key_input, value_input, out_gate, write_strength, decay_rate, head_gain, out_proj, post_gain, expert_ids, gate_weights, expert_gate, expert_up, expert_down):
    tok_rows = residual_in.shape[0]
    pieces = prepare(query_input, key_input, value_input, write_strength, decay_rate)

    def emit_block(passed_state, item):
        rescaled_query, mixed_query, newest_value, key_matrix, transition_matrix, increment_term = item
        emitted = block_output(passed_state, rescaled_query, mixed_query, newest_value, key_matrix)
        moved_forward = jnp.einsum('aip,ape->aie', transition_matrix, passed_state, precision=largest_value) + increment_term
        return (moved_forward, emitted)
    _, outputs = lax.scan(emit_block, jnp.zeros((GROUP_VALUE_HEADS, DK, DV), jnp.float32), pieces)
    core_out = finish_core(outputs, out_gate, head_gain)
    mixer_out = jnp.dot(core_out.astype(jnp.float32), out_proj.astype(jnp.float32), preferred_element_type=jnp.float32)
    hidden_state = (residual_in.astype(jnp.float32) + mixer_out).astype(jnp.bfloat16)
    normed = post_norm(hidden_state, post_gain)
    devices = EXPERTS // EXP_DEV
    per_device = expert_ids.reshape(devices, TOK_DEV * TOP)
    local_slots = lax.map(partial(slot_index, experts=EXPERTS, capacity=CAP), per_device)
    owner = jnp.arange(devices, dtype=jnp.int32)[:, None]
    global_slots = (local_slots // CAP * (devices * CAP) + owner * CAP + local_slots % CAP).astype(jnp.int32)
    token_ids = (jnp.arange(tok_rows * TOP, dtype=jnp.int32) // TOP).astype(jnp.int32)
    source = jnp.full((EXPERTS * devices * CAP,), tok_rows, dtype=jnp.int32).at[global_slots.reshape(-1)].set(token_ids)
    padded = jnp.concatenate([normed, jnp.zeros((1, D), jnp.bfloat16)], axis=0)

    def serve(item):
        table, weight_gate, weight_up, weight_down = item
        return expert_rows(padded[table], weight_gate, weight_up, weight_down)
    results = lax.map(serve, (source.reshape(EXPERTS, devices * CAP), expert_gate, expert_up, expert_down)).reshape(-1, D)

    def combine(item):
        slots, weights = item
        picked = results[slots].reshape(TOK_DEV, TOP, D).astype(jnp.float32)
        return lax.optimization_barrier(jnp.sum(weights[:, :, None] * picked, axis=1))
    routed = lax.map(combine, (global_slots, gate_weights.reshape(devices, TOK_DEV, TOP))).reshape(tok_rows, D)
    return (hidden_state.astype(jnp.float32) + routed).astype(jnp.bfloat16)
```

```python
import functools

import jax
import jax.numpy as jnp
from jax import lax
from jax.experimental import pallas as pl
from jax.experimental.pallas import tpu as pltpu
from jax.sharding import PartitionSpec as P

D = 2048
HK = 8
GROUP_VALUE_HEADS = 16
DK = 128
DV = 128
TOP = 10
HEADS_STEP = 4
BLOCKS_STEP = 8

F32 = jnp.float32
BF16 = jnp.bfloat16
AXES = ("seq", "exp")
MIB = 1 << 20


def halves(x):
    high = x.astype(BF16)
    return high, (x - high.astype(F32)).astype(BF16)


def dot(a, b):
    return jnp.dot(a, b, preferred_element_type=F32)


def product(left, right):
    n = right[0].shape[1]
    lhs = jnp.concatenate(left, axis=1)
    top = jnp.concatenate(right, axis=1)
    bottom = jnp.concatenate([right[0], jnp.zeros_like(right[0])], axis=1)
    both = dot(lhs, jnp.concatenate([top, bottom], axis=0))
    return both[:, :n] + both[:, n:]


def local_kernel(q_ref, k_ref, v_ref, logs_ref, logs_row_ref, strength_row_ref, strength_ref, maps_ref, mix_ref):
    n = k_ref.shape[0]
    row = lax.broadcasted_iota(jnp.int32, (n, n), 0)
    column = lax.broadcasted_iota(jnp.int32, (n, n), 1)
    inclusive, strict, diagonal = row >= column, row > column, row == column
    heads = maps_ref.shape[0]
    group = GROUP_VALUE_HEADS // HK
    identity = diagonal.astype(F32)

    keys = []
    for i in range(heads // group):
        lanes = slice(i * DK, (i + 1) * DK)
        k_raw, q_raw = k_ref[:, lanes], q_ref[:, lanes]
        k_wide, q_wide = k_raw.astype(F32), q_raw.astype(F32)
        dims = (((1,), (1,)), ((), ()))
        gram = lax.dot_general(k_raw, k_raw, dims, preferred_element_type=F32)
        scores = lax.dot_general(q_raw, k_raw, dims, preferred_element_type=F32)
        inv_k = lax.rsqrt(jnp.sum(k_wide * k_wide, axis=1, keepdims=True) + 1e-06)
        inv_k_row = lax.rsqrt(jnp.sum(jnp.where(diagonal, gram, 0.0), axis=0, keepdims=True) + 1e-06)
        inv_q = lax.rsqrt(jnp.sum(q_wide * q_wide, axis=1, keepdims=True) + 1e-06) * DK ** (-0.5)
        keys.append(
            dict(
                k=k_raw,
                k_t=jnp.transpose(k_wide).astype(BF16),
                q=q_wide * inv_q,
                gram=gram * inv_k * inv_k_row,
                scores=scores * inv_q * inv_k_row,
                inv=inv_k,
                inv_row=inv_k_row,
            )
        )

    ratios, systems, inverses = [], [], []
    for j in range(heads):
        logs, logs_row = logs_ref[0][:, j : j + 1], logs_row_ref[0][j : j + 1, :]
        ratio = jnp.where(inclusive, jnp.exp(jnp.where(inclusive, logs - logs_row, 0.0)), 0.0)
        system = jnp.where(strict, ratio * keys[j // group]["gram"], 0.0) * strength_ref[0][:, j : j + 1]
        first = (row // 2 == column // 2) & strict
        ratios.append(ratio)
        systems.append(halves(system))
        inverses.append(identity - jnp.where(first, system, 0.0))
    size = 2
    while size < n:
        pairs = (row // (2 * size) == column // (2 * size)) & (row // size > column // size)
        inverse_halves = [halves(t) for t in inverses]
        cut = [
            tuple(jnp.where(pairs, part.astype(F32), 0.0).astype(BF16) for part in s) for s in systems
        ]
        left = [product(t, c) for t, c in zip(inverse_halves, cut)]
        inverses = [
            t - product(halves(x), th) for t, x, th in zip(inverses, left, inverse_halves)
        ]
        size *= 2

    for j in range(heads):
        key = keys[j // group]
        logs, logs_row = logs_ref[0][:, j : j + 1], logs_row_ref[0][j : j + 1, :]
        strength_row = strength_row_ref[0][j : j + 1, :]
        value = v_ref[:, j * DV : (j + 1) * DV]
        t = inverses[j]
        new_value = dot(
            jnp.concatenate(halves(t * strength_row), axis=1), jnp.concatenate([value, value], axis=0)
        )
        key_matrix = dot(
            jnp.concatenate(halves(t * (strength_row * jnp.exp(logs_row) * key["inv_row"])), axis=1),
            jnp.concatenate([key["k"], key["k"]], axis=0),
        )
        both = jnp.concatenate([key_matrix, new_value], axis=1)
        last = logs[n - 1 : n, :]
        faded = halves(both * (jnp.exp(last - logs) * key["inv"]))
        state = dot(
            jnp.concatenate([key["k_t"], key["k_t"]], axis=1), jnp.concatenate(faded, axis=0)
        )
        maps_ref[j, :, :DK] = jnp.exp(last) * identity - state[:, :DK]
        maps_ref[j, :, DK:] = state[:, DK:]
        mixed = halves(ratios[j] * key["scores"])
        both_halves = halves(both)
        out = dot(
            jnp.concatenate(mixed, axis=1), jnp.concatenate([both_halves[0], both_halves[0]], axis=0)
        ) + dot(mixed[0], both_halves[1])
        mix_ref[j, :, :DK] = key["q"] * jnp.exp(logs) - out[:, :DK]
        mix_ref[j, :, DK:] = out[:, DK:]


def local_terms(query_input, key_input, value_input, write_strength, decay_rate):
    n = key_input.shape[0]
    groups, per_key = GROUP_VALUE_HEADS // HEADS_STEP, GROUP_VALUE_HEADS // HK
    lower = jnp.tril(jnp.ones((n, n), F32))
    logs = jnp.dot(lower, -decay_rate, precision=lax.Precision.HIGHEST)

    def columns(x):
        return jnp.swapaxes(x.reshape(n, groups, HEADS_STEP), 0, 1)

    def rows(x):
        return x.T.reshape(groups, HEADS_STEP, n)

    wide = HEADS_STEP // per_key * DK
    column_spec = pl.BlockSpec((1, n, HEADS_STEP), lambda i: (i, 0, 0))
    row_spec = pl.BlockSpec((1, HEADS_STEP, n), lambda i: (i, 0, 0))
    out_spec = pl.BlockSpec((HEADS_STEP, DK, DK + DV), lambda i: (i, 0, 0))
    mix_spec = pl.BlockSpec((HEADS_STEP, n, DK + DV), lambda i: (i, 0, 0))
    return pl.pallas_call(
        local_kernel,
        grid=(groups,),
        in_specs=[
            pl.BlockSpec((n, wide), lambda i: (0, i)),
            pl.BlockSpec((n, wide), lambda i: (0, i)),
            pl.BlockSpec((n, HEADS_STEP * DV), lambda i: (0, i)),
            column_spec,
            row_spec,
            row_spec,
            column_spec,
        ],
        out_specs=[out_spec, mix_spec],
        out_shape=[
            jax.ShapeDtypeStruct((GROUP_VALUE_HEADS, DK, DK + DV), F32),
            jax.ShapeDtypeStruct((GROUP_VALUE_HEADS, n, DK + DV), F32),
        ],
        compiler_params=pltpu.CompilerParams(vmem_limit_bytes=40 * MIB),
        name="local_terms",
    )(
        query_input,
        key_input,
        value_input,
        columns(logs),
        rows(logs),
        rows(write_strength),
        columns(write_strength),
    )


def chain_kernel(maps_ref, before_ref, whole_ref):
    row = lax.broadcasted_iota(jnp.int32, (DK, DK + DV), 0)
    column = lax.broadcasted_iota(jnp.int32, (DK, DK + DV), 1)
    passed = (row == column).astype(F32)
    for i in range(maps_ref.shape[0]):
        before_ref[i] = passed
        item = maps_ref[i]
        step = halves(item[:, :DK])
        high, low = halves(passed)
        passed = (
            dot(jnp.concatenate(step, axis=1), jnp.concatenate([high, high], axis=0))
            + dot(step[0], low)
            + jnp.where(column >= DK, item, 0.0)
        )
    whole_ref[...] = passed


def chain(maps):
    count = maps.shape[0]
    return pl.pallas_call(
        chain_kernel,
        out_shape=[
            jax.ShapeDtypeStruct((count, DK, DK + DV), F32),
            jax.ShapeDtypeStruct((DK, DK + DV), F32),
        ],
        compiler_params=pltpu.CompilerParams(vmem_limit_bytes=40 * MIB),
        name="chain",
    )(maps)


def entering_states(maps, devices):
    heads = maps.shape[0]
    segments = devices // heads
    groups = [[g * heads + h for h in range(heads)] for g in range(segments)]
    by_device = lax.all_to_all(
        maps, AXES, split_axis=0, concat_axis=0, axis_index_groups=groups, tiled=True
    )
    before, whole = chain(by_device)
    across = [[g * heads + h for g in range(segments)] for h in range(heads)]
    adds = lax.all_gather(whole[:, DK:], AXES, axis_index_groups=across)
    segment = lax.axis_index(AXES) // heads
    carry = adds[0]
    start = jnp.where(segment == 1, carry, 0.0)
    if segments > 2:
        steps = lax.all_gather(whole[:, :DK], AXES, axis_index_groups=across)
        for g in range(2, segments):
            carry = adds[g - 1] + jnp.dot(steps[g - 1], carry, precision=lax.Precision.HIGHEST)
            start = jnp.where(segment == g, carry, start)
    states = (
        jnp.dot(
            before[:, :, :DK].reshape(heads * DK, DK), start, precision=lax.Precision.HIGH
        ).reshape(heads, DK, DV)
        + before[:, :, DK:]
    ).astype(BF16)
    return lax.all_to_all(
        states, AXES, split_axis=0, concat_axis=0, axis_index_groups=groups, tiled=True
    )


def finish_kernel(mix_ref, state_ref, gate_ref, gain_ref, proj_ref, residual_ref, post_ref, hidden_ref, normed_ref, core_ref):
    for h in range(GROUP_VALUE_HEADS):
        lanes = slice(h * DV, (h + 1) * DV)
        state = state_ref[h]
        recurrent = (
            dot(
                jnp.concatenate(halves(mix_ref[h, :, :DK]), axis=1),
                jnp.concatenate([state, state], axis=0),
            )
            + mix_ref[h, :, DK:]
        )
        inv_rms = lax.rsqrt(jnp.mean(recurrent * recurrent, axis=1, keepdims=True) + 1e-06)
        gate = gate_ref[:, lanes].astype(F32)
        act = gate / (1.0 + jnp.exp(-gate))
        core_ref[:, lanes] = (recurrent * inv_rms * gain_ref[...] * act).astype(BF16)
    core = core_ref[...]
    wide = proj_ref.shape[2]
    squares = 0.0
    for e in range(proj_ref.shape[0]):
        lanes = slice(e * wide, (e + 1) * wide)
        hidden = (residual_ref[:, lanes].astype(F32) + dot(core, proj_ref[e])).astype(BF16)
        hidden_ref[:, lanes] = hidden
        widened = hidden.astype(F32)
        squares += jnp.sum(widened * widened, axis=1, keepdims=True)
    inv_rms = lax.rsqrt(squares * (1.0 / D) + 1e-06)
    normed_ref[...] = (hidden_ref[...].astype(F32) * inv_rms * post_ref[...]).astype(BF16)


def finish(mix, states, out_gate, head_gain, proj, residual_in, post_gain):
    shape = residual_in.shape
    return pl.pallas_call(
        finish_kernel,
        out_shape=[jax.ShapeDtypeStruct(shape, BF16), jax.ShapeDtypeStruct(shape, BF16)],
        scratch_shapes=[pltpu.VMEM(shape, BF16)],
        compiler_params=pltpu.CompilerParams(vmem_limit_bytes=48 * MIB),
        name="finish",
    )(mix, states, out_gate, head_gain.reshape(1, DV), proj, residual_in, post_gain.reshape(1, D))


def expert_kernel(capacity, tokens_ref, slot_row_ref, slot_ref, weight_ref, gate_ref, up_ref, down_ref, out_ref):
    blocks, rows, _ = tokens_ref.shape
    local = gate_ref.shape[0]
    slot_ids = lax.broadcasted_iota(jnp.int32, (capacity, rows), 0).astype(F32)
    taken = [[] for _ in range(local)]
    for b in range(blocks):
        chosen = jnp.concatenate(
            [(slot_row_ref[b, e : e + 1, :] == slot_ids).astype(F32) for e in range(local)], axis=0
        ).astype(BF16)
        picked = dot(chosen, tokens_ref[b])
        for e in range(local):
            taken[e].append(picked[e * capacity : (e + 1) * capacity])
    outs = []
    for e in range(local):
        received = jnp.concatenate(taken[e], axis=0).astype(BF16)
        gate = dot(received, gate_ref[e])
        up = dot(received, up_ref[e])
        inner = (gate / (1.0 + jnp.exp(-gate)) * up).astype(BF16)
        outs.append(dot(inner, down_ref[e]))
    span = local * capacity
    lane = lax.broadcasted_iota(jnp.int32, (rows, 2 * span), 1)
    lane_expert, lane_slot = lane // capacity % local, (lane % capacity).astype(F32)
    for b in range(blocks):
        slot = jnp.full((rows, 2 * span), -1.0, F32)
        weight = jnp.zeros((rows, 2 * span), F32)
        for e in range(local):
            slot = jnp.where(lane_expert == e, slot_ref[b, :, e : e + 1], slot)
            weight = jnp.where(lane_expert == e, weight_ref[b, :, e : e + 1], weight)
        high = weight.astype(BF16).astype(F32)
        spread = jnp.where(
            slot == lane_slot, jnp.where(lane < span, high, weight - high), 0.0
        ).astype(BF16)
        results = [out[b * capacity : (b + 1) * capacity] for out in outs]
        stacked = jnp.concatenate(results + results, axis=0).astype(BF16)
        out_ref[b] = dot(spread, stacked).astype(BF16)


def expert_part(tokens, slots, weights, expert_gate, expert_up, expert_down, capacity):
    devices, rows, _ = tokens.shape
    local = expert_gate.shape[0]

    def whole(x):
        return pl.BlockSpec(x.shape, lambda i: (0, 0, 0), pipeline_mode=pl.Buffered(1))

    column_spec = pl.BlockSpec((BLOCKS_STEP, rows, local), lambda i: (i, 0, 0))
    token_spec = pl.BlockSpec((BLOCKS_STEP, rows, D), lambda i: (i, 0, 0))
    return pl.pallas_call(
        functools.partial(expert_kernel, capacity),
        grid=(devices // BLOCKS_STEP,),
        in_specs=[
            token_spec,
            pl.BlockSpec((BLOCKS_STEP, local, rows), lambda i: (i, 0, 0)),
            column_spec,
            column_spec,
            whole(expert_gate),
            whole(expert_up),
            whole(expert_down),
        ],
        out_specs=token_spec,
        out_shape=jax.ShapeDtypeStruct(tokens.shape, BF16),
        compiler_params=pltpu.CompilerParams(vmem_limit_bytes=56 * MIB),
        name="experts",
    )(tokens, jnp.swapaxes(slots, 1, 2), slots, weights, expert_gate, expert_up, expert_down)


def routing(expert_ids, gate_weights, experts, local_experts):
    chosen = expert_ids[:, :, None] == jnp.arange(experts, dtype=jnp.int32)
    dense = jnp.sum(jnp.where(chosen, gate_weights[:, :, None], 0.0), axis=1)
    everyone = lax.all_gather(dense, AXES)
    weights = lax.dynamic_slice_in_dim(
        everyone, lax.axis_index(AXES) * local_experts, local_experts, axis=2
    )
    named = weights > 0.0
    rows = dense.shape[0]
    rank = jnp.einsum(
        "ts,bse->bte",
        jnp.tril(jnp.ones((rows, rows), BF16)),
        named.astype(BF16),
        preferred_element_type=F32,
    )
    return jnp.where(named, rank - 1.0, -1.0), weights


def shards(
    residual_in,
    query_input,
    key_input,
    value_input,
    out_gate,
    write_strength,
    decay_rate,
    head_gain,
    out_proj,
    post_gain,
    expert_ids,
    gate_weights,
    expert_gate,
    expert_up,
    expert_down,
):
    tok_rows = residual_in.shape[0]
    devices = lax.axis_size(AXES)
    local_experts = expert_gate.shape[0]
    experts = local_experts * devices
    capacity = max(2, tok_rows * TOP * 8 // (5 * experts))
    proj = lax.all_gather(out_proj, "exp")
    slots, weights = routing(expert_ids, gate_weights, experts, local_experts)
    maps, mix = local_terms(query_input, key_input, value_input, write_strength, decay_rate)
    states = entering_states(maps, devices)
    hidden, normed = finish(mix, states, out_gate, head_gain, proj, residual_in, post_gain)
    tokens = lax.all_gather(normed, AXES)
    partial = expert_part(tokens, slots, weights, expert_gate, expert_up, expert_down, capacity)
    routed = lax.psum_scatter(
        partial.reshape(devices * tok_rows, D), AXES, scatter_dimension=0, tiled=True
    )
    return (hidden.astype(F32) + routed.astype(F32)).astype(BF16)


def solution(mesh):
    rows = P(AXES, None)
    placed = (rows,) * 7 + (P(), P(None, "exp"), P(), rows, rows) + (P(AXES, None, None),) * 3
    return jax.shard_map(shards, mesh=mesh, in_specs=placed, out_specs=rows, check_vma=False)
```

```python
import functools

import jax
import jax.numpy as jnp
from jax import lax
from jax.experimental import pallas as pl
from jax.experimental.pallas import tpu as pltpu
from jax.sharding import Mesh, PartitionSpec as P

D = 2048
HK = 8
GROUP_VALUE_HEADS = 16
DK = 128
DV = 128
TOP = 10
HEADS_STEP = 4
BLOCKS_STEP = 16

F32 = jnp.float32
BF16 = jnp.bfloat16
AXES = ("outer", "mid", "core", "inner")
SAME_CORE = ("outer", "mid", "inner")
MIB = 1 << 20


def halves(x):
    high = x.astype(BF16)
    return high, (x - high.astype(F32)).astype(BF16)


def dot(a, b):
    return jnp.dot(a, b, preferred_element_type=F32)


def product(left, right):
    n = right[0].shape[1]
    lhs = jnp.concatenate(left, axis=1)
    top = jnp.concatenate(right, axis=1)
    bottom = jnp.concatenate([right[0], jnp.zeros_like(right[0])], axis=1)
    both = dot(lhs, jnp.concatenate([top, bottom], axis=0))
    return both[:, :n] + both[:, n:]


def local_kernel(q_ref, k_ref, v_ref, logs_ref, logs_row_ref, strength_row_ref, strength_ref, maps_ref, mix_ref):
    n = k_ref.shape[0]
    row = lax.broadcasted_iota(jnp.int32, (n, n), 0)
    column = lax.broadcasted_iota(jnp.int32, (n, n), 1)
    inclusive, strict, diagonal = row >= column, row > column, row == column
    heads = maps_ref.shape[0]
    group = GROUP_VALUE_HEADS // HK
    identity = diagonal.astype(F32)

    keys = []
    for i in range(heads // group):
        lanes = slice(i * DK, (i + 1) * DK)
        k_raw, q_raw = k_ref[:, lanes], q_ref[:, lanes]
        k_wide, q_wide = k_raw.astype(F32), q_raw.astype(F32)
        dims = (((1,), (1,)), ((), ()))
        gram = lax.dot_general(k_raw, k_raw, dims, preferred_element_type=F32)
        scores = lax.dot_general(q_raw, k_raw, dims, preferred_element_type=F32)
        inv_k = lax.rsqrt(jnp.sum(k_wide * k_wide, axis=1, keepdims=True) + 1e-06)
        inv_k_row = lax.rsqrt(jnp.sum(jnp.where(diagonal, gram, 0.0), axis=0, keepdims=True) + 1e-06)
        inv_q = lax.rsqrt(jnp.sum(q_wide * q_wide, axis=1, keepdims=True) + 1e-06) * DK ** (-0.5)
        keys.append(
            dict(
                k=k_raw,
                k_t=jnp.transpose(k_wide).astype(BF16),
                q=q_wide * inv_q,
                gram=gram * inv_k * inv_k_row,
                scores=scores * inv_q * inv_k_row,
                inv=inv_k,
                inv_row=inv_k_row,
            )
        )

    ratios, systems, inverses = [], [], []
    for j in range(heads):
        logs, logs_row = logs_ref[0][:, j : j + 1], logs_row_ref[0][j : j + 1, :]
        ratio = jnp.where(inclusive, jnp.exp(jnp.where(inclusive, logs - logs_row, 0.0)), 0.0)
        system = jnp.where(strict, ratio * keys[j // group]["gram"], 0.0) * strength_ref[0][:, j : j + 1]
        first = (row // 2 == column // 2) & strict
        ratios.append(ratio)
        systems.append(halves(system))
        inverses.append(identity - jnp.where(first, system, 0.0))
    size = 2
    while size < n:
        pairs = (row // (2 * size) == column // (2 * size)) & (row // size > column // size)
        inverse_halves = [halves(t) for t in inverses]
        cut = [
            tuple(jnp.where(pairs, part.astype(F32), 0.0).astype(BF16) for part in s) for s in systems
        ]
        left = [product(t, c) for t, c in zip(inverse_halves, cut)]
        inverses = [
            t - product(halves(x), th) for t, x, th in zip(inverses, left, inverse_halves)
        ]
        size *= 2

    for j in range(heads):
        key = keys[j // group]
        logs, logs_row = logs_ref[0][:, j : j + 1], logs_row_ref[0][j : j + 1, :]
        strength_row = strength_row_ref[0][j : j + 1, :]
        value = v_ref[:, j * DV : (j + 1) * DV]
        t = inverses[j]
        new_value = dot(
            jnp.concatenate(halves(t * strength_row), axis=1), jnp.concatenate([value, value], axis=0)
        )
        key_matrix = dot(
            jnp.concatenate(halves(t * (strength_row * jnp.exp(logs_row) * key["inv_row"])), axis=1),
            jnp.concatenate([key["k"], key["k"]], axis=0),
        )
        both = jnp.concatenate([key_matrix, new_value], axis=1)
        last = logs[n - 1 : n, :]
        faded = halves(both * (jnp.exp(last - logs) * key["inv"]))
        state = dot(
            jnp.concatenate([key["k_t"], key["k_t"]], axis=1), jnp.concatenate(faded, axis=0)
        )
        high, low = halves(jnp.exp(last) * identity - state[:, :DK])
        maps_ref[j, :, :DK] = high
        maps_ref[j, :, DK : 2 * DK] = low
        maps_ref[j, :, 2 * DK :] = state[:, DK:].astype(BF16)
        mixed = halves(ratios[j] * key["scores"])
        both_halves = halves(both)
        out = dot(
            jnp.concatenate(mixed, axis=1), jnp.concatenate([both_halves[0], both_halves[0]], axis=0)
        ) + dot(mixed[0], both_halves[1])
        mix_ref[j, :, :DK] = key["q"] * jnp.exp(logs) - out[:, :DK]
        mix_ref[j, :, DK:] = out[:, DK:]


def local_terms(query_input, key_input, value_input, write_strength, decay_rate):
    n = key_input.shape[0]
    groups, per_key = GROUP_VALUE_HEADS // HEADS_STEP, GROUP_VALUE_HEADS // HK
    lower = jnp.tril(jnp.ones((n, n), F32))
    logs = jnp.dot(lower, -decay_rate, precision=lax.Precision.HIGHEST)

    def columns(x):
        return jnp.swapaxes(x.reshape(n, groups, HEADS_STEP), 0, 1)

    def rows(x):
        return x.T.reshape(groups, HEADS_STEP, n)

    wide = HEADS_STEP // per_key * DK
    column_spec = pl.BlockSpec((1, n, HEADS_STEP), lambda i: (i, 0, 0))
    row_spec = pl.BlockSpec((1, HEADS_STEP, n), lambda i: (i, 0, 0))
    out_spec = pl.BlockSpec((HEADS_STEP, DK, 2 * DK + DV), lambda i: (i, 0, 0))
    mix_spec = pl.BlockSpec((HEADS_STEP, n, DK + DV), lambda i: (i, 0, 0))
    return pl.pallas_call(
        local_kernel,
        grid=(groups,),
        in_specs=[
            pl.BlockSpec((n, wide), lambda i: (0, i)),
            pl.BlockSpec((n, wide), lambda i: (0, i)),
            pl.BlockSpec((n, HEADS_STEP * DV), lambda i: (0, i)),
            column_spec,
            row_spec,
            row_spec,
            column_spec,
        ],
        out_specs=[out_spec, mix_spec],
        out_shape=[
            jax.ShapeDtypeStruct((GROUP_VALUE_HEADS, DK, 2 * DK + DV), BF16),
            jax.ShapeDtypeStruct((GROUP_VALUE_HEADS, n, DK + DV), F32),
        ],
        compiler_params=pltpu.CompilerParams(vmem_limit_bytes=40 * MIB),
        name="local_terms",
    )(
        query_input,
        key_input,
        value_input,
        columns(logs),
        rows(logs),
        rows(write_strength),
        columns(write_strength),
    )


def chain_kernel(maps_ref, before_ref, whole_ref):
    row = lax.broadcasted_iota(jnp.int32, (DK, DK + DV), 0)
    column = lax.broadcasted_iota(jnp.int32, (DK, DK + DV), 1)
    passed = (row == column).astype(F32)
    for i in range(maps_ref.shape[0]):
        before_ref[i] = passed
        high, low = halves(passed)
        passed = dot(maps_ref[i, :, : 2 * DK], jnp.concatenate([high, high], axis=0)) + dot(
            maps_ref[i, :, :DK], low
        )
        passed = jnp.concatenate(
            [passed[:, :DK], passed[:, DK:] + maps_ref[i, :, 2 * DK :].astype(F32)], axis=1
        )
    whole_ref[...] = passed


def chain(maps):
    count = maps.shape[0]
    return pl.pallas_call(
        chain_kernel,
        out_shape=[
            jax.ShapeDtypeStruct((count, DK, DK + DV), F32),
            jax.ShapeDtypeStruct((DK, DK + DV), F32),
        ],
        compiler_params=pltpu.CompilerParams(vmem_limit_bytes=40 * MIB),
        name="chain",
    )(maps)


def entering_states(maps, devices):
    heads = maps.shape[0]
    segments = devices // heads
    groups = [[g * heads + h for h in range(heads)] for g in range(segments)]
    by_device = lax.all_to_all(
        maps, AXES, split_axis=0, concat_axis=0, axis_index_groups=groups, tiled=True
    )
    before, whole = chain(by_device)
    across = [[g * heads + h for g in range(segments)] for h in range(heads)]
    adds = lax.all_gather(whole[:, DK:], AXES, axis_index_groups=across)
    segment = lax.axis_index(AXES) // heads
    carry = adds[0]
    start = jnp.where(segment == 1, carry, 0.0)
    if segments > 2:
        steps = lax.all_gather(whole[:, :DK], AXES, axis_index_groups=across)
        for g in range(2, segments):
            carry = adds[g - 1] + jnp.dot(steps[g - 1], carry, precision=lax.Precision.HIGHEST)
            start = jnp.where(segment == g, carry, start)
    states = (
        jnp.dot(
            before[:, :, :DK].reshape(heads * DK, DK), start, precision=lax.Precision.HIGH
        ).reshape(heads, DK, DV)
        + before[:, :, DK:]
    ).astype(BF16)
    return lax.all_to_all(
        states, AXES, split_axis=0, concat_axis=0, axis_index_groups=groups, tiled=True
    )


def finish_kernel(
    place_ref, mix_ref, state_ref, gate_ref, gain_ref, residual_ref, post_ref, *refs
):
    *proj_refs, hidden_ref, normed_ref, core_ref = refs
    for h in range(GROUP_VALUE_HEADS):
        lanes = slice(h * DV, (h + 1) * DV)
        state = state_ref[h]
        recurrent = (
            dot(
                jnp.concatenate(halves(mix_ref[h, :, :DK]), axis=1),
                jnp.concatenate([state, state], axis=0),
            )
            + mix_ref[h, :, DK:]
        )
        inv_rms = lax.rsqrt(jnp.mean(recurrent * recurrent, axis=1, keepdims=True) + 1e-06)
        gate = gate_ref[:, lanes].astype(F32)
        act = gate / (1.0 + jnp.exp(-gate))
        core_ref[:, lanes] = (recurrent * inv_rms * gain_ref[...] * act).astype(BF16)
    core = core_ref[...]
    squares = 0.0
    for i, proj_ref in enumerate(proj_refs):
        wide = proj_ref.shape[1]
        lanes = pl.ds(pl.multiple_of(place_ref[i] * wide, wide), wide)
        hidden = (residual_ref[:, lanes].astype(F32) + dot(core, proj_ref[...])).astype(BF16)
        hidden_ref[:, lanes] = hidden
        widened = hidden.astype(F32)
        squares += jnp.sum(widened * widened, axis=1, keepdims=True)
    inv_rms = lax.rsqrt(squares * (1.0 / D) + 1e-06)
    normed_ref[...] = (hidden_ref[...].astype(F32) * inv_rms * post_ref[...]).astype(BF16)


def finish(mix, states, out_gate, head_gain, proj, places, residual_in, post_gain):
    shape = residual_in.shape
    vmem = pl.BlockSpec(memory_space=pltpu.VMEM)
    return pl.pallas_call(
        finish_kernel,
        in_specs=[pl.BlockSpec(memory_space=pltpu.SMEM)] + [vmem] * (6 + len(proj)),
        out_shape=[jax.ShapeDtypeStruct(shape, BF16), jax.ShapeDtypeStruct(shape, BF16)],
        scratch_shapes=[pltpu.VMEM(shape, BF16)],
        compiler_params=pltpu.CompilerParams(vmem_limit_bytes=48 * MIB),
        name="finish",
    )(
        places,
        mix,
        states,
        out_gate,
        head_gain.reshape(1, DV),
        residual_in,
        post_gain.reshape(1, D),
        *proj,
    )


def expert_kernel(
    capacity,
    tokens_hbm,
    slot_row_ref,
    slot_ref,
    weight_ref,
    own_gate_ref,
    own_up_ref,
    own_down_ref,
    other_gate_ref,
    other_up_ref,
    other_down_ref,
    out_hbm,
    block_ref,
    taken_ref,
    in_sems,
    out_sems,
):
    group, expert = pl.program_id(0), pl.program_id(1)
    blocks, rows, _ = block_ref.shape
    served = taken_ref.shape[0]
    joined = max(1, 16 // capacity)

    def copy_in(b):
        return pltpu.make_async_copy(
            tokens_hbm.at[group * blocks + b], block_ref.at[b], in_sems.at[b]
        )

    def copy_out(b):
        return pltpu.make_async_copy(
            block_ref.at[b], out_hbm.at[group * blocks + b], out_sems.at[b]
        )

    @pl.when(expert == 0)
    def _():
        for b in range(blocks):
            copy_in(b).start()
        slot_ids = lax.broadcasted_iota(jnp.int32, (capacity, rows), 0).astype(F32)
        for first in range(0, blocks, joined):
            picked = []
            for b in range(first, first + joined):
                chosen = jnp.concatenate(
                    [(slot_row_ref[b, e : e + 1, :] == slot_ids).astype(F32) for e in range(served)],
                    axis=0,
                ).astype(BF16)
                copy_in(b).wait()
                picked.append(dot(chosen, block_ref[b]))
            for e in range(served):
                part = [p[e * capacity : (e + 1) * capacity] for p in picked]
                taken_ref[e, first * capacity : (first + joined) * capacity] = jnp.concatenate(
                    part, axis=0
                ).astype(BF16)

    def serve(gate_ref, up_ref, down_ref):
        received = taken_ref[expert]
        gate = dot(received, gate_ref[0])
        up = dot(received, up_ref[0])
        inner = (gate / (1.0 + jnp.exp(-gate)) * up).astype(BF16)
        taken_ref[expert] = dot(inner, down_ref[0]).astype(BF16)

    @pl.when(expert < served // 2)
    def _():
        serve(own_gate_ref, own_up_ref, own_down_ref)

    @pl.when(expert >= served // 2)
    def _():
        serve(other_gate_ref, other_up_ref, other_down_ref)

    @pl.when(expert == served - 1)
    def _():
        span = served * capacity
        lane = lax.broadcasted_iota(jnp.int32, (rows, 2 * span), 1)
        lane_expert, lane_slot = lane // capacity % served, (lane % capacity).astype(F32)
        for first in range(0, blocks, joined):
            results = [
                taken_ref[e, first * capacity : (first + joined) * capacity] for e in range(served)
            ]
            for b in range(first, first + joined):
                slot = jnp.full((rows, 2 * span), -1.0, F32)
                weight = jnp.zeros((rows, 2 * span), F32)
                for e in range(served):
                    slot = jnp.where(lane_expert == e, slot_ref[b, :, e : e + 1], slot)
                    weight = jnp.where(lane_expert == e, weight_ref[b, :, e : e + 1], weight)
                high = weight.astype(BF16).astype(F32)
                spread = jnp.where(
                    slot == lane_slot, jnp.where(lane < span, high, weight - high), 0.0
                ).astype(BF16)
                if joined == 1:
                    stacked = jnp.concatenate(results + results, axis=0)
                else:
                    start = (b - first) * capacity
                    mine = [r.astype(F32)[start : start + capacity] for r in results]
                    stacked = jnp.concatenate(mine + mine, axis=0).astype(BF16)
                block_ref[b] = dot(spread, stacked).astype(BF16)
                copy_out(b).start()
        for b in range(blocks):
            copy_out(b).wait()


def expert_part(tokens, weights, own, other, capacity):
    devices, rows, _ = tokens.shape
    local = own[0].shape[0]
    served = 2 * local
    named = weights > 0.0
    rank = jnp.einsum(
        "set,tu->seu",
        named.astype(BF16),
        jnp.triu(jnp.ones((rows, rows), BF16)),
        preferred_element_type=F32,
    )
    slots = jnp.where(named, rank - 1.0, -1.0)

    def own_spec(x):
        return pl.BlockSpec((1,) + x.shape[1:], lambda g, e: (jnp.minimum(e, local - 1), 0, 0))

    def other_spec(x):
        return pl.BlockSpec((1,) + x.shape[1:], lambda g, e: (jnp.maximum(e - local, 0), 0, 0))

    column_spec = pl.BlockSpec((BLOCKS_STEP, rows, served), lambda g, e: (g, 0, 0))
    return pl.pallas_call(
        functools.partial(expert_kernel, capacity),
        grid=(devices // BLOCKS_STEP, served),
        in_specs=[
            pl.BlockSpec(memory_space=pl.ANY),
            pl.BlockSpec((BLOCKS_STEP, served, rows), lambda g, e: (g, 0, 0)),
            column_spec,
            column_spec,
        ]
        + [own_spec(x) for x in own]
        + [other_spec(x) for x in other],
        out_specs=pl.BlockSpec(memory_space=pl.ANY),
        out_shape=jax.ShapeDtypeStruct(tokens.shape, BF16),
        scratch_shapes=[
            pltpu.VMEM((BLOCKS_STEP, rows, D), BF16),
            pltpu.VMEM((served, BLOCKS_STEP * capacity, D), BF16),
            pltpu.SemaphoreType.DMA((BLOCKS_STEP,)),
            pltpu.SemaphoreType.DMA((BLOCKS_STEP,)),
        ],
        compiler_params=pltpu.CompilerParams(vmem_limit_bytes=56 * MIB),
        name="experts",
    )(tokens, slots, jnp.swapaxes(slots, 1, 2), jnp.swapaxes(weights, 1, 2), *own, *other)


def routing(expert_ids, gate_weights, local_experts):
    outer, cores, inner = (lax.axis_size(a) for a in (("outer", "mid"), "core", "inner"))
    rows = expert_ids.shape[0]
    experts = local_experts * outer * cores * inner
    chosen = expert_ids.T[None] == jnp.arange(experts, dtype=jnp.int32)[:, None, None]
    dense = jnp.sum(jnp.where(chosen, gate_weights.T[None], 0.0), axis=1)
    by_chip = jnp.swapaxes(dense.reshape(outer, cores, inner, local_experts * rows), 1, 2)
    by_chip = by_chip.reshape(outer * inner, cores * local_experts, rows)
    weights = lax.all_to_all(by_chip, SAME_CORE, split_axis=0, concat_axis=0, tiled=True)
    turned = jnp.concatenate([weights[:, local_experts:], weights[:, :local_experts]], axis=1)
    return jnp.where(lax.axis_index("core") == 1, turned, weights)


def flipped(array, bit):
    devices = lax.axis_size(AXES)
    return lax.ppermute(array, AXES, [(i, i ^ bit) for i in range(devices)])


def shards(
    columns,
    residual_in,
    query_input,
    key_input,
    value_input,
    out_gate,
    write_strength,
    decay_rate,
    head_gain,
    out_proj,
    post_gain,
    expert_ids,
    gate_weights,
    expert_gate,
    expert_up,
    expert_down,
):
    tok_rows = residual_in.shape[0]
    devices = lax.axis_size(AXES)
    local_experts = expert_gate.shape[0]
    capacity = max(2, tok_rows * TOP * 8 // (5 * local_experts * devices))
    weights = routing(expert_ids, gate_weights, local_experts)
    proj, places = [out_proj], [lax.axis_index(AXES) % columns]
    bit = columns // 2
    while bit:
        proj = proj + [flipped(piece, bit) for piece in proj]
        places = places + [place ^ bit for place in places]
        bit //= 2
    own = (expert_gate, expert_up, expert_down)
    other = tuple(flipped(x, lax.axis_size("inner")) for x in own)
    maps, mix = local_terms(query_input, key_input, value_input, write_strength, decay_rate)
    states = entering_states(maps, devices)
    hidden, normed = finish(
        mix, states, out_gate, head_gain, proj, jnp.stack(places), residual_in, post_gain
    )
    tokens = lax.all_gather(normed, SAME_CORE)
    partial = expert_part(tokens, weights, own, other, capacity)
    routed = lax.psum_scatter(
        partial.reshape(-1, D), SAME_CORE, scatter_dimension=0, tiled=True
    )
    return (hidden.astype(F32) + routed.astype(F32)).astype(BF16)


def core_stride(devices):
    first = getattr(devices[0], "coords", None)
    for i in range(1, len(devices)):
        if first is not None and tuple(devices[i].coords) == tuple(first):
            return i
    return 1


def solution(mesh):
    devices = mesh.devices.reshape(-1)
    inner = core_stride(devices)
    columns = mesh.shape["exp"]
    if 2 * inner <= columns:
        shape, column_axes = (-1, columns // (2 * inner), 2, inner), AXES[1:]
    else:
        shape, column_axes = (-1, 1, 2, inner), ("inner",)
    view = Mesh(devices.reshape(shape), AXES)
    rows = P(AXES, None)
    placed = (
        (rows,) * 7 + (P(), P(None, column_axes), P(), rows, rows) + (P(AXES, None, None),) * 3
    )
    body = functools.partial(shards, columns)
    return jax.shard_map(body, mesh=view, in_specs=placed, out_specs=rows, check_vma=False)
```

```python
import functools

import jax
import jax.numpy as jnp
from jax import lax
from jax.experimental import pallas as pl
from jax.experimental.pallas import tpu as pltpu
from jax.sharding import Mesh, PartitionSpec as P

D = 2048
HK = 8
GROUP_VALUE_HEADS = 16
DK = 128
DV = 128
TOP = 10
HEADS_STEP = 4
BLOCKS_STEP = 16
SPLIT = 1024
STRIP = 256

F32 = jnp.float32
BF16 = jnp.bfloat16
AXES = ("outer", "mid", "core", "inner")
SAME_CORE = ("outer", "mid", "inner")
REST = ("mid", "inner")
MIB = 1 << 20


def halves(x):
    high = x.astype(BF16)
    return high, (x - high.astype(F32)).astype(BF16)


def dot(a, b):
    return jnp.dot(a, b, preferred_element_type=F32)


def product(left, right):
    n = right[0].shape[1]
    lhs = jnp.concatenate(left, axis=1)
    top = jnp.concatenate(right, axis=1)
    bottom = jnp.concatenate([right[0], jnp.zeros_like(right[0])], axis=1)
    both = dot(lhs, jnp.concatenate([top, bottom], axis=0))
    return both[:, :n] + both[:, n:]


def local_kernel(q_ref, k_ref, v_ref, logs_ref, logs_row_ref, strength_row_ref, strength_ref, maps_ref, mix_ref):
    n = k_ref.shape[0]
    row = lax.broadcasted_iota(jnp.int32, (n, n), 0)
    column = lax.broadcasted_iota(jnp.int32, (n, n), 1)
    inclusive, strict, diagonal = row >= column, row > column, row == column
    heads = maps_ref.shape[0]
    group = GROUP_VALUE_HEADS // HK
    identity = diagonal.astype(F32)

    keys = []
    for i in range(heads // group):
        lanes = slice(i * DK, (i + 1) * DK)
        k_raw, q_raw = k_ref[:, lanes], q_ref[:, lanes]
        k_wide, q_wide = k_raw.astype(F32), q_raw.astype(F32)
        dims = (((1,), (1,)), ((), ()))
        gram = lax.dot_general(k_raw, k_raw, dims, preferred_element_type=F32)
        scores = lax.dot_general(q_raw, k_raw, dims, preferred_element_type=F32)
        inv_k = lax.rsqrt(jnp.sum(k_wide * k_wide, axis=1, keepdims=True) + 1e-06)
        inv_k_row = lax.rsqrt(jnp.sum(jnp.where(diagonal, gram, 0.0), axis=0, keepdims=True) + 1e-06)
        inv_q = lax.rsqrt(jnp.sum(q_wide * q_wide, axis=1, keepdims=True) + 1e-06) * DK ** (-0.5)
        keys.append(
            dict(
                k=k_raw,
                k_t=jnp.transpose(k_wide).astype(BF16),
                q=q_wide * inv_q,
                gram=gram * inv_k * inv_k_row,
                scores=scores * inv_q * inv_k_row,
                inv=inv_k,
                inv_row=inv_k_row,
            )
        )

    ratios, systems, inverses = [], [], []
    for j in range(heads):
        logs, logs_row = logs_ref[0][:, j : j + 1], logs_row_ref[0][j : j + 1, :]
        ratio = jnp.where(inclusive, jnp.exp(jnp.where(inclusive, logs - logs_row, 0.0)), 0.0)
        system = jnp.where(strict, ratio * keys[j // group]["gram"], 0.0) * strength_ref[0][:, j : j + 1]
        first = (row // 2 == column // 2) & strict
        ratios.append(ratio)
        systems.append(halves(system))
        inverses.append(identity - jnp.where(first, system, 0.0))
    size = 2
    while size < n:
        pairs = (row // (2 * size) == column // (2 * size)) & (row // size > column // size)
        inverse_halves = [halves(t) for t in inverses]
        cut = [
            tuple(jnp.where(pairs, part.astype(F32), 0.0).astype(BF16) for part in s) for s in systems
        ]
        left = [product(t, c) for t, c in zip(inverse_halves, cut)]
        inverses = [
            t - product(halves(x), th) for t, x, th in zip(inverses, left, inverse_halves)
        ]
        size *= 2

    for j in range(heads):
        key = keys[j // group]
        logs, logs_row = logs_ref[0][:, j : j + 1], logs_row_ref[0][j : j + 1, :]
        strength_row = strength_row_ref[0][j : j + 1, :]
        value = v_ref[:, j * DV : (j + 1) * DV]
        t = inverses[j]
        new_value = dot(
            jnp.concatenate(halves(t * strength_row), axis=1), jnp.concatenate([value, value], axis=0)
        )
        key_matrix = dot(
            jnp.concatenate(halves(t * (strength_row * jnp.exp(logs_row) * key["inv_row"])), axis=1),
            jnp.concatenate([key["k"], key["k"]], axis=0),
        )
        both = jnp.concatenate([key_matrix, new_value], axis=1)
        last = logs[n - 1 : n, :]
        faded = halves(both * (jnp.exp(last - logs) * key["inv"]))
        state = dot(
            jnp.concatenate([key["k_t"], key["k_t"]], axis=1), jnp.concatenate(faded, axis=0)
        )
        high, low = halves(jnp.exp(last) * identity - state[:, :DK])
        maps_ref[j, :, :DK] = high
        maps_ref[j, :, DK : 2 * DK] = low
        maps_ref[j, :, 2 * DK :] = state[:, DK:].astype(BF16)
        mixed = halves(ratios[j] * key["scores"])
        both_halves = halves(both)
        out = dot(
            jnp.concatenate(mixed, axis=1), jnp.concatenate([both_halves[0], both_halves[0]], axis=0)
        ) + dot(mixed[0], both_halves[1])
        mix_ref[j, :, :DK] = key["q"] * jnp.exp(logs) - out[:, :DK]
        mix_ref[j, :, DK:] = out[:, DK:]


def local_terms(query_input, key_input, value_input, write_strength, decay_rate):
    n = key_input.shape[0]
    groups, per_key = GROUP_VALUE_HEADS // HEADS_STEP, GROUP_VALUE_HEADS // HK
    lower = jnp.tril(jnp.ones((n, n), F32))
    logs = jnp.dot(lower, -decay_rate, precision=lax.Precision.HIGHEST)

    def columns(x):
        return jnp.swapaxes(x.reshape(n, groups, HEADS_STEP), 0, 1)

    def rows(x):
        return x.T.reshape(groups, HEADS_STEP, n)

    wide = HEADS_STEP // per_key * DK
    column_spec = pl.BlockSpec((1, n, HEADS_STEP), lambda i: (i, 0, 0))
    row_spec = pl.BlockSpec((1, HEADS_STEP, n), lambda i: (i, 0, 0))
    out_spec = pl.BlockSpec((HEADS_STEP, DK, 2 * DK + DV), lambda i: (i, 0, 0))
    mix_spec = pl.BlockSpec((HEADS_STEP, n, DK + DV), lambda i: (i, 0, 0))
    return pl.pallas_call(
        local_kernel,
        grid=(groups,),
        in_specs=[
            pl.BlockSpec((n, wide), lambda i: (0, i)),
            pl.BlockSpec((n, wide), lambda i: (0, i)),
            pl.BlockSpec((n, HEADS_STEP * DV), lambda i: (0, i)),
            column_spec,
            row_spec,
            row_spec,
            column_spec,
        ],
        out_specs=[out_spec, mix_spec],
        out_shape=[
            jax.ShapeDtypeStruct((GROUP_VALUE_HEADS, DK, 2 * DK + DV), BF16),
            jax.ShapeDtypeStruct((GROUP_VALUE_HEADS, n, DK + DV), F32),
        ],
        compiler_params=pltpu.CompilerParams(vmem_limit_bytes=40 * MIB),
        name="local_terms",
    )(
        query_input,
        key_input,
        value_input,
        columns(logs),
        rows(logs),
        rows(write_strength),
        columns(write_strength),
    )


def chain_kernel(maps_ref, before_ref, whole_ref):
    row = lax.broadcasted_iota(jnp.int32, (DK, DK + DV), 0)
    column = lax.broadcasted_iota(jnp.int32, (DK, DK + DV), 1)
    passed = (row == column).astype(F32)
    for i in range(maps_ref.shape[0]):
        before_ref[i] = passed
        high, low = halves(passed)
        passed = dot(maps_ref[i, :, : 2 * DK], jnp.concatenate([high, high], axis=0)) + dot(
            maps_ref[i, :, :DK], low
        )
        passed = jnp.concatenate(
            [passed[:, :DK], passed[:, DK:] + maps_ref[i, :, 2 * DK :].astype(F32)], axis=1
        )
    whole_ref[...] = passed


def chain(maps):
    count = maps.shape[0]
    return pl.pallas_call(
        chain_kernel,
        out_shape=[
            jax.ShapeDtypeStruct((count, DK, DK + DV), F32),
            jax.ShapeDtypeStruct((DK, DK + DV), F32),
        ],
        compiler_params=pltpu.CompilerParams(vmem_limit_bytes=40 * MIB),
        name="chain",
    )(maps)


def entering_states(maps, devices):
    heads = maps.shape[0]
    segments = devices // heads
    groups = [[g * heads + h for h in range(heads)] for g in range(segments)]
    by_device = lax.all_to_all(
        maps, AXES, split_axis=0, concat_axis=0, axis_index_groups=groups, tiled=True
    )
    before, whole = chain(by_device)
    across = [[g * heads + h for g in range(segments)] for h in range(heads)]
    adds = lax.all_gather(whole[:, DK:], AXES, axis_index_groups=across)
    segment = lax.axis_index(AXES) // heads
    carry = adds[0]
    start = jnp.where(segment == 1, carry, 0.0)
    if segments > 2:
        steps = lax.all_gather(whole[:, :DK], AXES, axis_index_groups=across)
        for g in range(2, segments):
            carry = adds[g - 1] + jnp.dot(steps[g - 1], carry, precision=lax.Precision.HIGHEST)
            start = jnp.where(segment == g, carry, start)
    states = (
        jnp.dot(
            before[:, :, :DK].reshape(heads * DK, DK), start, precision=lax.Precision.HIGH
        ).reshape(heads, DK, DV)
        + before[:, :, DK:]
    ).astype(BF16)
    back = lax.all_to_all(
        states, AXES, split_axis=0, concat_axis=0, axis_index_groups=groups, tiled=True
    )
    return back, whole


def finish_kernel(
    place_ref, mix_ref, state_ref, gate_ref, gain_ref, residual_ref, post_ref, *refs
):
    *proj_refs, hidden_ref, first_ref, second_ref, core_ref = refs
    for h in range(GROUP_VALUE_HEADS):
        lanes = slice(h * DV, (h + 1) * DV)
        state = state_ref[h]
        recurrent = (
            dot(
                jnp.concatenate(halves(mix_ref[h, :, :DK]), axis=1),
                jnp.concatenate([state, state], axis=0),
            )
            + mix_ref[h, :, DK:]
        )
        inv_rms = lax.rsqrt(jnp.mean(recurrent * recurrent, axis=1, keepdims=True) + 1e-06)
        gate = gate_ref[:, lanes].astype(F32)
        act = gate / (1.0 + jnp.exp(-gate))
        core_ref[:, lanes] = (recurrent * inv_rms * gain_ref[...] * act).astype(BF16)
    core = core_ref[...]
    squares = 0.0
    pieces = [ref.at[i] for ref in proj_refs for i in range(ref.shape[0])]
    for i, proj_ref in enumerate(pieces):
        wide = proj_ref.shape[1]
        lanes = pl.ds(pl.multiple_of(place_ref[i] * wide, wide), wide)
        hidden = (residual_ref[:, lanes].astype(F32) + dot(core, proj_ref[...])).astype(BF16)
        hidden_ref[:, lanes] = hidden
        widened = hidden.astype(F32)
        squares += jnp.sum(widened * widened, axis=1, keepdims=True)
    inv_rms = lax.rsqrt(squares * (1.0 / D) + 1e-06)
    normed = (hidden_ref[...].astype(F32) * inv_rms * post_ref[...]).astype(BF16)
    first_ref[...] = normed[:, :SPLIT]
    second_ref[...] = normed[:, SPLIT:]


def finish(mix, states, out_gate, head_gain, proj, places, residual_in, post_gain):
    shape = residual_in.shape
    vmem = pl.BlockSpec(memory_space=pltpu.VMEM)
    return pl.pallas_call(
        finish_kernel,
        in_specs=[pl.BlockSpec(memory_space=pltpu.SMEM)] + [vmem] * (6 + len(proj)),
        out_shape=[
            jax.ShapeDtypeStruct((shape[0], wide), BF16) for wide in (D, SPLIT, D - SPLIT)
        ],
        scratch_shapes=[pltpu.VMEM(shape, BF16)],
        compiler_params=pltpu.CompilerParams(vmem_limit_bytes=48 * MIB),
        name="finish",
    )(
        places,
        mix,
        states,
        out_gate,
        head_gain.reshape(1, DV),
        residual_in,
        post_gain.reshape(1, D),
        *proj,
    )


def hidden_units_kernel(
    capacity,
    place_ref,
    slot_row_ref,
    slot_ref,
    weight_ref,
    own_gate_ref,
    own_up_ref,
    other_gate_ref,
    other_up_ref,
    *refs,
):
    *token_refs, inner_ref, spread_ref, block_ref, taken_ref, sems = refs
    group, expert = pl.program_id(0), pl.program_id(1)
    blocks, rows, _ = block_ref.shape
    served = taken_ref.shape[0]
    rest = len(token_refs) // 2
    joined = max(1, 16 // capacity)

    def copies(b):
        source = place_ref[0] ^ (group * (blocks // rest) + b // rest)
        lanes = (slice(0, SPLIT), slice(SPLIT, D))
        return [
            pltpu.make_async_copy(
                token_refs[part * rest + b % rest].at[source],
                block_ref.at[b, :, lanes[part]],
                sems.at[b, part],
            )
            for part in range(2)
        ]

    @pl.when(expert == 0)
    def _():
        for b in range(blocks):
            for copy in copies(b):
                copy.start()
        slot_ids = lax.broadcasted_iota(jnp.int32, (capacity, rows), 0).astype(F32)
        for first in range(0, blocks, joined):
            picked = []
            for b in range(first, first + joined):
                chosen = jnp.concatenate(
                    [(slot_row_ref[b, e : e + 1, :] == slot_ids).astype(F32) for e in range(served)],
                    axis=0,
                ).astype(BF16)
                for copy in copies(b):
                    copy.wait()
                picked.append(dot(chosen, block_ref[b]))
            for e in range(served):
                part = [p[e * capacity : (e + 1) * capacity] for p in picked]
                taken_ref[e, first * capacity : (first + joined) * capacity] = jnp.concatenate(
                    part, axis=0
                ).astype(BF16)

    def serve(gate_ref, up_ref):
        received = taken_ref[expert]
        gate = dot(received, gate_ref[0])
        up = dot(received, up_ref[0])
        inner_ref[0] = (gate / (1.0 + jnp.exp(-gate)) * up).astype(BF16)

    @pl.when(expert < served // 2)
    def _():
        serve(own_gate_ref, own_up_ref)

    @pl.when(expert >= served // 2)
    def _():
        serve(other_gate_ref, other_up_ref)

    span = served * capacity
    lane = lax.broadcasted_iota(jnp.int32, (rows, 2 * span), 1)
    lane_expert, lane_slot = lane // capacity % served, (lane % capacity).astype(F32)
    share = blocks // served
    for i in range(share):
        b = expert * share + i
        slots, weights = slot_ref[b], weight_ref[b]
        slot = jnp.full((rows, 2 * span), -1.0, F32)
        weight = jnp.zeros((rows, 2 * span), F32)
        for e in range(served):
            slot = jnp.where(lane_expert == e, slots[:, e : e + 1], slot)
            weight = jnp.where(lane_expert == e, weights[:, e : e + 1], weight)
        high = weight.astype(BF16).astype(F32)
        spread_ref[b] = jnp.where(
            slot == lane_slot, jnp.where(lane < span, high, weight - high), 0.0
        ).astype(BF16)


def hidden_units(tokens, place, weights, own, other, capacity):
    devices, served, rows = weights.shape
    local = own[0].shape[0]
    width = own[0].shape[2]
    named = weights > 0.0
    rank = jnp.einsum(
        "set,tu->seu",
        named.astype(BF16),
        jnp.triu(jnp.ones((rows, rows), BF16)),
        preferred_element_type=F32,
    )
    slots = jnp.where(named, rank - 1.0, -1.0)

    def own_spec(x):
        return pl.BlockSpec((1,) + x.shape[1:], lambda g, e: (jnp.minimum(e, local - 1), 0, 0))

    def other_spec(x):
        return pl.BlockSpec((1,) + x.shape[1:], lambda g, e: (jnp.maximum(e - local, 0), 0, 0))

    column_spec = pl.BlockSpec((BLOCKS_STEP, rows, served), lambda g, e: (g, 0, 0))
    return pl.pallas_call(
        functools.partial(hidden_units_kernel, capacity),
        grid=(devices // BLOCKS_STEP, served),
        in_specs=[
            pl.BlockSpec(memory_space=pltpu.SMEM),
            pl.BlockSpec((BLOCKS_STEP, served, rows), lambda g, e: (g, 0, 0)),
            column_spec,
            column_spec,
        ]
        + [own_spec(x) for x in own]
        + [other_spec(x) for x in other]
        + [pl.BlockSpec(memory_space=pl.ANY)] * len(tokens),
        out_specs=[
            pl.BlockSpec((1, BLOCKS_STEP * capacity, width), lambda g, e: (e, g, 0)),
            pl.BlockSpec((BLOCKS_STEP, rows, 2 * served * capacity), lambda g, e: (g, 0, 0)),
        ],
        out_shape=[
            jax.ShapeDtypeStruct((served, devices * capacity, width), BF16),
            jax.ShapeDtypeStruct((devices, rows, 2 * served * capacity), BF16),
        ],
        scratch_shapes=[
            pltpu.VMEM((BLOCKS_STEP, rows, D), BF16),
            pltpu.VMEM((served, BLOCKS_STEP * capacity, D), BF16),
            pltpu.SemaphoreType.DMA((BLOCKS_STEP, 2)),
        ],
        compiler_params=pltpu.CompilerParams(vmem_limit_bytes=56 * MIB),
        name="hidden_units",
    )(place, slots, jnp.swapaxes(slots, 1, 2), jnp.swapaxes(weights, 1, 2), *own, *other, *tokens)


def order_places(order):
    count = len(order)
    return [
        sum(((j >> (count - 1 - k)) & 1) << bit for k, bit in enumerate(order))
        for j in range(1 << count)
    ]


def down_kernel(capacity, order, inner_ref, spread_ref, own_ref, other_ref, keep_ref, send_ref, out_ref):
    served = inner_ref.shape[0]
    local = served // 2
    for e in range(served):
        down = own_ref[e] if e < local else other_ref[e - local]
        out_ref[e] = dot(inner_ref[e], down)
    places = order_places(order)
    half = len(places) // 2
    for j, place in enumerate(places):
        mine = [out_ref[e, place * capacity : (place + 1) * capacity] for e in range(served)]
        stacked = jnp.concatenate(mine, axis=0).astype(BF16)
        block = dot(spread_ref[place], jnp.concatenate([stacked, stacked], axis=0)).astype(BF16)
        if j < half:
            keep_ref[j] = block
        else:
            send_ref[j - half] = block


def down_strips(inner, spread, own, other, capacity, order, start, width):
    served, slots, units = inner.shape
    devices, rows, _ = spread.shape
    first = start // STRIP

    def whole(x):
        return pl.BlockSpec(x.shape, lambda i: (0, 0, 0), pipeline_mode=pl.Buffered(1))

    down_spec = pl.BlockSpec((own.shape[0], units, STRIP), lambda i: (0, 0, first + i))
    half_spec = pl.BlockSpec((devices // 2, rows, STRIP), lambda i: (0, 0, i))
    half_shape = jax.ShapeDtypeStruct((devices // 2, rows, width), BF16)
    return pl.pallas_call(
        functools.partial(down_kernel, capacity, order),
        grid=(width // STRIP,),
        in_specs=[whole(inner), whole(spread), down_spec, down_spec],
        out_specs=[half_spec, half_spec],
        out_shape=[half_shape, half_shape],
        scratch_shapes=[pltpu.VMEM((served, slots, STRIP), F32)],
        compiler_params=pltpu.CompilerParams(vmem_limit_bytes=48 * MIB),
        name="down_strips",
    )(inner, spread, own, other)


def sum_by_halving(keep, send, order):
    for bit in order[:-1]:
        total = (keep.astype(F32) + place_flip(send, bit).astype(F32)).astype(BF16)
        half = total.shape[0] // 2
        keep, send = total[:half], total[half:]
    return keep[0].astype(F32) + place_flip(send, order[-1])[0].astype(F32)


def routing(expert_ids, gate_weights, local_experts):
    outer, cores, inner = (lax.axis_size(a) for a in (("outer", "mid"), "core", "inner"))
    rows = expert_ids.shape[0]
    experts = local_experts * outer * cores * inner
    chosen = expert_ids.T[None] == jnp.arange(experts, dtype=jnp.int32)[:, None, None]
    dense = jnp.sum(jnp.where(chosen, gate_weights.T[None], 0.0), axis=1)
    by_chip = jnp.swapaxes(dense.reshape(outer, cores, inner, local_experts * rows), 1, 2)
    by_chip = by_chip.reshape(outer * inner, cores * local_experts, rows)
    weights = lax.all_to_all(by_chip, SAME_CORE, split_axis=0, concat_axis=0, tiled=True)
    turned = jnp.concatenate([weights[:, local_experts:], weights[:, :local_experts]], axis=1)
    weights = jnp.where(lax.axis_index("core") == 1, turned, weights)
    return jnp.take(weights, lax.axis_index(SAME_CORE) ^ jnp.arange(outer * inner), axis=0)


def flipped(array, bit):
    devices = lax.axis_size(AXES)
    return lax.ppermute(array, AXES, [(i, i ^ bit) for i in range(devices)])


def place_flip(array, bit):
    return flipped(array, 1 << (bit if 1 << bit < lax.axis_size("inner") else bit + 1))


def over_rest(array):
    pieces = [array]
    for bit in range(lax.axis_size(REST).bit_length() - 1):
        pieces = pieces + [place_flip(piece, bit) for piece in pieces]
    return pieces


def shards(
    split_core,
    residual_in,
    query_input,
    key_input,
    value_input,
    out_gate,
    write_strength,
    decay_rate,
    head_gain,
    out_proj,
    post_gain,
    expert_ids,
    gate_weights,
    expert_gate,
    expert_up,
    expert_down,
):
    tok_rows = residual_in.shape[0]
    devices = lax.axis_size(AXES)
    inner_size = lax.axis_size("inner")
    local_experts = expert_gate.shape[0]
    capacity = max(2, tok_rows * TOP * 8 // (5 * local_experts * devices))
    proj = lax.all_gather(out_proj, REST)
    weights = routing(expert_ids, gate_weights, local_experts)
    other_gate, other_up, other_down = (
        flipped(x, inner_size) for x in (expert_gate, expert_up, expert_down)
    )
    maps, mix = local_terms(query_input, key_input, value_input, write_strength, decay_rate)
    states, whole = entering_states(maps, devices)
    pieces = jnp.arange(proj.shape[0], dtype=jnp.int32)
    if split_core:
        core = lax.axis_index("core")
        ready, _ = lax.optimization_barrier((proj, whole))
        proj = (ready, flipped(ready, inner_size))
        base = pieces // inner_size * (2 * inner_size) + pieces % inner_size
        places = jnp.concatenate([base + core * inner_size, base + (1 - core) * inner_size])
    else:
        proj, places = (proj,), pieces
    hidden, first, second = finish(
        mix, states, out_gate, head_gain, proj, places, residual_in, post_gain
    )
    tokens = over_rest(lax.all_gather(first, "outer"))
    tokens = tokens + [lax.all_gather(piece, "outer") for piece in over_rest(second)]
    inner, spread = hidden_units(
        tokens,
        lax.axis_index("outer").reshape(1),
        weights,
        (expert_gate, expert_up),
        (other_gate, other_up),
        capacity,
    )
    bits = tuple(range(weights.shape[0].bit_length() - 1))
    sums, start = [], 0
    for width, order in (
        (768, bits),
        (768, (bits[1], bits[0]) + bits[2:]),
        (512, bits[2:] + bits[:2]),
    ):
        keep, send = down_strips(
            inner, spread, expert_down, other_down, capacity, order, start, width
        )
        sums.append(sum_by_halving(keep, send, order))
        start += width
    return (hidden.astype(F32) + jnp.concatenate(sums, axis=1)).astype(BF16)


def core_stride(devices):
    first = getattr(devices[0], "coords", None)
    for i in range(1, len(devices)):
        if first is not None and tuple(devices[i].coords) == tuple(first):
            return i
    return 1


def solution(mesh):
    devices = mesh.devices.reshape(-1)
    inner = core_stride(devices)
    columns = mesh.shape["exp"]
    if 2 * inner <= columns:
        shape, column_axes = (-1, columns // (2 * inner), 2, inner), AXES[1:]
    else:
        shape, column_axes = (-1, 1, 2, inner), ("inner",)
    split_core = "core" in column_axes
    view = Mesh(devices.reshape(shape), AXES)
    rows = P(AXES, None)
    placed = (
        (rows,) * 7 + (P(), P(None, column_axes), P(), rows, rows) + (P(AXES, None, None),) * 3
    )
    body = functools.partial(shards, split_core)
    return jax.shard_map(body, mesh=view, in_specs=placed, out_specs=rows, check_vma=False)
```

```python
import functools

import jax
import jax.numpy as jnp
from jax import lax
from jax.experimental import pallas as pl
from jax.experimental.pallas import tpu as pltpu
from jax.sharding import Mesh, PartitionSpec as P

D = 2048
HK = 8
GROUP_VALUE_HEADS = 16
DK = 128
DV = 128
TOP = 10
HEADS_STEP = 4
BLOCKS_STEP = 16
GROUPS = (768, 768, 512)
STRIP = 256

F32 = jnp.float32
BF16 = jnp.bfloat16
AXES = ("outer", "mid", "core", "inner")
SAME_CORE = ("outer", "mid", "inner")
REST = ("mid", "inner")
MIB = 1 << 20


def halves(x):
    high = x.astype(BF16)
    return high, (x - high.astype(F32)).astype(BF16)


def dot(a, b):
    return jnp.dot(a, b, preferred_element_type=F32)


def product(left, right):
    n = right[0].shape[1]
    lhs = jnp.concatenate(left, axis=1)
    top = jnp.concatenate(right, axis=1)
    bottom = jnp.concatenate([right[0], jnp.zeros_like(right[0])], axis=1)
    both = dot(lhs, jnp.concatenate([top, bottom], axis=0))
    return both[:, :n] + both[:, n:]


def local_kernel(q_ref, k_ref, v_ref, logs_ref, logs_row_ref, strength_row_ref, strength_ref, maps_ref, mix_ref):
    n = k_ref.shape[0]
    row = lax.broadcasted_iota(jnp.int32, (n, n), 0)
    column = lax.broadcasted_iota(jnp.int32, (n, n), 1)
    inclusive, strict, diagonal = row >= column, row > column, row == column
    heads = maps_ref.shape[0]
    group = GROUP_VALUE_HEADS // HK
    identity = diagonal.astype(F32)

    keys = []
    for i in range(heads // group):
        lanes = slice(i * DK, (i + 1) * DK)
        k_raw, q_raw = k_ref[:, lanes], q_ref[:, lanes]
        k_wide, q_wide = k_raw.astype(F32), q_raw.astype(F32)
        dims = (((1,), (1,)), ((), ()))
        gram = lax.dot_general(k_raw, k_raw, dims, preferred_element_type=F32)
        scores = lax.dot_general(q_raw, k_raw, dims, preferred_element_type=F32)
        inv_k = lax.rsqrt(jnp.sum(k_wide * k_wide, axis=1, keepdims=True) + 1e-06)
        inv_k_row = lax.rsqrt(jnp.sum(jnp.where(diagonal, gram, 0.0), axis=0, keepdims=True) + 1e-06)
        inv_q = lax.rsqrt(jnp.sum(q_wide * q_wide, axis=1, keepdims=True) + 1e-06) * DK ** (-0.5)
        keys.append(
            dict(
                k=k_raw,
                k_t=jnp.transpose(k_wide).astype(BF16),
                q=q_wide * inv_q,
                gram=gram * inv_k * inv_k_row,
                scores=scores * inv_q * inv_k_row,
                inv=inv_k,
                inv_row=inv_k_row,
            )
        )

    ratios, systems, inverses = [], [], []
    for j in range(heads):
        logs, logs_row = logs_ref[0][:, j : j + 1], logs_row_ref[0][j : j + 1, :]
        ratio = jnp.where(inclusive, jnp.exp(jnp.where(inclusive, logs - logs_row, 0.0)), 0.0)
        system = jnp.where(strict, ratio * keys[j // group]["gram"], 0.0) * strength_ref[0][:, j : j + 1]
        first = (row // 2 == column // 2) & strict
        ratios.append(ratio)
        systems.append(halves(system))
        inverses.append(identity - jnp.where(first, system, 0.0))
    size = 2
    while size < n:
        pairs = (row // (2 * size) == column // (2 * size)) & (row // size > column // size)
        inverse_halves = [halves(t) for t in inverses]
        cut = [
            tuple(jnp.where(pairs, part.astype(F32), 0.0).astype(BF16) for part in s) for s in systems
        ]
        left = [product(t, c) for t, c in zip(inverse_halves, cut)]
        inverses = [
            t - product(halves(x), th) for t, x, th in zip(inverses, left, inverse_halves)
        ]
        size *= 2

    for j in range(heads):
        key = keys[j // group]
        logs, logs_row = logs_ref[0][:, j : j + 1], logs_row_ref[0][j : j + 1, :]
        strength_row = strength_row_ref[0][j : j + 1, :]
        value = v_ref[:, j * DV : (j + 1) * DV]
        t = inverses[j]
        new_value = dot(
            jnp.concatenate(halves(t * strength_row), axis=1), jnp.concatenate([value, value], axis=0)
        )
        key_matrix = dot(
            jnp.concatenate(halves(t * (strength_row * jnp.exp(logs_row) * key["inv_row"])), axis=1),
            jnp.concatenate([key["k"], key["k"]], axis=0),
        )
        both = jnp.concatenate([key_matrix, new_value], axis=1)
        last = logs[n - 1 : n, :]
        faded = halves(both * (jnp.exp(last - logs) * key["inv"]))
        state = dot(
            jnp.concatenate([key["k_t"], key["k_t"]], axis=1), jnp.concatenate(faded, axis=0)
        )
        high, low = halves(jnp.exp(last) * identity - state[:, :DK])
        maps_ref[j, :, :DK] = high
        maps_ref[j, :, DK : 2 * DK] = low
        maps_ref[j, :, 2 * DK :] = state[:, DK:].astype(BF16)
        mixed = halves(ratios[j] * key["scores"])
        both_halves = halves(both)
        out = dot(
            jnp.concatenate(mixed, axis=1), jnp.concatenate([both_halves[0], both_halves[0]], axis=0)
        ) + dot(mixed[0], both_halves[1])
        mix_ref[j, :, :DK] = key["q"] * jnp.exp(logs) - out[:, :DK]
        mix_ref[j, :, DK:] = out[:, DK:]


def local_terms(query_input, key_input, value_input, write_strength, decay_rate):
    n = key_input.shape[0]
    groups, per_key = GROUP_VALUE_HEADS // HEADS_STEP, GROUP_VALUE_HEADS // HK
    lower = jnp.tril(jnp.ones((n, n), F32))
    logs = jnp.dot(lower, -decay_rate, precision=lax.Precision.HIGHEST)

    def columns(x):
        return jnp.swapaxes(x.reshape(n, groups, HEADS_STEP), 0, 1)

    def rows(x):
        return x.T.reshape(groups, HEADS_STEP, n)

    wide = HEADS_STEP // per_key * DK
    column_spec = pl.BlockSpec((1, n, HEADS_STEP), lambda i: (i, 0, 0))
    row_spec = pl.BlockSpec((1, HEADS_STEP, n), lambda i: (i, 0, 0))
    out_spec = pl.BlockSpec((HEADS_STEP, DK, 2 * DK + DV), lambda i: (i, 0, 0))
    mix_spec = pl.BlockSpec((HEADS_STEP, n, DK + DV), lambda i: (i, 0, 0))
    return pl.pallas_call(
        local_kernel,
        grid=(groups,),
        in_specs=[
            pl.BlockSpec((n, wide), lambda i: (0, i)),
            pl.BlockSpec((n, wide), lambda i: (0, i)),
            pl.BlockSpec((n, HEADS_STEP * DV), lambda i: (0, i)),
            column_spec,
            row_spec,
            row_spec,
            column_spec,
        ],
        out_specs=[out_spec, mix_spec],
        out_shape=[
            jax.ShapeDtypeStruct((GROUP_VALUE_HEADS, DK, 2 * DK + DV), BF16),
            jax.ShapeDtypeStruct((GROUP_VALUE_HEADS, n, DK + DV), F32),
        ],
        compiler_params=pltpu.CompilerParams(vmem_limit_bytes=40 * MIB),
        name="local_terms",
    )(
        query_input,
        key_input,
        value_input,
        columns(logs),
        rows(logs),
        rows(write_strength),
        columns(write_strength),
    )


def chain_kernel(maps_ref, before_ref, whole_ref):
    row = lax.broadcasted_iota(jnp.int32, (DK, DK + DV), 0)
    column = lax.broadcasted_iota(jnp.int32, (DK, DK + DV), 1)
    passed = (row == column).astype(F32)
    for i in range(maps_ref.shape[0]):
        before_ref[i] = passed
        high, low = halves(passed)
        passed = dot(maps_ref[i, :, : 2 * DK], jnp.concatenate([high, high], axis=0)) + dot(
            maps_ref[i, :, :DK], low
        )
        passed = jnp.concatenate(
            [passed[:, :DK], passed[:, DK:] + maps_ref[i, :, 2 * DK :].astype(F32)], axis=1
        )
    whole_ref[...] = passed


def chain(maps):
    count = maps.shape[0]
    return pl.pallas_call(
        chain_kernel,
        out_shape=[
            jax.ShapeDtypeStruct((count, DK, DK + DV), F32),
            jax.ShapeDtypeStruct((DK, DK + DV), F32),
        ],
        compiler_params=pltpu.CompilerParams(vmem_limit_bytes=40 * MIB),
        name="chain",
    )(maps)


def entering_states(maps, devices):
    heads = maps.shape[0]
    segments = devices // heads
    groups = [[g * heads + h for h in range(heads)] for g in range(segments)]
    by_device = lax.all_to_all(
        maps, AXES, split_axis=0, concat_axis=0, axis_index_groups=groups, tiled=True
    )
    before, whole = chain(by_device)
    across = [[g * heads + h for g in range(segments)] for h in range(heads)]
    adds = lax.all_gather(whole[:, DK:], AXES, axis_index_groups=across)
    segment = lax.axis_index(AXES) // heads
    carry = adds[0]
    start = jnp.where(segment == 1, carry, 0.0)
    if segments > 2:
        steps = lax.all_gather(whole[:, :DK], AXES, axis_index_groups=across)
        for g in range(2, segments):
            carry = adds[g - 1] + jnp.dot(steps[g - 1], carry, precision=lax.Precision.HIGHEST)
            start = jnp.where(segment == g, carry, start)
    states = (
        jnp.dot(
            before[:, :, :DK].reshape(heads * DK, DK), start, precision=lax.Precision.HIGH
        ).reshape(heads, DK, DV)
        + before[:, :, DK:]
    ).astype(BF16)
    back = lax.all_to_all(
        states, AXES, split_axis=0, concat_axis=0, axis_index_groups=groups, tiled=True
    )
    return back, whole


def finish_kernel(
    place_ref, mix_ref, state_ref, gate_ref, gain_ref, residual_ref, post_ref, *refs
):
    *proj_refs, hidden_ref, first_ref, second_ref, third_ref, core_ref = refs
    for h in range(GROUP_VALUE_HEADS):
        lanes = slice(h * DV, (h + 1) * DV)
        state = state_ref[h]
        recurrent = (
            dot(
                jnp.concatenate(halves(mix_ref[h, :, :DK]), axis=1),
                jnp.concatenate([state, state], axis=0),
            )
            + mix_ref[h, :, DK:]
        )
        inv_rms = lax.rsqrt(jnp.mean(recurrent * recurrent, axis=1, keepdims=True) + 1e-06)
        gate = gate_ref[:, lanes].astype(F32)
        act = gate / (1.0 + jnp.exp(-gate))
        core_ref[:, lanes] = (recurrent * inv_rms * gain_ref[...] * act).astype(BF16)
    core = core_ref[...]
    squares = 0.0
    for i, proj_ref in enumerate(proj_refs):
        wide = proj_ref.shape[1]
        lanes = pl.ds(pl.multiple_of(place_ref[i] * wide, wide), wide)
        hidden = (residual_ref[:, lanes].astype(F32) + dot(core, proj_ref[...])).astype(BF16)
        hidden_ref[:, lanes] = hidden
        widened = hidden.astype(F32)
        squares += jnp.sum(widened * widened, axis=1, keepdims=True)
    inv_rms = lax.rsqrt(squares * (1.0 / D) + 1e-06)
    normed = (hidden_ref[...].astype(F32) * inv_rms * post_ref[...]).astype(BF16)
    start = 0
    for ref, width in zip((first_ref, second_ref, third_ref), GROUPS):
        ref[...] = normed[:, start : start + width]
        start += width


def finish(mix, states, out_gate, head_gain, proj, places, residual_in, post_gain):
    shape = residual_in.shape
    vmem = pl.BlockSpec(memory_space=pltpu.VMEM)
    return pl.pallas_call(
        finish_kernel,
        in_specs=[pl.BlockSpec(memory_space=pltpu.SMEM)] + [vmem] * (6 + len(proj)),
        out_shape=[
            jax.ShapeDtypeStruct((shape[0], wide), BF16) for wide in (D,) + GROUPS
        ],
        scratch_shapes=[pltpu.VMEM(shape, BF16)],
        compiler_params=pltpu.CompilerParams(vmem_limit_bytes=48 * MIB),
        name="finish",
    )(
        places,
        mix,
        states,
        out_gate,
        head_gain.reshape(1, DV),
        residual_in,
        post_gain.reshape(1, D),
        *proj,
    )


def hidden_units_kernel(
    capacity,
    pieces,
    slot_row_ref,
    slot_ref,
    weight_ref,
    own_gate_ref,
    own_up_ref,
    other_gate_ref,
    other_up_ref,
    *refs,
):
    *token_refs, inner_ref, spread_ref, block_ref, taken_ref, sems = refs
    group, expert = pl.program_id(0), pl.program_id(1)
    blocks, rows, _ = block_ref.shape
    served = taken_ref.shape[0]
    joined = max(1, 16 // capacity)

    def copies(step, b):
        found = []
        start = 0
        for part, width in enumerate(GROUPS):
            for ref, (column, places) in zip(token_refs, pieces):
                place = step * blocks + b
                if column == part and place in places:
                    found.append(
                        pltpu.make_async_copy(
                            ref.at[places.index(place)],
                            block_ref.at[b, :, start : start + width],
                            sems.at[b, part],
                        )
                    )
            start += width
        return found

    def load(step):
        @pl.when((expert == 0) & (group == step))
        def _():
            for b in range(blocks):
                for copy in copies(step, b):
                    copy.start()

    for step in range(sum(len(places) for column, places in pieces if column == 0) // blocks):
        load(step)

    @pl.when(expert == 0)
    def _():
        slot_ids = lax.broadcasted_iota(jnp.int32, (capacity, rows), 0).astype(F32)
        for first in range(0, blocks, joined):
            picked = []
            for b in range(first, first + joined):
                chosen = jnp.concatenate(
                    [(slot_row_ref[b, e : e + 1, :] == slot_ids).astype(F32) for e in range(served)],
                    axis=0,
                ).astype(BF16)
                for copy in copies(0, b):
                    copy.wait()
                picked.append(dot(chosen, block_ref[b]))
            for e in range(served):
                part = [p[e * capacity : (e + 1) * capacity] for p in picked]
                taken_ref[e, first * capacity : (first + joined) * capacity] = jnp.concatenate(
                    part, axis=0
                ).astype(BF16)

    def serve(gate_ref, up_ref):
        received = taken_ref[expert]
        gate = dot(received, gate_ref[0])
        up = dot(received, up_ref[0])
        inner_ref[0] = (gate / (1.0 + jnp.exp(-gate)) * up).astype(BF16)

    @pl.when(expert < served // 2)
    def _():
        serve(own_gate_ref, own_up_ref)

    @pl.when(expert >= served // 2)
    def _():
        serve(other_gate_ref, other_up_ref)

    span = served * capacity
    lane = lax.broadcasted_iota(jnp.int32, (rows, 2 * span), 1)
    lane_expert, lane_slot = lane // capacity % served, (lane % capacity).astype(F32)
    share = blocks // served
    for i in range(share):
        b = expert * share + i
        slots, weights = slot_ref[b], weight_ref[b]
        slot = jnp.full((rows, 2 * span), -1.0, F32)
        weight = jnp.zeros((rows, 2 * span), F32)
        for e in range(served):
            slot = jnp.where(lane_expert == e, slots[:, e : e + 1], slot)
            weight = jnp.where(lane_expert == e, weights[:, e : e + 1], weight)
        high = weight.astype(BF16).astype(F32)
        spread_ref[b] = jnp.where(
            slot == lane_slot, jnp.where(lane < span, high, weight - high), 0.0
        ).astype(BF16)


def hidden_units(tokens, weights, own, other, capacity):
    devices, served, rows = weights.shape
    local = own[0].shape[0]
    width = own[0].shape[2]
    pieces = [(column, places) for column, places, _ in tokens]
    named = weights > 0.0
    rank = jnp.einsum(
        "set,tu->seu",
        named.astype(BF16),
        jnp.triu(jnp.ones((rows, rows), BF16)),
        preferred_element_type=F32,
    )
    slots = jnp.where(named, rank - 1.0, -1.0)

    def own_spec(x):
        return pl.BlockSpec((1,) + x.shape[1:], lambda g, e: (jnp.minimum(e, local - 1), 0, 0))

    def other_spec(x):
        return pl.BlockSpec((1,) + x.shape[1:], lambda g, e: (jnp.maximum(e - local, 0), 0, 0))

    column_spec = pl.BlockSpec((BLOCKS_STEP, rows, served), lambda g, e: (g, 0, 0))
    return pl.pallas_call(
        functools.partial(hidden_units_kernel, capacity, pieces),
        grid=(devices // BLOCKS_STEP, served),
        in_specs=[
            pl.BlockSpec((BLOCKS_STEP, served, rows), lambda g, e: (g, 0, 0)),
            column_spec,
            column_spec,
        ]
        + [own_spec(x) for x in own]
        + [other_spec(x) for x in other]
        + [pl.BlockSpec(memory_space=pl.ANY)] * len(tokens),
        out_specs=[
            pl.BlockSpec((1, BLOCKS_STEP * capacity, width), lambda g, e: (e, g, 0)),
            pl.BlockSpec((BLOCKS_STEP, rows, 2 * served * capacity), lambda g, e: (g, 0, 0)),
        ],
        out_shape=[
            jax.ShapeDtypeStruct((served, devices * capacity, width), BF16),
            jax.ShapeDtypeStruct((devices, rows, 2 * served * capacity), BF16),
        ],
        scratch_shapes=[
            pltpu.VMEM((BLOCKS_STEP, rows, D), BF16),
            pltpu.VMEM((served, BLOCKS_STEP * capacity, D), BF16),
            pltpu.SemaphoreType.DMA((BLOCKS_STEP, len(GROUPS))),
        ],
        compiler_params=pltpu.CompilerParams(vmem_limit_bytes=56 * MIB),
        name="hidden_units",
    )(
        slots,
        jnp.swapaxes(slots, 1, 2),
        jnp.swapaxes(weights, 1, 2),
        *own,
        *other,
        *[array for _, _, array in tokens],
    )


def order_places(order):
    count = len(order)
    return [
        sum(((j >> (count - 1 - k)) & 1) << bit for k, bit in enumerate(order))
        for j in range(1 << count)
    ]


def down_kernel(capacity, order, inner_ref, spread_ref, own_ref, other_ref, keep_ref, send_ref, out_ref):
    served = inner_ref.shape[0]
    local = served // 2
    for e in range(served):
        down = own_ref[e] if e < local else other_ref[e - local]
        out_ref[e] = dot(inner_ref[e], down)
    places = order_places(order)
    half = len(places) // 2
    for j, place in enumerate(places):
        mine = [out_ref[e, place * capacity : (place + 1) * capacity] for e in range(served)]
        stacked = jnp.concatenate(mine, axis=0).astype(BF16)
        block = dot(spread_ref[place], jnp.concatenate([stacked, stacked], axis=0)).astype(BF16)
        if j < half:
            keep_ref[j] = block
        else:
            send_ref[j - half] = block


def down_strips(inner, spread, own, other, capacity, order, start, width):
    served, slots, units = inner.shape
    devices, rows, _ = spread.shape
    first = start // STRIP

    def whole(x):
        return pl.BlockSpec(x.shape, lambda i: (0, 0, 0), pipeline_mode=pl.Buffered(1))

    down_spec = pl.BlockSpec((own.shape[0], units, STRIP), lambda i: (0, 0, first + i))
    half_spec = pl.BlockSpec((devices // 2, rows, STRIP), lambda i: (0, 0, i))
    half_shape = jax.ShapeDtypeStruct((devices // 2, rows, width), BF16)
    return pl.pallas_call(
        functools.partial(down_kernel, capacity, order),
        grid=(width // STRIP,),
        in_specs=[whole(inner), whole(spread), down_spec, down_spec],
        out_specs=[half_spec, half_spec],
        out_shape=[half_shape, half_shape],
        scratch_shapes=[pltpu.VMEM((served, slots, STRIP), F32)],
        compiler_params=pltpu.CompilerParams(vmem_limit_bytes=48 * MIB),
        name="down_strips",
    )(inner, spread, own, other)


def sum_by_halving(keep, send, order):
    for bit in order[:-1]:
        total = (keep.astype(F32) + place_flip(send, bit).astype(F32)).astype(BF16)
        half = total.shape[0] // 2
        keep, send = total[:half], total[half:]
    return keep[0].astype(F32) + place_flip(send, order[-1])[0].astype(F32)


def routing(expert_ids, gate_weights, local_experts):
    outer, cores, inner = (lax.axis_size(a) for a in (("outer", "mid"), "core", "inner"))
    rows = expert_ids.shape[0]
    experts = local_experts * outer * cores * inner
    chosen = expert_ids.T[None] == jnp.arange(experts, dtype=jnp.int32)[:, None, None]
    dense = jnp.sum(jnp.where(chosen, gate_weights.T[None], 0.0), axis=1)
    by_chip = jnp.swapaxes(dense.reshape(outer, cores, inner, local_experts * rows), 1, 2)
    by_chip = by_chip.reshape(outer * inner, cores * local_experts, rows)
    weights = lax.all_to_all(by_chip, SAME_CORE, split_axis=0, concat_axis=0, tiled=True)
    turned = jnp.concatenate([weights[:, local_experts:], weights[:, :local_experts]], axis=1)
    weights = jnp.where(lax.axis_index("core") == 1, turned, weights)
    return jnp.take(weights, lax.axis_index(SAME_CORE) ^ jnp.arange(outer * inner), axis=0)


def flipped(array, bit):
    devices = lax.axis_size(AXES)
    return lax.ppermute(array, AXES, [(i, i ^ bit) for i in range(devices)])


def place_flip(array, bit):
    return flipped(array, 1 << (bit if 1 << bit < lax.axis_size("inner") else bit + 1))


def over_rest(array):
    pieces = [array]
    for bit in range(lax.axis_size(REST).bit_length() - 1):
        pieces = pieces + [place_flip(piece, bit) for piece in pieces]
    return pieces


def to_everyone(array, order, joined):
    pieces = [((0,), array[None])]
    for stage, bit in enumerate(order):
        sent = pieces
        if stage in joined or stage > 3:
            sent = [
                (
                    sum((places for places, _ in pieces), ()),
                    jnp.concatenate([piece for _, piece in pieces], axis=0),
                )
            ]
            if stage > 1:
                pieces = sent
        pieces = pieces + [
            (tuple(place ^ (1 << bit) for place in places), place_flip(piece, bit))
            for places, piece in sent
        ]
    return pieces


def shards(
    split_core,
    residual_in,
    query_input,
    key_input,
    value_input,
    out_gate,
    write_strength,
    decay_rate,
    head_gain,
    out_proj,
    post_gain,
    expert_ids,
    gate_weights,
    expert_gate,
    expert_up,
    expert_down,
):
    tok_rows = residual_in.shape[0]
    devices = lax.axis_size(AXES)
    inner_size = lax.axis_size("inner")
    local_experts = expert_gate.shape[0]
    capacity = max(2, tok_rows * TOP * 8 // (5 * local_experts * devices))
    proj = over_rest(out_proj)
    weights = routing(expert_ids, gate_weights, local_experts)
    other_gate, other_up, other_down = (
        flipped(x, inner_size) for x in (expert_gate, expert_up, expert_down)
    )
    maps, mix = local_terms(query_input, key_input, value_input, write_strength, decay_rate)
    states, whole = entering_states(maps, devices)
    places = lax.axis_index(REST) ^ jnp.arange(len(proj), dtype=jnp.int32)
    if split_core:
        core = lax.axis_index("core")
        late, _ = lax.optimization_barrier((proj[1:], whole))
        proj = proj + [flipped(piece, inner_size) for piece in [out_proj] + late]
        base = places // inner_size * (2 * inner_size) + places % inner_size
        places = jnp.concatenate([base + core * inner_size, base + (1 - core) * inner_size])
    hidden, *normed = finish(
        mix, states, out_gate, head_gain, proj, places, residual_in, post_gain
    )
    normed, other_gate, other_up, other_down = lax.optimization_barrier(
        (normed, other_gate, other_up, other_down)
    )
    bits = tuple(range(weights.shape[0].bit_length() - 1))
    first, second, third = bits, (bits[1], bits[0]) + bits[2:], bits[2:] + bits[:2]
    tokens = []
    for column, (part, order, joined) in enumerate(
        zip(normed, (first, second, third), ((1,), (1,), (1, 2)))
    ):
        tokens += [
            (column, places, piece) for places, piece in to_everyone(part, order[::-1], joined)
        ]
    inner, spread = hidden_units(
        tokens, weights, (expert_gate, expert_up), (other_gate, other_up), capacity
    )
    sums, start = [], 0
    for width, order in ((512, first), (512, second), (512, third), (256, first), (256, second)):
        keep, send = down_strips(
            inner, spread, expert_down, other_down, capacity, order, start, width
        )
        sums.append(sum_by_halving(keep, send, order))
        start += width
    return (hidden.astype(F32) + jnp.concatenate(sums, axis=1)).astype(BF16)


def core_stride(devices):
    first = getattr(devices[0], "coords", None)
    for i in range(1, len(devices)):
        if first is not None and tuple(devices[i].coords) == tuple(first):
            return i
    return 1


def solution(mesh):
    devices = mesh.devices.reshape(-1)
    inner = core_stride(devices)
    columns = mesh.shape["exp"]
    if 2 * inner <= columns:
        shape, column_axes = (-1, columns // (2 * inner), 2, inner), AXES[1:]
    else:
        shape, column_axes = (-1, 1, 2, inner), ("inner",)
    split_core = "core" in column_axes
    view = Mesh(devices.reshape(shape), AXES)
    rows = P(AXES, None)
    placed = (
        (rows,) * 7 + (P(), P(None, column_axes), P(), rows, rows) + (P(AXES, None, None),) * 3
    )
    body = functools.partial(shards, split_core)
    return jax.shard_map(body, mesh=view, in_specs=placed, out_specs=rows, check_vma=False)
```

```python
import functools

import jax
import jax.numpy as jnp
from jax import lax
from jax.experimental import pallas as pl
from jax.experimental.pallas import tpu as pltpu
from jax.sharding import Mesh, PartitionSpec as P

D = 2048
HK = 8
GROUP_VALUE_HEADS = 16
DK = 128
DV = 128
TOP = 10
HEADS_STEP = 4
BLOCKS_STEP = 16
GROUPS = (768, 768, 512)
STRIP = 256
EARLY_ROWS = 768

F32 = jnp.float32
BF16 = jnp.bfloat16
AXES = ("outer", "mid", "core", "inner")
SAME_CORE = ("outer", "mid", "inner")
REST = ("mid", "inner")
MIB = 1 << 20


def halves(x):
    high = x.astype(BF16)
    return high, (x - high.astype(F32)).astype(BF16)


def dot(a, b):
    return jnp.dot(a, b, preferred_element_type=F32)


def product(left, right):
    n = right[0].shape[1]
    lhs = jnp.concatenate(left, axis=1)
    top = jnp.concatenate(right, axis=1)
    bottom = jnp.concatenate([right[0], jnp.zeros_like(right[0])], axis=1)
    both = dot(lhs, jnp.concatenate([top, bottom], axis=0))
    return both[:, :n] + both[:, n:]


def local_kernel(q_ref, k_ref, v_ref, logs_ref, logs_row_ref, strength_row_ref, strength_ref, maps_ref, mix_ref):
    n = k_ref.shape[0]
    row = lax.broadcasted_iota(jnp.int32, (n, n), 0)
    column = lax.broadcasted_iota(jnp.int32, (n, n), 1)
    inclusive, strict, diagonal = row >= column, row > column, row == column
    heads = maps_ref.shape[0]
    group = GROUP_VALUE_HEADS // HK
    identity = diagonal.astype(F32)

    keys = []
    for i in range(heads // group):
        lanes = slice(i * DK, (i + 1) * DK)
        k_raw, q_raw = k_ref[:, lanes], q_ref[:, lanes]
        k_wide, q_wide = k_raw.astype(F32), q_raw.astype(F32)
        dims = (((1,), (1,)), ((), ()))
        gram = lax.dot_general(k_raw, k_raw, dims, preferred_element_type=F32)
        scores = lax.dot_general(q_raw, k_raw, dims, preferred_element_type=F32)
        inv_k = lax.rsqrt(jnp.sum(k_wide * k_wide, axis=1, keepdims=True) + 1e-06)
        inv_k_row = lax.rsqrt(jnp.sum(jnp.where(diagonal, gram, 0.0), axis=0, keepdims=True) + 1e-06)
        inv_q = lax.rsqrt(jnp.sum(q_wide * q_wide, axis=1, keepdims=True) + 1e-06) * DK ** (-0.5)
        keys.append(
            dict(
                k=k_raw,
                k_t=jnp.transpose(k_wide).astype(BF16),
                q=q_wide * inv_q,
                gram=gram * inv_k * inv_k_row,
                scores=scores * inv_q * inv_k_row,
                inv=inv_k,
                inv_row=inv_k_row,
            )
        )

    ratios, systems, inverses = [], [], []
    for j in range(heads):
        logs, logs_row = logs_ref[0][:, j : j + 1], logs_row_ref[0][j : j + 1, :]
        ratio = jnp.where(inclusive, jnp.exp(jnp.where(inclusive, logs - logs_row, 0.0)), 0.0)
        system = jnp.where(strict, ratio * keys[j // group]["gram"], 0.0) * strength_ref[0][:, j : j + 1]
        first = (row // 2 == column // 2) & strict
        ratios.append(ratio)
        systems.append(halves(system))
        inverses.append(identity - jnp.where(first, system, 0.0))
    size = 2
    while size < n:
        pairs = (row // (2 * size) == column // (2 * size)) & (row // size > column // size)
        inverse_halves = [halves(t) for t in inverses]
        cut = [
            tuple(jnp.where(pairs, part.astype(F32), 0.0).astype(BF16) for part in s) for s in systems
        ]
        left = [product(t, c) for t, c in zip(inverse_halves, cut)]
        inverses = [
            t - product(halves(x), th) for t, x, th in zip(inverses, left, inverse_halves)
        ]
        size *= 2

    for j in range(heads):
        key = keys[j // group]
        logs, logs_row = logs_ref[0][:, j : j + 1], logs_row_ref[0][j : j + 1, :]
        strength_row = strength_row_ref[0][j : j + 1, :]
        value = v_ref[:, j * DV : (j + 1) * DV]
        t = inverses[j]
        new_value = dot(
            jnp.concatenate(halves(t * strength_row), axis=1), jnp.concatenate([value, value], axis=0)
        )
        key_matrix = dot(
            jnp.concatenate(halves(t * (strength_row * jnp.exp(logs_row) * key["inv_row"])), axis=1),
            jnp.concatenate([key["k"], key["k"]], axis=0),
        )
        both = jnp.concatenate([key_matrix, new_value], axis=1)
        last = logs[n - 1 : n, :]
        faded = halves(both * (jnp.exp(last - logs) * key["inv"]))
        state = dot(
            jnp.concatenate([key["k_t"], key["k_t"]], axis=1), jnp.concatenate(faded, axis=0)
        )
        high, low = halves(jnp.exp(last) * identity - state[:, :DK])
        maps_ref[j, :, :DK] = high
        maps_ref[j, :, DK : 2 * DK] = low
        maps_ref[j, :, 2 * DK :] = state[:, DK:].astype(BF16)
        mixed = halves(ratios[j] * key["scores"])
        both_halves = halves(both)
        out = dot(
            jnp.concatenate(mixed, axis=1), jnp.concatenate([both_halves[0], both_halves[0]], axis=0)
        ) + dot(mixed[0], both_halves[1])
        mix_ref[j, :, :DK] = key["q"] * jnp.exp(logs) - out[:, :DK]
        mix_ref[j, :, DK:] = out[:, DK:]


def local_terms(query_input, key_input, value_input, write_strength, decay_rate):
    n = key_input.shape[0]
    groups, per_key = GROUP_VALUE_HEADS // HEADS_STEP, GROUP_VALUE_HEADS // HK
    lower = jnp.tril(jnp.ones((n, n), F32))
    logs = jnp.dot(lower, -decay_rate, precision=lax.Precision.HIGHEST)

    def columns(x):
        return jnp.swapaxes(x.reshape(n, groups, HEADS_STEP), 0, 1)

    def rows(x):
        return x.T.reshape(groups, HEADS_STEP, n)

    wide = HEADS_STEP // per_key * DK
    column_spec = pl.BlockSpec((1, n, HEADS_STEP), lambda i: (i, 0, 0))
    row_spec = pl.BlockSpec((1, HEADS_STEP, n), lambda i: (i, 0, 0))
    out_spec = pl.BlockSpec((HEADS_STEP, DK, 2 * DK + DV), lambda i: (i, 0, 0))
    mix_spec = pl.BlockSpec((HEADS_STEP, n, DK + DV), lambda i: (i, 0, 0))
    return pl.pallas_call(
        local_kernel,
        grid=(groups,),
        in_specs=[
            pl.BlockSpec((n, wide), lambda i: (0, i)),
            pl.BlockSpec((n, wide), lambda i: (0, i)),
            pl.BlockSpec((n, HEADS_STEP * DV), lambda i: (0, i)),
            column_spec,
            row_spec,
            row_spec,
            column_spec,
        ],
        out_specs=[out_spec, mix_spec],
        out_shape=[
            jax.ShapeDtypeStruct((GROUP_VALUE_HEADS, DK, 2 * DK + DV), BF16),
            jax.ShapeDtypeStruct((GROUP_VALUE_HEADS, n, DK + DV), F32),
        ],
        compiler_params=pltpu.CompilerParams(vmem_limit_bytes=40 * MIB),
        name="local_terms",
    )(
        query_input,
        key_input,
        value_input,
        columns(logs),
        rows(logs),
        rows(write_strength),
        columns(write_strength),
    )


def chain_kernel(maps_ref, before_ref, whole_ref):
    row = lax.broadcasted_iota(jnp.int32, (DK, DK + DV), 0)
    column = lax.broadcasted_iota(jnp.int32, (DK, DK + DV), 1)
    passed = (row == column).astype(F32)
    for i in range(maps_ref.shape[0]):
        before_ref[i] = passed
        high, low = halves(passed)
        passed = dot(maps_ref[i, :, : 2 * DK], jnp.concatenate([high, high], axis=0)) + dot(
            maps_ref[i, :, :DK], low
        )
        passed = jnp.concatenate(
            [passed[:, :DK], passed[:, DK:] + maps_ref[i, :, 2 * DK :].astype(F32)], axis=1
        )
    whole_ref[...] = passed


def chain(maps):
    count = maps.shape[0]
    return pl.pallas_call(
        chain_kernel,
        out_shape=[
            jax.ShapeDtypeStruct((count, DK, DK + DV), F32),
            jax.ShapeDtypeStruct((DK, DK + DV), F32),
        ],
        compiler_params=pltpu.CompilerParams(vmem_limit_bytes=40 * MIB),
        name="chain",
    )(maps)


def tie_kernel(*refs):
    pass


def after(array, *others):
    anywhere = pl.BlockSpec(memory_space=pl.ANY)
    return pl.pallas_call(
        tie_kernel,
        in_specs=[anywhere] * (1 + len(others)),
        out_specs=anywhere,
        out_shape=jax.ShapeDtypeStruct(array.shape, array.dtype),
        input_output_aliases={0: 0},
        name="after",
    )(array, *others)


def entering_states(maps, devices):
    heads = maps.shape[0]
    segments = devices // heads
    groups = [[g * heads + h for h in range(heads)] for g in range(segments)]
    by_device = lax.all_to_all(
        maps, AXES, split_axis=0, concat_axis=0, axis_index_groups=groups, tiled=True
    )
    before, whole = chain(by_device)
    if segments == 2:
        start = lax.ppermute(whole[:, DK:], AXES, [(h, heads + h) for h in range(heads)])
    else:
        across = [[g * heads + h for g in range(segments)] for h in range(heads)]
        adds = lax.all_gather(whole[:, DK:], AXES, axis_index_groups=across)
        steps = lax.all_gather(whole[:, :DK], AXES, axis_index_groups=across)
        segment = lax.axis_index(AXES) // heads
        carry = adds[0]
        start = jnp.where(segment == 1, carry, 0.0)
        for g in range(2, segments):
            carry = adds[g - 1] + jnp.dot(steps[g - 1], carry, precision=lax.Precision.HIGHEST)
            start = jnp.where(segment == g, carry, start)
    states = (
        jnp.dot(
            before[:, :, :DK].reshape(heads * DK, DK), start, precision=lax.Precision.HIGH
        ).reshape(heads, DK, DV)
        + before[:, :, DK:]
    ).astype(BF16)
    back = lax.all_to_all(
        states, AXES, split_axis=0, concat_axis=0, axis_index_groups=groups, tiled=True
    )
    return back, states


def finish_kernel(
    parts, place_ref, mix_ref, state_ref, gate_ref, gain_ref, residual_ref, post_ref, *refs
):
    *proj_refs, hidden_ref, first_ref, second_ref, third_ref, core_ref = refs
    for h in range(GROUP_VALUE_HEADS):
        lanes = slice(h * DV, (h + 1) * DV)
        state = state_ref[h]
        recurrent = (
            dot(
                jnp.concatenate(halves(mix_ref[h, :, :DK]), axis=1),
                jnp.concatenate([state, state], axis=0),
            )
            + mix_ref[h, :, DK:]
        )
        inv_rms = lax.rsqrt(jnp.mean(recurrent * recurrent, axis=1, keepdims=True) + 1e-06)
        gate = gate_ref[:, lanes].astype(F32)
        act = gate / (1.0 + jnp.exp(-gate))
        core_ref[:, lanes] = (recurrent * inv_rms * gain_ref[...] * act).astype(BF16)
    core = core_ref[...]
    squares = 0.0
    proj_refs = list(proj_refs)
    for i, count in enumerate(parts):
        refs, proj_refs = proj_refs[:count], proj_refs[count:]
        wide = refs[0].shape[1]
        lanes = pl.ds(pl.multiple_of(place_ref[i] * wide, wide), wide)
        mixed, first = residual_ref[:, lanes].astype(F32), 0
        for ref in refs:
            mixed += dot(core[:, first : first + ref.shape[0]], ref[...])
            first += ref.shape[0]
        hidden = mixed.astype(BF16)
        hidden_ref[:, lanes] = hidden
        widened = hidden.astype(F32)
        squares += jnp.sum(widened * widened, axis=1, keepdims=True)
    inv_rms = lax.rsqrt(squares * (1.0 / D) + 1e-06)
    normed = (hidden_ref[...].astype(F32) * inv_rms * post_ref[...]).astype(BF16)
    start = 0
    for ref, width in zip((first_ref, second_ref, third_ref), GROUPS):
        ref[...] = normed[:, start : start + width]
        start += width


def finish(mix, states, out_gate, head_gain, proj, places, residual_in, post_gain):
    shape = residual_in.shape
    vmem = pl.BlockSpec(memory_space=pltpu.VMEM)
    flat = [part for piece in proj for part in piece]
    return pl.pallas_call(
        functools.partial(finish_kernel, [len(piece) for piece in proj]),
        in_specs=[pl.BlockSpec(memory_space=pltpu.SMEM)] + [vmem] * (6 + len(flat)),
        out_shape=[
            jax.ShapeDtypeStruct((shape[0], wide), BF16) for wide in (D,) + GROUPS
        ],
        scratch_shapes=[pltpu.VMEM(shape, BF16)],
        compiler_params=pltpu.CompilerParams(vmem_limit_bytes=48 * MIB),
        name="finish",
    )(
        places,
        mix,
        states,
        out_gate,
        head_gain.reshape(1, DV),
        residual_in,
        post_gain.reshape(1, D),
        *flat,
    )


def hidden_units_kernel(
    capacity,
    pieces,
    slot_row_ref,
    slot_ref,
    weight_ref,
    own_gate_ref,
    own_up_ref,
    other_gate_ref,
    other_up_ref,
    *refs,
):
    *token_refs, inner_ref, spread_ref, block_ref, taken_ref, sems = refs
    group, expert = pl.program_id(0), pl.program_id(1)
    blocks, rows, _ = block_ref.shape
    served = taken_ref.shape[0]
    joined = max(1, 16 // capacity)

    def copies(step, b):
        found = []
        start = 0
        for part, width in enumerate(GROUPS):
            for ref, (column, places) in zip(token_refs, pieces):
                place = step * blocks + b
                if column == part and place in places:
                    found.append(
                        pltpu.make_async_copy(
                            ref.at[places.index(place)],
                            block_ref.at[b, :, start : start + width],
                            sems.at[b, part],
                        )
                    )
            start += width
        return found

    def load(step):
        @pl.when((expert == 0) & (group == step))
        def _():
            for b in range(blocks):
                for copy in copies(step, b):
                    copy.start()

    for step in range(sum(len(places) for column, places in pieces if column == 0) // blocks):
        load(step)

    @pl.when(expert == 0)
    def _():
        slot_ids = lax.broadcasted_iota(jnp.int32, (capacity, rows), 0).astype(F32)
        for first in range(0, blocks, joined):
            picked = []
            for b in range(first, first + joined):
                chosen = jnp.concatenate(
                    [(slot_row_ref[b, e : e + 1, :] == slot_ids).astype(F32) for e in range(served)],
                    axis=0,
                ).astype(BF16)
                for copy in copies(0, b):
                    copy.wait()
                picked.append(dot(chosen, block_ref[b]))
            for e in range(served):
                part = [p[e * capacity : (e + 1) * capacity] for p in picked]
                taken_ref[e, first * capacity : (first + joined) * capacity] = jnp.concatenate(
                    part, axis=0
                ).astype(BF16)

    def serve(gate_ref, up_ref):
        received = taken_ref[expert]
        gate = dot(received, gate_ref[0])
        up = dot(received, up_ref[0])
        inner_ref[0] = (gate / (1.0 + jnp.exp(-gate)) * up).astype(BF16)

    @pl.when(expert < served // 2)
    def _():
        serve(own_gate_ref, own_up_ref)

    @pl.when(expert >= served // 2)
    def _():
        serve(other_gate_ref, other_up_ref)

    span = served * capacity
    lane = lax.broadcasted_iota(jnp.int32, (rows, 2 * span), 1)
    lane_expert, lane_slot = lane // capacity % served, (lane % capacity).astype(F32)
    share = blocks // served
    for i in range(share):
        b = expert * share + i
        slots, weights = slot_ref[b], weight_ref[b]
        slot = jnp.full((rows, 2 * span), -1.0, F32)
        weight = jnp.zeros((rows, 2 * span), F32)
        for e in range(served):
            slot = jnp.where(lane_expert == e, slots[:, e : e + 1], slot)
            weight = jnp.where(lane_expert == e, weights[:, e : e + 1], weight)
        high = weight.astype(BF16).astype(F32)
        spread_ref[b] = jnp.where(
            slot == lane_slot, jnp.where(lane < span, high, weight - high), 0.0
        ).astype(BF16)


def hidden_units(tokens, weights, own, other, capacity):
    devices, served, rows = weights.shape
    local = own[0].shape[0]
    width = own[0].shape[2]
    pieces = [(column, places) for column, places, _ in tokens]
    named = weights > 0.0
    rank = jnp.einsum(
        "set,tu->seu",
        named.astype(BF16),
        jnp.triu(jnp.ones((rows, rows), BF16)),
        preferred_element_type=F32,
    )
    slots = jnp.where(named, rank - 1.0, -1.0)

    def own_spec(x):
        return pl.BlockSpec((1,) + x.shape[1:], lambda g, e: (jnp.minimum(e, local - 1), 0, 0))

    def other_spec(x):
        return pl.BlockSpec((1,) + x.shape[1:], lambda g, e: (jnp.maximum(e - local, 0), 0, 0))

    column_spec = pl.BlockSpec((BLOCKS_STEP, rows, served), lambda g, e: (g, 0, 0))
    return pl.pallas_call(
        functools.partial(hidden_units_kernel, capacity, pieces),
        grid=(devices // BLOCKS_STEP, served),
        in_specs=[
            pl.BlockSpec((BLOCKS_STEP, served, rows), lambda g, e: (g, 0, 0)),
            column_spec,
            column_spec,
        ]
        + [own_spec(x) for x in own]
        + [other_spec(x) for x in other]
        + [pl.BlockSpec(memory_space=pl.ANY)] * len(tokens),
        out_specs=[
            pl.BlockSpec((1, BLOCKS_STEP * capacity, width), lambda g, e: (e, g, 0)),
            pl.BlockSpec((BLOCKS_STEP, rows, 2 * served * capacity), lambda g, e: (g, 0, 0)),
        ],
        out_shape=[
            jax.ShapeDtypeStruct((served, devices * capacity, width), BF16),
            jax.ShapeDtypeStruct((devices, rows, 2 * served * capacity), BF16),
        ],
        scratch_shapes=[
            pltpu.VMEM((BLOCKS_STEP, rows, D), BF16),
            pltpu.VMEM((served, BLOCKS_STEP * capacity, D), BF16),
            pltpu.SemaphoreType.DMA((BLOCKS_STEP, len(GROUPS))),
        ],
        compiler_params=pltpu.CompilerParams(vmem_limit_bytes=56 * MIB),
        name="hidden_units",
    )(
        slots,
        jnp.swapaxes(slots, 1, 2),
        jnp.swapaxes(weights, 1, 2),
        *own,
        *other,
        *[array for _, _, array in tokens],
    )


def order_places(order):
    count = len(order)
    return [
        sum(((j >> (count - 1 - k)) & 1) << bit for k, bit in enumerate(order))
        for j in range(1 << count)
    ]


def down_kernel(capacity, order, inner_ref, spread_ref, own_ref, other_ref, *refs):
    *_, keep_ref, send_ref, out_ref = refs
    served = inner_ref.shape[0]
    local = served // 2
    for e in range(served):
        down = own_ref[e] if e < local else other_ref[e - local]
        out_ref[e] = dot(inner_ref[e], down)
    places = order_places(order)
    half = len(places) // 2
    for j, place in enumerate(places):
        mine = [out_ref[e, place * capacity : (place + 1) * capacity] for e in range(served)]
        stacked = jnp.concatenate(mine, axis=0).astype(BF16)
        block = dot(spread_ref[place], jnp.concatenate([stacked, stacked], axis=0)).astype(BF16)
        if j < half:
            keep_ref[j] = block
        else:
            send_ref[j - half] = block


def down_strips(inner, spread, own, other, capacity, order, start, width, before):
    served, slots, units = inner.shape
    devices, rows, _ = spread.shape
    first = start // STRIP

    def whole(x):
        return pl.BlockSpec(x.shape, lambda i: (0, 0, 0), pipeline_mode=pl.Buffered(1))

    down_spec = pl.BlockSpec((own.shape[0], units, STRIP), lambda i: (0, 0, first + i))
    half_spec = pl.BlockSpec((devices // 2, rows, STRIP), lambda i: (0, 0, i))
    half_shape = jax.ShapeDtypeStruct((devices // 2, rows, width), BF16)
    return pl.pallas_call(
        functools.partial(down_kernel, capacity, order),
        grid=(width // STRIP,),
        in_specs=[whole(inner), whole(spread), down_spec, down_spec]
        + [pl.BlockSpec(memory_space=pl.ANY)] * len(before),
        out_specs=[half_spec, half_spec],
        out_shape=[half_shape, half_shape],
        scratch_shapes=[pltpu.VMEM((served, slots, STRIP), F32)],
        compiler_params=pltpu.CompilerParams(vmem_limit_bytes=48 * MIB),
        name="down_strips",
    )(inner, spread, own, other, *before)


def sum_by_halving(keep, send, order):
    for bit in order[:-1]:
        total = (keep.astype(F32) + place_flip(send, bit).astype(F32)).astype(BF16)
        half = total.shape[0] // 2
        keep, send = total[:half], total[half:]
    return keep[0].astype(F32) + place_flip(send, order[-1])[0].astype(F32)


def routing(expert_ids, gate_weights, local_experts):
    outer, cores, inner = (lax.axis_size(a) for a in (("outer", "mid"), "core", "inner"))
    rows = expert_ids.shape[0]
    experts = local_experts * outer * cores * inner
    chosen = expert_ids.T[None] == jnp.arange(experts, dtype=jnp.int32)[:, None, None]
    dense = jnp.sum(jnp.where(chosen, gate_weights.T[None], 0.0), axis=1)
    by_chip = jnp.swapaxes(dense.reshape(outer, cores, inner, local_experts * rows), 1, 2)
    by_chip = by_chip.reshape(outer * inner, cores * local_experts, rows)
    weights = lax.all_to_all(by_chip, SAME_CORE, split_axis=0, concat_axis=0, tiled=True)
    turned = jnp.concatenate([weights[:, local_experts:], weights[:, :local_experts]], axis=1)
    weights = jnp.where(lax.axis_index("core") == 1, turned, weights)
    return jnp.take(weights, lax.axis_index(SAME_CORE) ^ jnp.arange(outer * inner), axis=0)


def flipped(array, bit):
    devices = lax.axis_size(AXES)
    return lax.ppermute(array, AXES, [(i, i ^ bit) for i in range(devices)])


def place_flip(array, bit):
    return flipped(array, 1 << (bit if 1 << bit < lax.axis_size("inner") else bit + 1))


def over_rest(array):
    pieces = [array]
    for bit in range(lax.axis_size(REST).bit_length() - 1):
        pieces = pieces + [place_flip(piece, bit) for piece in pieces]
    return pieces


def to_everyone(array, order, joined):
    pieces = [((0,), array[None])]
    for stage, bit in enumerate(order):
        sent = pieces
        if stage in joined or stage > 3:
            sent = [
                (
                    sum((places for places, _ in pieces), ()),
                    jnp.concatenate([piece for _, piece in pieces], axis=0),
                )
            ]
            pieces = sent
        pieces = pieces + [
            (tuple(place ^ (1 << bit) for place in places), place_flip(piece, bit))
            for places, piece in sent
        ]
    return pieces


def shards(
    split_core,
    residual_in,
    query_input,
    key_input,
    value_input,
    out_gate,
    write_strength,
    decay_rate,
    head_gain,
    out_proj,
    post_gain,
    expert_ids,
    gate_weights,
    expert_gate,
    expert_up,
    expert_down,
):
    tok_rows = residual_in.shape[0]
    devices = lax.axis_size(AXES)
    inner_size = lax.axis_size("inner")
    local_experts = expert_gate.shape[0]
    capacity = max(2, tok_rows * TOP * 8 // (5 * local_experts * devices))
    early, late = (
        over_rest(part)[1:] for part in (out_proj[:EARLY_ROWS], out_proj[EARLY_ROWS:])
    )
    weights = routing(expert_ids, gate_weights, local_experts)
    other_gate, other_up, other_down = (
        flipped(x, inner_size) for x in (expert_gate, expert_up, expert_down)
    )
    maps, mix = local_terms(query_input, key_input, value_input, write_strength, decay_rate)
    maps = after(maps, *early)
    states, leaving = entering_states(maps, devices)
    proj = [(out_proj,)] + list(zip(early, late))
    places = lax.axis_index(REST) ^ jnp.arange(len(proj), dtype=jnp.int32)
    if split_core:
        core = lax.axis_index("core")
        late = [after(piece, leaving) for piece in late]
        proj += [(flipped(out_proj, inner_size),)]
        proj += [
            (flipped(first, inner_size), flipped(last, inner_size))
            for first, last in zip(early, late)
        ]
        base = places // inner_size * (2 * inner_size) + places % inner_size
        places = jnp.concatenate([base + core * inner_size, base + (1 - core) * inner_size])
    hidden, *normed = finish(
        mix, states, out_gate, head_gain, proj, places, residual_in, post_gain
    )
    normed, other_gate, other_up, other_down = lax.optimization_barrier(
        (normed, other_gate, other_up, other_down)
    )
    bits = tuple(range(weights.shape[0].bit_length() - 1))
    first, second, third = bits, (bits[1], bits[0]) + bits[:1:-1], bits[2:] + bits[:2]
    tokens = []
    for column, (part, order, joined) in enumerate(
        zip(normed, (first, second, third), ((1,), (1,), (1, 2)))
    ):
        tokens += [
            (column, places, piece) for places, piece in to_everyone(part, order[::-1], joined)
        ]
    inner, spread = hidden_units(
        tokens, weights, (expert_gate, expert_up), (other_gate, other_up), capacity
    )
    sums, start, before = [], 0, ()
    for width, order in ((512, first), (512, second), (512, third), (256, first), (256, second)):
        keep, send = down_strips(
            inner, spread, expert_down, other_down, capacity, order, start, width, before
        )
        before = (keep,)
        sums.append(sum_by_halving(keep, send, order))
        start += width
    return (hidden.astype(F32) + jnp.concatenate(sums, axis=1)).astype(BF16)


def core_stride(devices):
    first = getattr(devices[0], "coords", None)
    for i in range(1, len(devices)):
        if first is not None and tuple(devices[i].coords) == tuple(first):
            return i
    return 1


def solution(mesh):
    devices = mesh.devices.reshape(-1)
    inner = core_stride(devices)
    columns = mesh.shape["exp"]
    if 2 * inner <= columns:
        shape, column_axes = (-1, columns // (2 * inner), 2, inner), AXES[1:]
    else:
        shape, column_axes = (-1, 1, 2, inner), ("inner",)
    split_core = "core" in column_axes
    view = Mesh(devices.reshape(shape), AXES)
    rows = P(AXES, None)
    placed = (
        (rows,) * 7 + (P(), P(None, column_axes), P(), rows, rows) + (P(AXES, None, None),) * 3
    )
    body = functools.partial(shards, split_core)
    return jax.shard_map(body, mesh=view, in_specs=placed, out_specs=rows, check_vma=False)
```

```python
import functools

import jax
import jax.numpy as jnp
from jax import lax
from jax.experimental import pallas as pl
from jax.experimental.pallas import tpu as pltpu
from jax.sharding import Mesh, PartitionSpec as P

D = 2048
HK = 8
GROUP_VALUE_HEADS = 16
DK = 128
DV = 128
TOP = 10
HEADS_STEP = 4
BLOCKS_STEP = 16
GROUPS = (1536, 512)
STRIP = 256
ROW_CUTS = (768, 1280)

F32 = jnp.float32
BF16 = jnp.bfloat16
AXES = ("outer", "mid", "core", "inner")
SAME_CORE = ("outer", "mid", "inner")
REST = ("mid", "inner")
MIB = 1 << 20


def halves(x):
    high = x.astype(BF16)
    return high, (x - high.astype(F32)).astype(BF16)


def dot(a, b):
    return jnp.dot(a, b, preferred_element_type=F32)


def product(left, right):
    n = right[0].shape[1]
    lhs = jnp.concatenate(left, axis=1)
    top = jnp.concatenate(right, axis=1)
    bottom = jnp.concatenate([right[0], jnp.zeros_like(right[0])], axis=1)
    both = dot(lhs, jnp.concatenate([top, bottom], axis=0))
    return both[:, :n] + both[:, n:]


def local_kernel(q_ref, k_ref, v_ref, logs_ref, logs_row_ref, strength_row_ref, strength_ref, maps_ref, mix_ref):
    n = k_ref.shape[0]
    row = lax.broadcasted_iota(jnp.int32, (n, n), 0)
    column = lax.broadcasted_iota(jnp.int32, (n, n), 1)
    inclusive, strict, diagonal = row >= column, row > column, row == column
    heads = maps_ref.shape[0]
    group = GROUP_VALUE_HEADS // HK
    identity = diagonal.astype(F32)

    keys = []
    for i in range(heads // group):
        lanes = slice(i * DK, (i + 1) * DK)
        k_raw, q_raw = k_ref[:, lanes], q_ref[:, lanes]
        k_wide, q_wide = k_raw.astype(F32), q_raw.astype(F32)
        dims = (((1,), (1,)), ((), ()))
        gram = lax.dot_general(k_raw, k_raw, dims, preferred_element_type=F32)
        scores = lax.dot_general(q_raw, k_raw, dims, preferred_element_type=F32)
        inv_k = lax.rsqrt(jnp.sum(k_wide * k_wide, axis=1, keepdims=True) + 1e-06)
        inv_k_row = lax.rsqrt(jnp.sum(jnp.where(diagonal, gram, 0.0), axis=0, keepdims=True) + 1e-06)
        inv_q = lax.rsqrt(jnp.sum(q_wide * q_wide, axis=1, keepdims=True) + 1e-06) * DK ** (-0.5)
        keys.append(
            dict(
                k=k_raw,
                k_t=jnp.transpose(k_wide).astype(BF16),
                q=q_wide * inv_q,
                gram=gram * inv_k * inv_k_row,
                scores=scores * inv_q * inv_k_row,
                inv=inv_k,
                inv_row=inv_k_row,
            )
        )

    ratios, systems, inverses = [], [], []
    for j in range(heads):
        logs, logs_row = logs_ref[0][:, j : j + 1], logs_row_ref[0][j : j + 1, :]
        ratio = jnp.where(inclusive, jnp.exp(jnp.where(inclusive, logs - logs_row, 0.0)), 0.0)
        system = jnp.where(strict, ratio * keys[j // group]["gram"], 0.0) * strength_ref[0][:, j : j + 1]
        first = (row // 2 == column // 2) & strict
        ratios.append(ratio)
        systems.append(halves(system))
        inverses.append(identity - jnp.where(first, system, 0.0))
    size = 2
    while size < n:
        pairs = (row // (2 * size) == column // (2 * size)) & (row // size > column // size)
        inverse_halves = [halves(t) for t in inverses]
        cut = [
            tuple(jnp.where(pairs, part.astype(F32), 0.0).astype(BF16) for part in s) for s in systems
        ]
        left = [product(t, c) for t, c in zip(inverse_halves, cut)]
        inverses = [
            t - product(halves(x), th) for t, x, th in zip(inverses, left, inverse_halves)
        ]
        size *= 2

    for j in range(heads):
        key = keys[j // group]
        logs, logs_row = logs_ref[0][:, j : j + 1], logs_row_ref[0][j : j + 1, :]
        strength_row = strength_row_ref[0][j : j + 1, :]
        value = v_ref[:, j * DV : (j + 1) * DV]
        t = inverses[j]
        new_value = dot(
            jnp.concatenate(halves(t * strength_row), axis=1), jnp.concatenate([value, value], axis=0)
        )
        key_matrix = dot(
            jnp.concatenate(halves(t * (strength_row * jnp.exp(logs_row) * key["inv_row"])), axis=1),
            jnp.concatenate([key["k"], key["k"]], axis=0),
        )
        both = jnp.concatenate([key_matrix, new_value], axis=1)
        last = logs[n - 1 : n, :]
        faded = halves(both * (jnp.exp(last - logs) * key["inv"]))
        state = dot(
            jnp.concatenate([key["k_t"], key["k_t"]], axis=1), jnp.concatenate(faded, axis=0)
        )
        high, low = halves(jnp.exp(last) * identity - state[:, :DK])
        maps_ref[j, :, :DK] = high
        maps_ref[j, :, DK : 2 * DK] = low
        maps_ref[j, :, 2 * DK :] = state[:, DK:].astype(BF16)
        mixed = halves(ratios[j] * key["scores"])
        both_halves = halves(both)
        out = dot(
            jnp.concatenate(mixed, axis=1), jnp.concatenate([both_halves[0], both_halves[0]], axis=0)
        ) + dot(mixed[0], both_halves[1])
        mix_ref[j, :, :DK] = key["q"] * jnp.exp(logs) - out[:, :DK]
        mix_ref[j, :, DK:] = out[:, DK:]


def local_terms(query_input, key_input, value_input, write_strength, decay_rate):
    n = key_input.shape[0]
    groups, per_key = GROUP_VALUE_HEADS // HEADS_STEP, GROUP_VALUE_HEADS // HK
    lower = jnp.tril(jnp.ones((n, n), F32))
    logs = jnp.dot(lower, -decay_rate, precision=lax.Precision.HIGHEST)

    def columns(x):
        return jnp.swapaxes(x.reshape(n, groups, HEADS_STEP), 0, 1)

    def rows(x):
        return x.T.reshape(groups, HEADS_STEP, n)

    wide = HEADS_STEP // per_key * DK
    column_spec = pl.BlockSpec((1, n, HEADS_STEP), lambda i: (i, 0, 0))
    row_spec = pl.BlockSpec((1, HEADS_STEP, n), lambda i: (i, 0, 0))
    out_spec = pl.BlockSpec((HEADS_STEP, DK, 2 * DK + DV), lambda i: (i, 0, 0))
    mix_spec = pl.BlockSpec((HEADS_STEP, n, DK + DV), lambda i: (i, 0, 0))
    return pl.pallas_call(
        local_kernel,
        grid=(groups,),
        in_specs=[
            pl.BlockSpec((n, wide), lambda i: (0, i)),
            pl.BlockSpec((n, wide), lambda i: (0, i)),
            pl.BlockSpec((n, HEADS_STEP * DV), lambda i: (0, i)),
            column_spec,
            row_spec,
            row_spec,
            column_spec,
        ],
        out_specs=[out_spec, mix_spec],
        out_shape=[
            jax.ShapeDtypeStruct((GROUP_VALUE_HEADS, DK, 2 * DK + DV), BF16),
            jax.ShapeDtypeStruct((GROUP_VALUE_HEADS, n, DK + DV), F32),
        ],
        compiler_params=pltpu.CompilerParams(vmem_limit_bytes=40 * MIB),
        name="local_terms",
    )(
        query_input,
        key_input,
        value_input,
        columns(logs),
        rows(logs),
        rows(write_strength),
        columns(write_strength),
    )


def chain_kernel(maps_ref, *refs):
    *_, before_ref, whole_ref = refs
    row = lax.broadcasted_iota(jnp.int32, (DK, DK + DV), 0)
    column = lax.broadcasted_iota(jnp.int32, (DK, DK + DV), 1)
    passed = (row == column).astype(F32)
    for i in range(maps_ref.shape[0]):
        before_ref[i] = passed
        high, low = halves(passed)
        passed = dot(maps_ref[i, :, : 2 * DK], jnp.concatenate([high, high], axis=0)) + dot(
            maps_ref[i, :, :DK], low
        )
        passed = jnp.concatenate(
            [passed[:, :DK], passed[:, DK:] + maps_ref[i, :, 2 * DK :].astype(F32)], axis=1
        )
    whole_ref[...] = passed


def chain(maps, *others):
    count = maps.shape[0]
    return pl.pallas_call(
        chain_kernel,
        in_specs=[pl.BlockSpec(memory_space=pltpu.VMEM)]
        + [pl.BlockSpec(memory_space=pl.ANY)] * len(others),
        out_shape=[
            jax.ShapeDtypeStruct((count, DK, DK + DV), F32),
            jax.ShapeDtypeStruct((DK, DK + DV), F32),
        ],
        compiler_params=pltpu.CompilerParams(vmem_limit_bytes=40 * MIB),
        name="chain",
    )(maps, *others)


def tie_kernel(*refs):
    pass


def after(array, *others):
    anywhere = pl.BlockSpec(memory_space=pl.ANY)
    return pl.pallas_call(
        tie_kernel,
        in_specs=[anywhere] * (1 + len(others)),
        out_specs=anywhere,
        out_shape=jax.ShapeDtypeStruct(array.shape, array.dtype),
        input_output_aliases={0: 0},
        name="after",
    )(array, *others)


def entering_states(maps, devices, others):
    heads = maps.shape[0]
    segments = devices // heads
    groups = [[g * heads + h for h in range(heads)] for g in range(segments)]
    by_device = lax.all_to_all(
        maps, AXES, split_axis=0, concat_axis=0, axis_index_groups=groups, tiled=True
    )
    before, whole = chain(by_device, *others)
    if segments == 2:
        start = lax.ppermute(whole[:, DK:], AXES, [(h, heads + h) for h in range(heads)])
    else:
        across = [[g * heads + h for g in range(segments)] for h in range(heads)]
        adds = lax.all_gather(whole[:, DK:], AXES, axis_index_groups=across)
        steps = lax.all_gather(whole[:, :DK], AXES, axis_index_groups=across)
        segment = lax.axis_index(AXES) // heads
        carry = adds[0]
        start = jnp.where(segment == 1, carry, 0.0)
        for g in range(2, segments):
            carry = adds[g - 1] + jnp.dot(steps[g - 1], carry, precision=lax.Precision.HIGHEST)
            start = jnp.where(segment == g, carry, start)
    states = (
        jnp.dot(
            before[:, :, :DK].reshape(heads * DK, DK), start, precision=lax.Precision.HIGH
        ).reshape(heads, DK, DV)
        + before[:, :, DK:]
    ).astype(BF16)
    back = lax.all_to_all(
        states, AXES, split_axis=0, concat_axis=0, axis_index_groups=groups, tiled=True
    )
    return back, whole


def finish_kernel(
    parts, place_ref, mix_ref, state_ref, gate_ref, gain_ref, residual_ref, post_ref, *refs
):
    *proj_refs, hidden_ref, first_ref, second_ref, core_ref = refs
    for h in range(GROUP_VALUE_HEADS):
        lanes = slice(h * DV, (h + 1) * DV)
        state = state_ref[h]
        recurrent = (
            dot(
                jnp.concatenate(halves(mix_ref[h, :, :DK]), axis=1),
                jnp.concatenate([state, state], axis=0),
            )
            + mix_ref[h, :, DK:]
        )
        inv_rms = lax.rsqrt(jnp.mean(recurrent * recurrent, axis=1, keepdims=True) + 1e-06)
        gate = gate_ref[:, lanes].astype(F32)
        act = gate / (1.0 + jnp.exp(-gate))
        core_ref[:, lanes] = (recurrent * inv_rms * gain_ref[...] * act).astype(BF16)
    core = core_ref[...]
    squares = 0.0
    proj_refs = list(proj_refs)
    for i, count in enumerate(parts):
        refs, proj_refs = proj_refs[:count], proj_refs[count:]
        wide = refs[0].shape[1]
        lanes = pl.ds(pl.multiple_of(place_ref[i] * wide, wide), wide)
        mixed, first = residual_ref[:, lanes].astype(F32), 0
        for ref in refs:
            mixed += dot(core[:, first : first + ref.shape[0]], ref[...])
            first += ref.shape[0]
        hidden = mixed.astype(BF16)
        hidden_ref[:, lanes] = hidden
        widened = hidden.astype(F32)
        squares += jnp.sum(widened * widened, axis=1, keepdims=True)
    inv_rms = lax.rsqrt(squares * (1.0 / D) + 1e-06)
    normed = (hidden_ref[...].astype(F32) * inv_rms * post_ref[...]).astype(BF16)
    start = 0
    for ref, width in zip((first_ref, second_ref), GROUPS):
        ref[...] = normed[:, start : start + width]
        start += width


def finish(mix, states, out_gate, head_gain, proj, places, residual_in, post_gain):
    shape = residual_in.shape
    vmem = pl.BlockSpec(memory_space=pltpu.VMEM)
    flat = [part for piece in proj for part in piece]
    return pl.pallas_call(
        functools.partial(finish_kernel, [len(piece) for piece in proj]),
        in_specs=[pl.BlockSpec(memory_space=pltpu.SMEM)] + [vmem] * (6 + len(flat)),
        out_shape=[
            jax.ShapeDtypeStruct((shape[0], wide), BF16) for wide in (D,) + GROUPS
        ],
        scratch_shapes=[pltpu.VMEM(shape, BF16)],
        compiler_params=pltpu.CompilerParams(vmem_limit_bytes=48 * MIB),
        name="finish",
    )(
        places,
        mix,
        states,
        out_gate,
        head_gain.reshape(1, DV),
        residual_in,
        post_gain.reshape(1, D),
        *flat,
    )


def hidden_units_kernel(
    capacity,
    pieces,
    slot_row_ref,
    slot_ref,
    weight_ref,
    own_gate_ref,
    own_up_ref,
    other_gate_ref,
    other_up_ref,
    *refs,
):
    *token_refs, inner_ref, spread_ref, block_ref, taken_ref, sems = refs
    group, expert = pl.program_id(0), pl.program_id(1)
    blocks, rows, _ = block_ref.shape
    served = taken_ref.shape[0]
    joined = max(1, 16 // capacity)

    def copies(step, b):
        found = []
        start = 0
        for part, width in enumerate(GROUPS):
            for ref, (column, places) in zip(token_refs, pieces):
                place = step * blocks + b
                if column == part and place in places:
                    found.append(
                        pltpu.make_async_copy(
                            ref.at[places.index(place)],
                            block_ref.at[b, :, start : start + width],
                            sems.at[b, part],
                        )
                    )
            start += width
        return found

    def load(step):
        @pl.when((expert == 0) & (group == step))
        def _():
            for b in range(blocks):
                for copy in copies(step, b):
                    copy.start()

    for step in range(sum(len(places) for column, places in pieces if column == 0) // blocks):
        load(step)

    @pl.when(expert == 0)
    def _():
        slot_ids = lax.broadcasted_iota(jnp.int32, (capacity, rows), 0).astype(F32)
        for first in range(0, blocks, joined):
            picked = []
            for b in range(first, first + joined):
                chosen = jnp.concatenate(
                    [(slot_row_ref[b, e : e + 1, :] == slot_ids).astype(F32) for e in range(served)],
                    axis=0,
                ).astype(BF16)
                for copy in copies(0, b):
                    copy.wait()
                picked.append(dot(chosen, block_ref[b]))
            for e in range(served):
                part = [p[e * capacity : (e + 1) * capacity] for p in picked]
                taken_ref[e, first * capacity : (first + joined) * capacity] = jnp.concatenate(
                    part, axis=0
                ).astype(BF16)

    def serve(gate_ref, up_ref):
        received = taken_ref[expert]
        gate = dot(received, gate_ref[0])
        up = dot(received, up_ref[0])
        inner_ref[0] = (gate / (1.0 + jnp.exp(-gate)) * up).astype(BF16)

    @pl.when(expert < served // 2)
    def _():
        serve(own_gate_ref, own_up_ref)

    @pl.when(expert >= served // 2)
    def _():
        serve(other_gate_ref, other_up_ref)

    span = served * capacity
    lane = lax.broadcasted_iota(jnp.int32, (rows, 2 * span), 1)
    lane_expert, lane_slot = lane // capacity % served, (lane % capacity).astype(F32)
    share = blocks // served
    for i in range(share):
        b = expert * share + i
        slots, weights = slot_ref[b], weight_ref[b]
        slot = jnp.full((rows, 2 * span), -1.0, F32)
        weight = jnp.zeros((rows, 2 * span), F32)
        for e in range(served):
            slot = jnp.where(lane_expert == e, slots[:, e : e + 1], slot)
            weight = jnp.where(lane_expert == e, weights[:, e : e + 1], weight)
        high = weight.astype(BF16).astype(F32)
        spread_ref[b] = jnp.where(
            slot == lane_slot, jnp.where(lane < span, high, weight - high), 0.0
        ).astype(BF16)


def hidden_units(tokens, slots, own, other, capacity):
    devices, served, rows = slots[0].shape
    local = own[0].shape[0]
    width = own[0].shape[2]
    pieces = [(column, places) for column, places, _ in tokens]
    def own_spec(x):
        return pl.BlockSpec((1,) + x.shape[1:], lambda g, e: (jnp.minimum(e, local - 1), 0, 0))

    def other_spec(x):
        return pl.BlockSpec((1,) + x.shape[1:], lambda g, e: (jnp.maximum(e - local, 0), 0, 0))

    column_spec = pl.BlockSpec((BLOCKS_STEP, rows, served), lambda g, e: (g, 0, 0))
    return pl.pallas_call(
        functools.partial(hidden_units_kernel, capacity, pieces),
        grid=(devices // BLOCKS_STEP, served),
        in_specs=[
            pl.BlockSpec((BLOCKS_STEP, served, rows), lambda g, e: (g, 0, 0)),
            column_spec,
            column_spec,
        ]
        + [own_spec(x) for x in own]
        + [other_spec(x) for x in other]
        + [pl.BlockSpec(memory_space=pl.ANY)] * len(tokens),
        out_specs=[
            pl.BlockSpec((1, BLOCKS_STEP * capacity, width), lambda g, e: (e, g, 0)),
            pl.BlockSpec((BLOCKS_STEP, rows, 2 * served * capacity), lambda g, e: (g, 0, 0)),
        ],
        out_shape=[
            jax.ShapeDtypeStruct((served, devices * capacity, width), BF16),
            jax.ShapeDtypeStruct((devices, rows, 2 * served * capacity), BF16),
        ],
        scratch_shapes=[
            pltpu.VMEM((BLOCKS_STEP, rows, D), BF16),
            pltpu.VMEM((served, BLOCKS_STEP * capacity, D), BF16),
            pltpu.SemaphoreType.DMA((BLOCKS_STEP, len(GROUPS))),
        ],
        compiler_params=pltpu.CompilerParams(vmem_limit_bytes=56 * MIB),
        name="hidden_units",
    )(
        *slots,
        *own,
        *other,
        *[array for _, _, array in tokens],
    )


def order_places(order):
    count = len(order)
    return [
        sum(((j >> (count - 1 - k)) & 1) << bit for k, bit in enumerate(order))
        for j in range(1 << count)
    ]


def down_kernel(capacity, order, inner_ref, spread_ref, own_ref, other_ref, keep_ref, send_ref, out_ref):
    served = inner_ref.shape[0]
    local = served // 2
    for e in range(served):
        down = own_ref[e] if e < local else other_ref[e - local]
        out_ref[e] = dot(inner_ref[e], down)
    places = order_places(order)
    half = len(places) // 2
    for j, place in enumerate(places):
        mine = [out_ref[e, place * capacity : (place + 1) * capacity] for e in range(served)]
        stacked = jnp.concatenate(mine, axis=0).astype(BF16)
        block = dot(spread_ref[place], jnp.concatenate([stacked, stacked], axis=0)).astype(BF16)
        if j < half:
            keep_ref[j] = block
        else:
            send_ref[j - half] = block


def down_strips(inner, spread, own, other, capacity, order, start, width):
    served, slots, units = inner.shape
    devices, rows, _ = spread.shape
    first = start // STRIP

    def whole(x):
        return pl.BlockSpec(x.shape, lambda i: (0, 0, 0), pipeline_mode=pl.Buffered(1))

    down_spec = pl.BlockSpec((own.shape[0], units, STRIP), lambda i: (0, 0, first + i))
    half_spec = pl.BlockSpec((devices // 2, rows, STRIP), lambda i: (0, 0, i))
    half_shape = jax.ShapeDtypeStruct((devices // 2, rows, width), BF16)
    return pl.pallas_call(
        functools.partial(down_kernel, capacity, order),
        grid=(width // STRIP,),
        in_specs=[whole(inner), whole(spread), down_spec, down_spec],
        out_specs=[half_spec, half_spec],
        out_shape=[half_shape, half_shape],
        scratch_shapes=[pltpu.VMEM((served, slots, STRIP), F32)],
        compiler_params=pltpu.CompilerParams(vmem_limit_bytes=48 * MIB),
        name="down_strips",
    )(inner, spread, own, other)


def sum_by_halving(keep, send, stages):
    for stage in stages[:-1]:
        total = (keep.astype(F32) + stage_flip(send, stage).astype(F32)).astype(BF16)
        half = total.shape[0] // 2
        keep, send = total[:half], total[half:]
    return keep[0].astype(F32) + stage_flip(send, stages[-1])[0].astype(F32)


def routing(expert_ids, gate_weights, local_experts):
    outer, cores, inner = (lax.axis_size(a) for a in (("outer", "mid"), "core", "inner"))
    rows = expert_ids.shape[0]
    experts = local_experts * outer * cores * inner
    chosen = expert_ids.T[None] == jnp.arange(experts, dtype=jnp.int32)[:, None, None]
    dense = jnp.sum(jnp.where(chosen, gate_weights.T[None], 0.0), axis=1)
    by_chip = jnp.swapaxes(dense.reshape(outer, cores, inner, local_experts * rows), 1, 2)
    by_chip = by_chip.reshape(outer * inner, cores * local_experts, rows)
    weights = lax.all_to_all(by_chip, SAME_CORE, split_axis=0, concat_axis=0, tiled=True)
    turned = jnp.concatenate([weights[:, local_experts:], weights[:, :local_experts]], axis=1)
    weights = jnp.where(lax.axis_index("core") == 1, turned, weights)
    bits = (outer * inner).bit_length() - 1
    table = jnp.asarray([order_places(order[::-1]) for order in core_orders(bits)], jnp.int32)
    source = lax.axis_index(SAME_CORE) ^ table[lax.axis_index("core")]
    weights = jnp.take(weights, source, axis=0, mode="clip")
    named = weights > 0.0
    rank = jnp.einsum(
        "set,tu->seu",
        named.astype(BF16),
        jnp.triu(jnp.ones((rows, rows), BF16)),
        preferred_element_type=F32,
    )
    slots = jnp.where(named, rank - 1.0, -1.0)
    return slots, jnp.swapaxes(slots, 1, 2), jnp.swapaxes(weights, 1, 2)


def core_orders(bits):
    first = tuple(range(bits))[::-1]
    second = tuple(first[n ^ 1] if n ^ 1 < bits else first[n] for n in range(bits))
    return first, second


def flipped(array, bit):
    devices = lax.axis_size(AXES)
    return lax.ppermute(array, AXES, [(i, i ^ bit) for i in range(devices)])


def place_flip(array, bit):
    return flipped(array, 1 << (bit if 1 << bit < lax.axis_size("inner") else bit + 1))


def over_rest(array):
    pieces = [array]
    for bit in range(lax.axis_size(REST).bit_length() - 1):
        pieces = pieces + [place_flip(piece, bit) for piece in pieces]
    return pieces


def stage_flip(array, stage):
    inner, devices = lax.axis_size("inner"), lax.axis_size(AXES)
    bits = lax.axis_size(SAME_CORE).bit_length() - 1

    def partner(i):
        bit = core_orders(bits)[i // inner % 2][stage]
        return i ^ (1 << (bit if 1 << bit < inner else bit + 1))

    return lax.ppermute(array, AXES, [(i, partner(i)) for i in range(devices)])


def to_everyone(array, stages, joined):
    pieces = [((0,), array[None])]
    for step, stage in enumerate(stages):
        if step in joined or step > 3:
            pieces = [
                (
                    sum((places for places, _ in pieces), ()),
                    jnp.concatenate([piece for _, piece in pieces], axis=0),
                )
            ]
        pieces = pieces + [
            (tuple(place | (1 << stage) for place in places), stage_flip(piece, stage))
            for places, piece in pieces
        ]
    return pieces


def shards(
    split_core,
    residual_in,
    query_input,
    key_input,
    value_input,
    out_gate,
    write_strength,
    decay_rate,
    head_gain,
    out_proj,
    post_gain,
    expert_ids,
    gate_weights,
    expert_gate,
    expert_up,
    expert_down,
):
    tok_rows = residual_in.shape[0]
    devices = lax.axis_size(AXES)
    inner_size = lax.axis_size("inner")
    local_experts = expert_gate.shape[0]
    capacity = max(2, tok_rows * TOP * 8 // (5 * local_experts * devices))
    first_cut, last_cut = ROW_CUTS
    early, middle = (
        over_rest(part)[1:] for part in (out_proj[:first_cut], out_proj[first_cut:last_cut])
    )
    slots = routing(expert_ids, gate_weights, local_experts)
    other_gate, other_up, other_down = (
        flipped(x, inner_size) for x in (expert_gate, expert_up, expert_down)
    )
    maps, mix = local_terms(query_input, key_input, value_input, write_strength, decay_rate)
    maps = after(maps, *early)
    others = (other_gate, other_up, other_down, *middle, *slots)
    if split_core:
        core_early = [flipped(first, inner_size) for first in [out_proj] + early]
        others += tuple(core_early)
    states, whole = entering_states(maps, devices, others)
    late = over_rest(after(out_proj[last_cut:], whole))[1:]
    proj = [(out_proj,)] + list(zip(early, middle, late))
    places = lax.axis_index(REST) ^ jnp.arange(len(proj), dtype=jnp.int32)
    if split_core:
        core = lax.axis_index("core")
        core_middle = [flipped(piece, inner_size) for piece in middle]
        core_late = [flipped(after(piece, states), inner_size) for piece in late]
        proj += [(core_early[0],)] + list(zip(core_early[1:], core_middle, core_late))
        base = places // inner_size * (2 * inner_size) + places % inner_size
        places = jnp.concatenate([base + core * inner_size, base + (1 - core) * inner_size])
    hidden, *normed = finish(
        mix, states, out_gate, head_gain, proj, places, residual_in, post_gain
    )
    bits = slots[0].shape[0].bit_length() - 1
    plain, turned = tuple(range(bits)), tuple((n + bits - 2) % bits for n in range(bits))
    tokens = []
    for column, (part, stages, joined) in enumerate(
        zip(normed, (plain, turned), ((1,), (1, 2)))
    ):
        tokens += [(column, places, piece) for places, piece in to_everyone(part, stages, joined)]
    inner, spread = hidden_units(
        tokens, slots, (expert_gate, expert_up), (other_gate, other_up), capacity
    )
    sums, start = [], 0
    for width, stages in ((512, plain), (512, turned), (1024, plain)):
        keep, send = down_strips(
            inner, spread, expert_down, other_down, capacity, stages[::-1], start, width
        )
        sums.append(sum_by_halving(keep, send, stages[::-1]))
        start += width
    return (hidden.astype(F32) + jnp.concatenate(sums, axis=1)).astype(BF16)


def core_stride(devices):
    first = getattr(devices[0], "coords", None)
    for i in range(1, len(devices)):
        if first is not None and tuple(devices[i].coords) == tuple(first):
            return i
    return 1


def solution(mesh):
    devices = mesh.devices.reshape(-1)
    inner = core_stride(devices)
    columns = mesh.shape["exp"]
    if 2 * inner <= columns:
        shape, column_axes = (-1, columns // (2 * inner), 2, inner), AXES[1:]
    else:
        shape, column_axes = (-1, 1, 2, inner), ("inner",)
    split_core = "core" in column_axes
    view = Mesh(devices.reshape(shape), AXES)
    rows = P(AXES, None)
    placed = (
        (rows,) * 7 + (P(), P(None, column_axes), P(), rows, rows) + (P(AXES, None, None),) * 3
    )
    body = functools.partial(shards, split_core)
    return jax.shard_map(body, mesh=view, in_specs=placed, out_specs=rows, check_vma=False)
```

```python
import functools

import jax
import jax.numpy as jnp
from jax import lax
from jax.experimental import pallas as pl
from jax.experimental.pallas import tpu as pltpu
from jax.sharding import Mesh, PartitionSpec as P

D = 2048
HK = 8
GROUP_VALUE_HEADS = 16
DK = 128
DV = 128
TOP = 10
HEADS_STEP = 4
BLOCKS_STEP = 16
GROUPS = (1664, 384)
STRIP = 256
EARLY_ROWS = 1024

F32 = jnp.float32
BF16 = jnp.bfloat16
AXES = ("outer", "mid", "core", "inner")
SAME_CORE = ("outer", "mid", "inner")
REST = ("mid", "inner")
MIB = 1 << 20


def halves(x):
    high = x.astype(BF16)
    return high, (x - high.astype(F32)).astype(BF16)


def dot(a, b):
    return jnp.dot(a, b, preferred_element_type=F32)


def product(left, right):
    n = right[0].shape[1]
    lhs = jnp.concatenate(left, axis=1)
    top = jnp.concatenate(right, axis=1)
    bottom = jnp.concatenate([right[0], jnp.zeros_like(right[0])], axis=1)
    both = dot(lhs, jnp.concatenate([top, bottom], axis=0))
    return both[:, :n] + both[:, n:]


def local_kernel(q_ref, k_ref, v_ref, logs_ref, logs_row_ref, strength_row_ref, strength_ref, maps_ref, mix_ref):
    n = k_ref.shape[0]
    row = lax.broadcasted_iota(jnp.int32, (n, n), 0)
    column = lax.broadcasted_iota(jnp.int32, (n, n), 1)
    inclusive, strict, diagonal = row >= column, row > column, row == column
    heads = maps_ref.shape[0]
    group = GROUP_VALUE_HEADS // HK
    identity = diagonal.astype(F32)

    keys = []
    for i in range(heads // group):
        lanes = slice(i * DK, (i + 1) * DK)
        k_raw, q_raw = k_ref[:, lanes], q_ref[:, lanes]
        k_wide, q_wide = k_raw.astype(F32), q_raw.astype(F32)
        dims = (((1,), (1,)), ((), ()))
        gram = lax.dot_general(k_raw, k_raw, dims, preferred_element_type=F32)
        scores = lax.dot_general(q_raw, k_raw, dims, preferred_element_type=F32)
        inv_k = lax.rsqrt(jnp.sum(k_wide * k_wide, axis=1, keepdims=True) + 1e-06)
        inv_k_row = lax.rsqrt(jnp.sum(jnp.where(diagonal, gram, 0.0), axis=0, keepdims=True) + 1e-06)
        inv_q = lax.rsqrt(jnp.sum(q_wide * q_wide, axis=1, keepdims=True) + 1e-06) * DK ** (-0.5)
        keys.append(
            dict(
                k=k_raw,
                k_t=jnp.transpose(k_wide).astype(BF16),
                q=q_wide * inv_q,
                gram=gram * inv_k * inv_k_row,
                scores=scores * inv_q * inv_k_row,
                inv=inv_k,
                inv_row=inv_k_row,
            )
        )

    ratios, systems, inverses = [], [], []
    for j in range(heads):
        logs, logs_row = logs_ref[0][:, j : j + 1], logs_row_ref[0][j : j + 1, :]
        ratio = jnp.where(inclusive, jnp.exp(jnp.where(inclusive, logs - logs_row, 0.0)), 0.0)
        system = jnp.where(strict, ratio * keys[j // group]["gram"], 0.0) * strength_ref[0][:, j : j + 1]
        first = (row // 2 == column // 2) & strict
        ratios.append(ratio)
        systems.append(halves(system))
        inverses.append(identity - jnp.where(first, system, 0.0))
    size = 2
    while size < n:
        pairs = (row // (2 * size) == column // (2 * size)) & (row // size > column // size)
        inverse_halves = [halves(t) for t in inverses]
        cut = [
            tuple(jnp.where(pairs, part.astype(F32), 0.0).astype(BF16) for part in s) for s in systems
        ]
        left = [product(t, c) for t, c in zip(inverse_halves, cut)]
        inverses = [
            t - product(halves(x), th) for t, x, th in zip(inverses, left, inverse_halves)
        ]
        size *= 2

    for j in range(heads):
        key = keys[j // group]
        logs, logs_row = logs_ref[0][:, j : j + 1], logs_row_ref[0][j : j + 1, :]
        strength_row = strength_row_ref[0][j : j + 1, :]
        value = v_ref[:, j * DV : (j + 1) * DV]
        t = inverses[j]
        new_value = dot(
            jnp.concatenate(halves(t * strength_row), axis=1), jnp.concatenate([value, value], axis=0)
        )
        key_matrix = dot(
            jnp.concatenate(halves(t * (strength_row * jnp.exp(logs_row) * key["inv_row"])), axis=1),
            jnp.concatenate([key["k"], key["k"]], axis=0),
        )
        both = jnp.concatenate([key_matrix, new_value], axis=1)
        last = logs[n - 1 : n, :]
        faded = halves(both * (jnp.exp(last - logs) * key["inv"]))
        state = dot(
            jnp.concatenate([key["k_t"], key["k_t"]], axis=1), jnp.concatenate(faded, axis=0)
        )
        high, low = halves(jnp.exp(last) * identity - state[:, :DK])
        maps_ref[j, :, :DK] = high
        maps_ref[j, :, DK : 2 * DK] = low
        maps_ref[j, :, 2 * DK :] = state[:, DK:].astype(BF16)
        mixed = halves(ratios[j] * key["scores"])
        both_halves = halves(both)
        out = dot(
            jnp.concatenate(mixed, axis=1), jnp.concatenate([both_halves[0], both_halves[0]], axis=0)
        ) + dot(mixed[0], both_halves[1])
        mix_ref[j, :, :DK] = key["q"] * jnp.exp(logs) - out[:, :DK]
        mix_ref[j, :, DK:] = out[:, DK:]


def local_terms(query_input, key_input, value_input, write_strength, decay_rate):
    n = key_input.shape[0]
    groups, per_key = GROUP_VALUE_HEADS // HEADS_STEP, GROUP_VALUE_HEADS // HK
    lower = jnp.tril(jnp.ones((n, n), F32))
    logs = jnp.dot(lower, -decay_rate, precision=lax.Precision.HIGHEST)

    def columns(x):
        return jnp.swapaxes(x.reshape(n, groups, HEADS_STEP), 0, 1)

    def rows(x):
        return x.T.reshape(groups, HEADS_STEP, n)

    wide = HEADS_STEP // per_key * DK
    column_spec = pl.BlockSpec((1, n, HEADS_STEP), lambda i: (i, 0, 0))
    row_spec = pl.BlockSpec((1, HEADS_STEP, n), lambda i: (i, 0, 0))
    out_spec = pl.BlockSpec((HEADS_STEP, DK, 2 * DK + DV), lambda i: (i, 0, 0))
    mix_spec = pl.BlockSpec((HEADS_STEP, n, DK + DV), lambda i: (i, 0, 0))
    return pl.pallas_call(
        local_kernel,
        grid=(groups,),
        in_specs=[
            pl.BlockSpec((n, wide), lambda i: (0, i)),
            pl.BlockSpec((n, wide), lambda i: (0, i)),
            pl.BlockSpec((n, HEADS_STEP * DV), lambda i: (0, i)),
            column_spec,
            row_spec,
            row_spec,
            column_spec,
        ],
        out_specs=[out_spec, mix_spec],
        out_shape=[
            jax.ShapeDtypeStruct((GROUP_VALUE_HEADS, DK, 2 * DK + DV), BF16),
            jax.ShapeDtypeStruct((GROUP_VALUE_HEADS, n, DK + DV), F32),
        ],
        compiler_params=pltpu.CompilerParams(vmem_limit_bytes=40 * MIB),
        name="local_terms",
    )(
        query_input,
        key_input,
        value_input,
        columns(logs),
        rows(logs),
        rows(write_strength),
        columns(write_strength),
    )


def chain_kernel(maps_ref, *refs):
    *_, before_ref, whole_ref = refs
    row = lax.broadcasted_iota(jnp.int32, (DK, DK + DV), 0)
    column = lax.broadcasted_iota(jnp.int32, (DK, DK + DV), 1)
    passed = (row == column).astype(F32)
    for i in range(maps_ref.shape[0]):
        before_ref[i] = passed
        high, low = halves(passed)
        passed = dot(maps_ref[i, :, : 2 * DK], jnp.concatenate([high, high], axis=0)) + dot(
            maps_ref[i, :, :DK], low
        )
        passed = jnp.concatenate(
            [passed[:, :DK], passed[:, DK:] + maps_ref[i, :, 2 * DK :].astype(F32)], axis=1
        )
    whole_ref[...] = passed


def chain(maps, *others):
    count = maps.shape[0]
    return pl.pallas_call(
        chain_kernel,
        in_specs=[pl.BlockSpec(memory_space=pltpu.VMEM)]
        + [pl.BlockSpec(memory_space=pl.ANY)] * len(others),
        out_shape=[
            jax.ShapeDtypeStruct((count, DK, DK + DV), F32),
            jax.ShapeDtypeStruct((DK, DK + DV), F32),
        ],
        compiler_params=pltpu.CompilerParams(vmem_limit_bytes=40 * MIB),
        name="chain",
    )(maps, *others)


def tie_kernel(*refs):
    pass


def after(array, *others):
    anywhere = pl.BlockSpec(memory_space=pl.ANY)
    return pl.pallas_call(
        tie_kernel,
        in_specs=[anywhere] * (1 + len(others)),
        out_specs=anywhere,
        out_shape=jax.ShapeDtypeStruct(array.shape, array.dtype),
        input_output_aliases={0: 0},
        name="after",
    )(array, *others)


def entering_states(maps, devices, others):
    heads = maps.shape[0]
    segments = devices // heads
    groups = [[g * heads + h for h in range(heads)] for g in range(segments)]
    by_device = lax.all_to_all(
        maps, AXES, split_axis=0, concat_axis=0, axis_index_groups=groups, tiled=True
    )
    before, whole = chain(by_device, *others)
    if segments == 2:
        start = lax.ppermute(whole[:, DK:], AXES, [(h, heads + h) for h in range(heads)])
    else:
        across = [[g * heads + h for g in range(segments)] for h in range(heads)]
        adds = lax.all_gather(whole[:, DK:], AXES, axis_index_groups=across)
        steps = lax.all_gather(whole[:, :DK], AXES, axis_index_groups=across)
        segment = lax.axis_index(AXES) // heads
        carry = adds[0]
        start = jnp.where(segment == 1, carry, 0.0)
        for g in range(2, segments):
            carry = adds[g - 1] + jnp.dot(steps[g - 1], carry, precision=lax.Precision.HIGHEST)
            start = jnp.where(segment == g, carry, start)
    states = (
        jnp.dot(
            before[:, :, :DK].reshape(heads * DK, DK), start, precision=lax.Precision.HIGH
        ).reshape(heads, DK, DV)
        + before[:, :, DK:]
    ).astype(BF16)
    back = lax.all_to_all(
        states, AXES, split_axis=0, concat_axis=0, axis_index_groups=groups, tiled=True
    )
    return back, whole


def finish_kernel(
    parts, place_ref, mix_ref, state_ref, gate_ref, gain_ref, residual_ref, post_ref, *refs
):
    *proj_refs, hidden_ref, first_ref, second_ref, core_ref = refs
    for h in range(GROUP_VALUE_HEADS):
        lanes = slice(h * DV, (h + 1) * DV)
        state = state_ref[h]
        recurrent = (
            dot(
                jnp.concatenate(halves(mix_ref[h, :, :DK]), axis=1),
                jnp.concatenate([state, state], axis=0),
            )
            + mix_ref[h, :, DK:]
        )
        inv_rms = lax.rsqrt(jnp.mean(recurrent * recurrent, axis=1, keepdims=True) + 1e-06)
        gate = gate_ref[:, lanes].astype(F32)
        act = gate / (1.0 + jnp.exp(-gate))
        core_ref[:, lanes] = (recurrent * inv_rms * gain_ref[...] * act).astype(BF16)
    core = core_ref[...]
    squares = 0.0
    proj_refs = list(proj_refs)
    for i, count in enumerate(parts):
        refs, proj_refs = proj_refs[:count], proj_refs[count:]
        wide = refs[0].shape[1]
        lanes = pl.ds(pl.multiple_of(place_ref[i] * wide, wide), wide)
        mixed, first = residual_ref[:, lanes].astype(F32), 0
        for ref in refs:
            mixed += dot(core[:, first : first + ref.shape[0]], ref[...])
            first += ref.shape[0]
        hidden = mixed.astype(BF16)
        hidden_ref[:, lanes] = hidden
        widened = hidden.astype(F32)
        squares += jnp.sum(widened * widened, axis=1, keepdims=True)
    inv_rms = lax.rsqrt(squares * (1.0 / D) + 1e-06)
    normed = (hidden_ref[...].astype(F32) * inv_rms * post_ref[...]).astype(BF16)
    start = 0
    for ref, width in zip((first_ref, second_ref), GROUPS):
        ref[...] = normed[:, start : start + width]
        start += width


def finish(mix, states, out_gate, head_gain, proj, places, residual_in, post_gain):
    shape = residual_in.shape
    vmem = pl.BlockSpec(memory_space=pltpu.VMEM)
    flat = [part for piece in proj for part in piece]
    return pl.pallas_call(
        functools.partial(finish_kernel, [len(piece) for piece in proj]),
        in_specs=[pl.BlockSpec(memory_space=pltpu.SMEM)] + [vmem] * (6 + len(flat)),
        out_shape=[
            jax.ShapeDtypeStruct((shape[0], wide), BF16) for wide in (D,) + GROUPS
        ],
        scratch_shapes=[pltpu.VMEM(shape, BF16)],
        compiler_params=pltpu.CompilerParams(vmem_limit_bytes=48 * MIB),
        name="finish",
    )(
        places,
        mix,
        states,
        out_gate,
        head_gain.reshape(1, DV),
        residual_in,
        post_gain.reshape(1, D),
        *flat,
    )


def hidden_units_kernel(
    capacity,
    pieces,
    slot_row_ref,
    slot_ref,
    weight_ref,
    own_gate_ref,
    own_up_ref,
    other_gate_ref,
    other_up_ref,
    *refs,
):
    *token_refs, inner_ref, spread_ref, block_ref, taken_ref, sems = refs
    group, expert = pl.program_id(0), pl.program_id(1)
    blocks, rows, _ = block_ref.shape
    served = taken_ref.shape[0]
    joined = max(1, 16 // capacity)

    def copies(step, b):
        found = []
        start = 0
        for part, width in enumerate(GROUPS):
            for ref, (column, places) in zip(token_refs, pieces):
                place = step * blocks + b
                if column == part and place in places:
                    found.append(
                        pltpu.make_async_copy(
                            ref.at[places.index(place)],
                            block_ref.at[b, :, start : start + width],
                            sems.at[b, part],
                        )
                    )
            start += width
        return found

    def load(step):
        @pl.when((expert == 0) & (group == step))
        def _():
            for b in range(blocks):
                for copy in copies(step, b):
                    copy.start()

    for step in range(sum(len(places) for column, places in pieces if column == 0) // blocks):
        load(step)

    @pl.when(expert == 0)
    def _():
        slot_ids = lax.broadcasted_iota(jnp.int32, (capacity, rows), 0).astype(F32)
        for first in range(0, blocks, joined):
            picked = []
            for b in range(first, first + joined):
                chosen = jnp.concatenate(
                    [(slot_row_ref[b, e : e + 1, :] == slot_ids).astype(F32) for e in range(served)],
                    axis=0,
                ).astype(BF16)
                for copy in copies(0, b):
                    copy.wait()
                picked.append(dot(chosen, block_ref[b]))
            for e in range(served):
                part = [p[e * capacity : (e + 1) * capacity] for p in picked]
                taken_ref[e, first * capacity : (first + joined) * capacity] = jnp.concatenate(
                    part, axis=0
                ).astype(BF16)

    def serve(gate_ref, up_ref):
        received = taken_ref[expert]
        gate = dot(received, gate_ref[0])
        up = dot(received, up_ref[0])
        inner_ref[0] = (gate / (1.0 + jnp.exp(-gate)) * up).astype(BF16)

    @pl.when(expert < served // 2)
    def _():
        serve(own_gate_ref, own_up_ref)

    @pl.when(expert >= served // 2)
    def _():
        serve(other_gate_ref, other_up_ref)

    span = served * capacity
    lane = lax.broadcasted_iota(jnp.int32, (rows, 2 * span), 1)
    lane_expert, lane_slot = lane // capacity % served, (lane % capacity).astype(F32)
    share = blocks // served
    for i in range(share):
        b = expert * share + i
        slots, weights = slot_ref[b], weight_ref[b]
        slot = jnp.full((rows, 2 * span), -1.0, F32)
        weight = jnp.zeros((rows, 2 * span), F32)
        for e in range(served):
            slot = jnp.where(lane_expert == e, slots[:, e : e + 1], slot)
            weight = jnp.where(lane_expert == e, weights[:, e : e + 1], weight)
        high = weight.astype(BF16).astype(F32)
        spread_ref[b] = jnp.where(
            slot == lane_slot, jnp.where(lane < span, high, weight - high), 0.0
        ).astype(BF16)


def hidden_units(tokens, slots, own, other, capacity):
    devices, served, rows = slots[0].shape
    local = own[0].shape[0]
    width = own[0].shape[2]
    pieces = [(column, places) for column, places, _ in tokens]
    def own_spec(x):
        return pl.BlockSpec((1,) + x.shape[1:], lambda g, e: (jnp.minimum(e, local - 1), 0, 0))

    def other_spec(x):
        return pl.BlockSpec((1,) + x.shape[1:], lambda g, e: (jnp.maximum(e - local, 0), 0, 0))

    column_spec = pl.BlockSpec((BLOCKS_STEP, rows, served), lambda g, e: (g, 0, 0))
    return pl.pallas_call(
        functools.partial(hidden_units_kernel, capacity, pieces),
        grid=(devices // BLOCKS_STEP, served),
        in_specs=[
            pl.BlockSpec((BLOCKS_STEP, served, rows), lambda g, e: (g, 0, 0)),
            column_spec,
            column_spec,
        ]
        + [own_spec(x) for x in own]
        + [other_spec(x) for x in other]
        + [pl.BlockSpec(memory_space=pl.ANY)] * len(tokens),
        out_specs=[
            pl.BlockSpec((1, BLOCKS_STEP * capacity, width), lambda g, e: (e, g, 0)),
            pl.BlockSpec((BLOCKS_STEP, rows, 2 * served * capacity), lambda g, e: (g, 0, 0)),
        ],
        out_shape=[
            jax.ShapeDtypeStruct((served, devices * capacity, width), BF16),
            jax.ShapeDtypeStruct((devices, rows, 2 * served * capacity), BF16),
        ],
        scratch_shapes=[
            pltpu.VMEM((BLOCKS_STEP, rows, D), BF16),
            pltpu.VMEM((served, BLOCKS_STEP * capacity, D), BF16),
            pltpu.SemaphoreType.DMA((BLOCKS_STEP, len(GROUPS))),
        ],
        compiler_params=pltpu.CompilerParams(vmem_limit_bytes=56 * MIB),
        name="hidden_units",
    )(
        *slots,
        *own,
        *other,
        *[array for _, _, array in tokens],
    )


def order_places(order):
    count = len(order)
    return [
        sum(((j >> (count - 1 - k)) & 1) << bit for k, bit in enumerate(order))
        for j in range(1 << count)
    ]


def down_kernel(capacity, order, inner_ref, spread_ref, own_ref, other_ref, keep_ref, send_ref, out_ref):
    served = inner_ref.shape[0]
    local = served // 2
    for e in range(served):
        down = own_ref[e] if e < local else other_ref[e - local]
        out_ref[e] = dot(inner_ref[e], down)
    places = order_places(order)
    half = len(places) // 2
    for j, place in enumerate(places):
        mine = [out_ref[e, place * capacity : (place + 1) * capacity] for e in range(served)]
        stacked = jnp.concatenate(mine, axis=0).astype(BF16)
        block = dot(spread_ref[place], jnp.concatenate([stacked, stacked], axis=0)).astype(BF16)
        if j < half:
            keep_ref[j] = block
        else:
            send_ref[j - half] = block


def down_strips(inner, spread, own, other, capacity, order, start, width):
    served, slots, units = inner.shape
    devices, rows, _ = spread.shape
    first = start // STRIP

    def whole(x):
        return pl.BlockSpec(x.shape, lambda i: (0, 0, 0), pipeline_mode=pl.Buffered(1))

    down_spec = pl.BlockSpec((own.shape[0], units, STRIP), lambda i: (0, 0, first + i))
    half_spec = pl.BlockSpec((devices // 2, rows, STRIP), lambda i: (0, 0, i))
    half_shape = jax.ShapeDtypeStruct((devices // 2, rows, width), BF16)
    return pl.pallas_call(
        functools.partial(down_kernel, capacity, order),
        grid=(width // STRIP,),
        in_specs=[whole(inner), whole(spread), down_spec, down_spec],
        out_specs=[half_spec, half_spec],
        out_shape=[half_shape, half_shape],
        scratch_shapes=[pltpu.VMEM((served, slots, STRIP), F32)],
        compiler_params=pltpu.CompilerParams(vmem_limit_bytes=48 * MIB),
        name="down_strips",
    )(inner, spread, own, other)


def sum_by_halving(keep, send, stages):
    for stage in stages[:-1]:
        total = (keep.astype(F32) + stage_flip(send, stage).astype(F32)).astype(BF16)
        half = total.shape[0] // 2
        keep, send = total[:half], total[half:]
    return keep[0].astype(F32) + stage_flip(send, stages[-1])[0].astype(F32)


def routing(expert_ids, gate_weights, local_experts):
    outer, cores, inner = (lax.axis_size(a) for a in (("outer", "mid"), "core", "inner"))
    rows = expert_ids.shape[0]
    experts = local_experts * outer * cores * inner
    chosen = expert_ids.T[None] == jnp.arange(experts, dtype=jnp.int32)[:, None, None]
    dense = jnp.sum(jnp.where(chosen, gate_weights.T[None], 0.0), axis=1)
    by_chip = jnp.swapaxes(dense.reshape(outer, cores, inner, local_experts * rows), 1, 2)
    by_chip = by_chip.reshape(outer * inner, cores * local_experts, rows)
    return lax.all_to_all(by_chip, SAME_CORE, split_axis=0, concat_axis=0, tiled=True)


def positions(weights, local_experts):
    rows = weights.shape[2]
    turned = jnp.concatenate([weights[:, local_experts:], weights[:, :local_experts]], axis=1)
    weights = jnp.where(lax.axis_index("core") == 1, turned, weights)
    bits = weights.shape[0].bit_length() - 1
    table = jnp.asarray([order_places(order[::-1]) for order in core_orders(bits)], jnp.int32)
    source = lax.axis_index(SAME_CORE) ^ table[lax.axis_index("core")]
    weights = jnp.take(weights, source, axis=0, mode="clip")
    named = weights > 0.0
    rank = jnp.einsum(
        "set,tu->seu",
        named.astype(BF16),
        jnp.triu(jnp.ones((rows, rows), BF16)),
        preferred_element_type=F32,
    )
    slots = jnp.where(named, rank - 1.0, -1.0)
    return slots, jnp.swapaxes(slots, 1, 2), jnp.swapaxes(weights, 1, 2)


def core_orders(bits):
    first = tuple(range(bits))[::-1]
    second = tuple(first[n ^ 1] if n ^ 1 < bits else first[n] for n in range(bits))
    return first, second


def flipped(array, bit):
    devices = lax.axis_size(AXES)
    return lax.ppermute(array, AXES, [(i, i ^ bit) for i in range(devices)])


def place_flip(array, bit):
    return flipped(array, 1 << (bit if 1 << bit < lax.axis_size("inner") else bit + 1))


def over_rest(array):
    pieces = [array]
    for bit in range(lax.axis_size(REST).bit_length() - 1):
        pieces = pieces + [place_flip(piece, bit) for piece in pieces]
    return pieces


def stage_flip(array, stage):
    inner, devices = lax.axis_size("inner"), lax.axis_size(AXES)
    bits = lax.axis_size(SAME_CORE).bit_length() - 1

    def partner(i):
        bit = core_orders(bits)[i // inner % 2][stage]
        return i ^ (1 << (bit if 1 << bit < inner else bit + 1))

    return lax.ppermute(array, AXES, [(i, partner(i)) for i in range(devices)])


def to_everyone(array, stages, plan):
    pieces = [((0,), array[None])]
    for step, stage in enumerate(stages):
        for chosen in plan[step] if step < len(plan) else [range(len(pieces))]:
            picked = [pieces[i] for i in chosen]
            places = sum((places for places, _ in picked), ())
            joined = jnp.concatenate([piece for _, piece in picked], axis=0)
            pieces.append(
                (tuple(place | (1 << stage) for place in places), stage_flip(joined, stage))
            )
    return pieces


def shards(
    split_core,
    residual_in,
    query_input,
    key_input,
    value_input,
    out_gate,
    write_strength,
    decay_rate,
    head_gain,
    out_proj,
    post_gain,
    expert_ids,
    gate_weights,
    expert_gate,
    expert_up,
    expert_down,
):
    tok_rows = residual_in.shape[0]
    devices = lax.axis_size(AXES)
    inner_size = lax.axis_size("inner")
    local_experts = expert_gate.shape[0]
    capacity = max(2, tok_rows * TOP * 8 // (5 * local_experts * devices))
    early = over_rest(out_proj[:EARLY_ROWS])[1:]
    other_gate, other_up, other_down = (
        flipped(x, inner_size) for x in (expert_gate, expert_up, expert_down)
    )
    maps, mix = local_terms(query_input, key_input, value_input, write_strength, decay_rate)
    maps = after(maps, *early)
    served_weights = routing(after(expert_ids, maps), gate_weights, local_experts)
    others = (other_gate, other_up, other_down, served_weights)
    if split_core:
        core_early = [flipped(first, inner_size) for first in [out_proj] + early]
        others += tuple(core_early)
    states, whole = entering_states(maps, devices, others)
    late = over_rest(after(out_proj[EARLY_ROWS:], whole))[1:]
    slots = positions(served_weights, local_experts)
    proj = [(out_proj,)] + list(zip(early, late))
    places = lax.axis_index(REST) ^ jnp.arange(len(proj), dtype=jnp.int32)
    if split_core:
        core = lax.axis_index("core")
        core_late = [flipped(after(piece, states), inner_size) for piece in late]
        proj += [(core_early[0],)] + list(zip(core_early[1:], core_late))
        base = places // inner_size * (2 * inner_size) + places % inner_size
        places = jnp.concatenate([base + core * inner_size, base + (1 - core) * inner_size])
    hidden, *normed = finish(
        mix, states, out_gate, head_gain, proj, places, residual_in, post_gain
    )
    bits = slots[0].shape[0].bit_length() - 1
    plain, turned = tuple(range(bits)), tuple((n + bits - 2) % bits for n in range(bits))
    plans = (
        [[(0,)], [(0, 1)], [(0,), (1,), (2,)], [(0,), (1,), (2,), (3, 4), (5,)]],
        [[(0,)], [(0, 1)], [(0, 1, 2)], [(0, 1, 2), (3,)]],
    )
    tokens = []
    for column, (part, stages, plan) in enumerate(zip(normed, (plain, turned), plans)):
        tokens += [(column, places, piece) for places, piece in to_everyone(part, stages, plan)]
    inner, spread = hidden_units(
        tokens, slots, (expert_gate, expert_up), (other_gate, other_up), capacity
    )
    sums, start = [], 0
    for width, stages in ((512, plain), (512, plain), (512, turned), (512, plain)):
        keep, send = down_strips(
            inner, spread, expert_down, other_down, capacity, stages[::-1], start, width
        )
        sums.append(sum_by_halving(keep, send, stages[::-1]))
        start += width
    return (hidden.astype(F32) + jnp.concatenate(sums, axis=1)).astype(BF16)


def core_stride(devices):
    first = getattr(devices[0], "coords", None)
    for i in range(1, len(devices)):
        if first is not None and tuple(devices[i].coords) == tuple(first):
            return i
    return 1


def solution(mesh):
    devices = mesh.devices.reshape(-1)
    inner = core_stride(devices)
    columns = mesh.shape["exp"]
    if 2 * inner <= columns:
        shape, column_axes = (-1, columns // (2 * inner), 2, inner), AXES[1:]
    else:
        shape, column_axes = (-1, 1, 2, inner), ("inner",)
    split_core = "core" in column_axes
    view = Mesh(devices.reshape(shape), AXES)
    rows = P(AXES, None)
    placed = (
        (rows,) * 7 + (P(), P(None, column_axes), P(), rows, rows) + (P(AXES, None, None),) * 3
    )
    body = functools.partial(shards, split_core)
    return jax.shard_map(body, mesh=view, in_specs=placed, out_specs=rows, check_vma=False)
```

```python
import functools

import jax
import jax.numpy as jnp
from jax import lax
from jax.experimental import pallas as pl
from jax.experimental.pallas import tpu as pltpu
from jax.sharding import Mesh, PartitionSpec as P

D = 2048
HK = 8
GROUP_VALUE_HEADS = 16
DK = 128
DV = 128
TOP = 10
HEADS_STEP = 4
BLOCKS_STEP = 16
GROUPS = (1536, 512)
STRIP = 256
EARLY_ROWS = 768

F32 = jnp.float32
BF16 = jnp.bfloat16
AXES = ("outer", "mid", "core", "inner")
SAME_CORE = ("outer", "mid", "inner")
REST = ("mid", "inner")
MIB = 1 << 20


def halves(x):
    high = x.astype(BF16)
    return high, (x - high.astype(F32)).astype(BF16)


def dot(a, b):
    return jnp.dot(a, b, preferred_element_type=F32)


def product(left, right):
    n = right[0].shape[1]
    lhs = jnp.concatenate(left, axis=1)
    top = jnp.concatenate(right, axis=1)
    bottom = jnp.concatenate([right[0], jnp.zeros_like(right[0])], axis=1)
    both = dot(lhs, jnp.concatenate([top, bottom], axis=0))
    return both[:, :n] + both[:, n:]


def local_kernel(q_ref, k_ref, v_ref, logs_ref, logs_row_ref, strength_row_ref, strength_ref, maps_ref, mix_ref):
    n = k_ref.shape[0]
    row = lax.broadcasted_iota(jnp.int32, (n, n), 0)
    column = lax.broadcasted_iota(jnp.int32, (n, n), 1)
    inclusive, strict, diagonal = row >= column, row > column, row == column
    heads = maps_ref.shape[0]
    group = GROUP_VALUE_HEADS // HK
    identity = diagonal.astype(F32)

    keys = []
    for i in range(heads // group):
        lanes = slice(i * DK, (i + 1) * DK)
        k_raw, q_raw = k_ref[:, lanes], q_ref[:, lanes]
        k_wide, q_wide = k_raw.astype(F32), q_raw.astype(F32)
        dims = (((1,), (1,)), ((), ()))
        gram = lax.dot_general(k_raw, k_raw, dims, preferred_element_type=F32)
        scores = lax.dot_general(q_raw, k_raw, dims, preferred_element_type=F32)
        inv_k = lax.rsqrt(jnp.sum(k_wide * k_wide, axis=1, keepdims=True) + 1e-06)
        inv_k_row = lax.rsqrt(jnp.sum(jnp.where(diagonal, gram, 0.0), axis=0, keepdims=True) + 1e-06)
        inv_q = lax.rsqrt(jnp.sum(q_wide * q_wide, axis=1, keepdims=True) + 1e-06) * DK ** (-0.5)
        keys.append(
            dict(
                k=k_raw,
                k_t=jnp.transpose(k_wide).astype(BF16),
                q=q_wide * inv_q,
                gram=gram * inv_k * inv_k_row,
                scores=scores * inv_q * inv_k_row,
                inv=inv_k,
                inv_row=inv_k_row,
            )
        )

    ratios, systems, inverses = [], [], []
    for j in range(heads):
        logs, logs_row = logs_ref[0][:, j : j + 1], logs_row_ref[0][j : j + 1, :]
        ratio = jnp.where(inclusive, jnp.exp(jnp.where(inclusive, logs - logs_row, 0.0)), 0.0)
        system = jnp.where(strict, ratio * keys[j // group]["gram"], 0.0) * strength_ref[0][:, j : j + 1]
        first = (row // 2 == column // 2) & strict
        ratios.append(ratio)
        systems.append(halves(system))
        inverses.append(identity - jnp.where(first, system, 0.0))
    size = 2
    while size < n:
        pairs = (row // (2 * size) == column // (2 * size)) & (row // size > column // size)
        inverse_halves = [halves(t) for t in inverses]
        cut = [
            tuple(jnp.where(pairs, part.astype(F32), 0.0).astype(BF16) for part in s) for s in systems
        ]
        left = [product(t, c) for t, c in zip(inverse_halves, cut)]
        inverses = [
            t - product(halves(x), th) for t, x, th in zip(inverses, left, inverse_halves)
        ]
        size *= 2

    for j in range(heads):
        key = keys[j // group]
        logs, logs_row = logs_ref[0][:, j : j + 1], logs_row_ref[0][j : j + 1, :]
        strength_row = strength_row_ref[0][j : j + 1, :]
        value = v_ref[:, j * DV : (j + 1) * DV]
        t = inverses[j]
        new_value = dot(
            jnp.concatenate(halves(t * strength_row), axis=1), jnp.concatenate([value, value], axis=0)
        )
        key_matrix = dot(
            jnp.concatenate(halves(t * (strength_row * jnp.exp(logs_row) * key["inv_row"])), axis=1),
            jnp.concatenate([key["k"], key["k"]], axis=0),
        )
        both = jnp.concatenate([key_matrix, new_value], axis=1)
        last = logs[n - 1 : n, :]
        faded = halves(both * (jnp.exp(last - logs) * key["inv"]))
        state = dot(
            jnp.concatenate([key["k_t"], key["k_t"]], axis=1), jnp.concatenate(faded, axis=0)
        )
        high, low = halves(jnp.exp(last) * identity - state[:, :DK])
        maps_ref[j, :, :DK] = high
        maps_ref[j, :, DK : 2 * DK] = low
        maps_ref[j, :, 2 * DK :] = state[:, DK:].astype(BF16)
        mixed = halves(ratios[j] * key["scores"])
        both_halves = halves(both)
        out = dot(
            jnp.concatenate(mixed, axis=1), jnp.concatenate([both_halves[0], both_halves[0]], axis=0)
        ) + dot(mixed[0], both_halves[1])
        mix_ref[j, :, :DK] = key["q"] * jnp.exp(logs) - out[:, :DK]
        mix_ref[j, :, DK:] = out[:, DK:]


def local_terms(query_input, key_input, value_input, write_strength, decay_rate):
    n = key_input.shape[0]
    groups, per_key = GROUP_VALUE_HEADS // HEADS_STEP, GROUP_VALUE_HEADS // HK
    lower = jnp.tril(jnp.ones((n, n), F32))
    logs = jnp.dot(lower, -decay_rate, precision=lax.Precision.HIGHEST)

    def columns(x):
        return jnp.swapaxes(x.reshape(n, groups, HEADS_STEP), 0, 1)

    def rows(x):
        return x.T.reshape(groups, HEADS_STEP, n)

    wide = HEADS_STEP // per_key * DK
    column_spec = pl.BlockSpec((1, n, HEADS_STEP), lambda i: (i, 0, 0))
    row_spec = pl.BlockSpec((1, HEADS_STEP, n), lambda i: (i, 0, 0))
    out_spec = pl.BlockSpec((HEADS_STEP, DK, 2 * DK + DV), lambda i: (i, 0, 0))
    mix_spec = pl.BlockSpec((HEADS_STEP, n, DK + DV), lambda i: (i, 0, 0))
    return pl.pallas_call(
        local_kernel,
        grid=(groups,),
        in_specs=[
            pl.BlockSpec((n, wide), lambda i: (0, i)),
            pl.BlockSpec((n, wide), lambda i: (0, i)),
            pl.BlockSpec((n, HEADS_STEP * DV), lambda i: (0, i)),
            column_spec,
            row_spec,
            row_spec,
            column_spec,
        ],
        out_specs=[out_spec, mix_spec],
        out_shape=[
            jax.ShapeDtypeStruct((GROUP_VALUE_HEADS, DK, 2 * DK + DV), BF16),
            jax.ShapeDtypeStruct((GROUP_VALUE_HEADS, n, DK + DV), F32),
        ],
        compiler_params=pltpu.CompilerParams(vmem_limit_bytes=40 * MIB),
        name="local_terms",
    )(
        query_input,
        key_input,
        value_input,
        columns(logs),
        rows(logs),
        rows(write_strength),
        columns(write_strength),
    )


def chain_kernel(maps_ref, *refs):
    *_, before_ref, whole_ref = refs
    row = lax.broadcasted_iota(jnp.int32, (DK, DK + DV), 0)
    column = lax.broadcasted_iota(jnp.int32, (DK, DK + DV), 1)
    passed = (row == column).astype(F32)
    for i in range(maps_ref.shape[0]):
        before_ref[i] = passed
        high, low = halves(passed)
        passed = dot(maps_ref[i, :, : 2 * DK], jnp.concatenate([high, high], axis=0)) + dot(
            maps_ref[i, :, :DK], low
        )
        passed = jnp.concatenate(
            [passed[:, :DK], passed[:, DK:] + maps_ref[i, :, 2 * DK :].astype(F32)], axis=1
        )
    whole_ref[...] = passed


def chain(maps, *others):
    count = maps.shape[0]
    return pl.pallas_call(
        chain_kernel,
        in_specs=[pl.BlockSpec(memory_space=pltpu.VMEM)]
        + [pl.BlockSpec(memory_space=pl.ANY)] * len(others),
        out_shape=[
            jax.ShapeDtypeStruct((count, DK, DK + DV), F32),
            jax.ShapeDtypeStruct((DK, DK + DV), F32),
        ],
        compiler_params=pltpu.CompilerParams(vmem_limit_bytes=40 * MIB),
        name="chain",
    )(maps, *others)


def tie_kernel(*refs):
    pass


def after(array, *others):
    anywhere = pl.BlockSpec(memory_space=pl.ANY)
    return pl.pallas_call(
        tie_kernel,
        in_specs=[anywhere] * (1 + len(others)),
        out_specs=anywhere,
        out_shape=jax.ShapeDtypeStruct(array.shape, array.dtype),
        input_output_aliases={0: 0},
        name="after",
    )(array, *others)


def entering_states(maps, devices, others):
    heads = maps.shape[0]
    segments = devices // heads
    groups = [[g * heads + h for h in range(heads)] for g in range(segments)]
    by_device = lax.all_to_all(
        maps, AXES, split_axis=0, concat_axis=0, axis_index_groups=groups, tiled=True
    )
    before, whole = chain(by_device, *others)
    if segments == 2:
        start = lax.ppermute(whole[:, DK:], AXES, [(h, heads + h) for h in range(heads)])
    else:
        across = [[g * heads + h for g in range(segments)] for h in range(heads)]
        adds = lax.all_gather(whole[:, DK:], AXES, axis_index_groups=across)
        steps = lax.all_gather(whole[:, :DK], AXES, axis_index_groups=across)
        segment = lax.axis_index(AXES) // heads
        carry = adds[0]
        start = jnp.where(segment == 1, carry, 0.0)
        for g in range(2, segments):
            carry = adds[g - 1] + jnp.dot(steps[g - 1], carry, precision=lax.Precision.HIGHEST)
            start = jnp.where(segment == g, carry, start)
    states = (
        jnp.dot(
            before[:, :, :DK].reshape(heads * DK, DK), start, precision=lax.Precision.HIGH
        ).reshape(heads, DK, DV)
        + before[:, :, DK:]
    ).astype(BF16)
    back = lax.all_to_all(
        states, AXES, split_axis=0, concat_axis=0, axis_index_groups=groups, tiled=True
    )
    return back, states


def finish_kernel(
    parts, place_ref, mix_ref, state_ref, gate_ref, gain_ref, residual_ref, post_ref, *refs
):
    *proj_refs, hidden_ref, first_ref, second_ref, core_ref = refs
    for h in range(GROUP_VALUE_HEADS):
        lanes = slice(h * DV, (h + 1) * DV)
        state = state_ref[h]
        recurrent = (
            dot(
                jnp.concatenate(halves(mix_ref[h, :, :DK]), axis=1),
                jnp.concatenate([state, state], axis=0),
            )
            + mix_ref[h, :, DK:]
        )
        inv_rms = lax.rsqrt(jnp.mean(recurrent * recurrent, axis=1, keepdims=True) + 1e-06)
        gate = gate_ref[:, lanes].astype(F32)
        act = gate / (1.0 + jnp.exp(-gate))
        core_ref[:, lanes] = (recurrent * inv_rms * gain_ref[...] * act).astype(BF16)
    core = core_ref[...]
    squares = 0.0
    proj_refs = list(proj_refs)
    for i, count in enumerate(parts):
        refs, proj_refs = proj_refs[:count], proj_refs[count:]
        wide = refs[0].shape[1]
        lanes = pl.ds(pl.multiple_of(place_ref[i] * wide, wide), wide)
        mixed, first = residual_ref[:, lanes].astype(F32), 0
        for ref in refs:
            mixed += dot(core[:, first : first + ref.shape[0]], ref[...])
            first += ref.shape[0]
        hidden = mixed.astype(BF16)
        hidden_ref[:, lanes] = hidden
        widened = hidden.astype(F32)
        squares += jnp.sum(widened * widened, axis=1, keepdims=True)
    inv_rms = lax.rsqrt(squares * (1.0 / D) + 1e-06)
    normed = (hidden_ref[...].astype(F32) * inv_rms * post_ref[...]).astype(BF16)
    start = 0
    for ref, width in zip((first_ref, second_ref), GROUPS):
        ref[...] = normed[:, start : start + width]
        start += width


def finish(mix, states, out_gate, head_gain, proj, places, residual_in, post_gain):
    shape = residual_in.shape
    vmem = pl.BlockSpec(memory_space=pltpu.VMEM)
    flat = [part for piece in proj for part in piece]
    return pl.pallas_call(
        functools.partial(finish_kernel, [len(piece) for piece in proj]),
        in_specs=[pl.BlockSpec(memory_space=pltpu.SMEM)] + [vmem] * (6 + len(flat)),
        out_shape=[
            jax.ShapeDtypeStruct((shape[0], wide), BF16) for wide in (D,) + GROUPS
        ],
        scratch_shapes=[pltpu.VMEM(shape, BF16)],
        compiler_params=pltpu.CompilerParams(vmem_limit_bytes=48 * MIB),
        name="finish",
    )(
        places,
        mix,
        states,
        out_gate,
        head_gain.reshape(1, DV),
        residual_in,
        post_gain.reshape(1, D),
        *flat,
    )


def hidden_units_kernel(
    capacity,
    pieces,
    slot_row_ref,
    slot_ref,
    weight_ref,
    own_gate_ref,
    own_up_ref,
    other_gate_ref,
    other_up_ref,
    *refs,
):
    *token_refs, inner_ref, spread_ref, block_ref, taken_ref, sems = refs
    group, expert = pl.program_id(0), pl.program_id(1)
    blocks, rows, _ = block_ref.shape
    served = taken_ref.shape[0]
    joined = max(1, 16 // capacity)

    def copies(step, b):
        found = []
        start = 0
        for part, width in enumerate(GROUPS):
            for ref, (column, places) in zip(token_refs, pieces):
                place = step * blocks + b
                if column == part and place in places:
                    found.append(
                        pltpu.make_async_copy(
                            ref.at[places.index(place)],
                            block_ref.at[b, :, start : start + width],
                            sems.at[b, part],
                        )
                    )
            start += width
        return found

    def load(step):
        @pl.when((expert == 0) & (group == step))
        def _():
            for b in range(blocks):
                for copy in copies(step, b):
                    copy.start()

    for step in range(sum(len(places) for column, places in pieces if column == 0) // blocks):
        load(step)

    @pl.when(expert == 0)
    def _():
        slot_ids = lax.broadcasted_iota(jnp.int32, (capacity, rows), 0).astype(F32)
        for first in range(0, blocks, joined):
            picked = []
            for b in range(first, first + joined):
                chosen = jnp.concatenate(
                    [(slot_row_ref[b, e : e + 1, :] == slot_ids).astype(F32) for e in range(served)],
                    axis=0,
                ).astype(BF16)
                for copy in copies(0, b):
                    copy.wait()
                picked.append(dot(chosen, block_ref[b]))
            for e in range(served):
                part = [p[e * capacity : (e + 1) * capacity] for p in picked]
                taken_ref[e, first * capacity : (first + joined) * capacity] = jnp.concatenate(
                    part, axis=0
                ).astype(BF16)

    def serve(gate_ref, up_ref):
        received = taken_ref[expert]
        gate = dot(received, gate_ref[0])
        up = dot(received, up_ref[0])
        inner_ref[0] = (gate / (1.0 + jnp.exp(-gate)) * up).astype(BF16)

    @pl.when(expert < served // 2)
    def _():
        serve(own_gate_ref, own_up_ref)

    @pl.when(expert >= served // 2)
    def _():
        serve(other_gate_ref, other_up_ref)

    span = served * capacity
    lane = lax.broadcasted_iota(jnp.int32, (rows, 2 * span), 1)
    lane_expert, lane_slot = lane // capacity % served, (lane % capacity).astype(F32)
    share = blocks // served
    for i in range(share):
        b = expert * share + i
        slots, weights = slot_ref[b], weight_ref[b]
        slot = jnp.full((rows, 2 * span), -1.0, F32)
        weight = jnp.zeros((rows, 2 * span), F32)
        for e in range(served):
            slot = jnp.where(lane_expert == e, slots[:, e : e + 1], slot)
            weight = jnp.where(lane_expert == e, weights[:, e : e + 1], weight)
        high = weight.astype(BF16).astype(F32)
        spread_ref[b] = jnp.where(
            slot == lane_slot, jnp.where(lane < span, high, weight - high), 0.0
        ).astype(BF16)


def hidden_units(tokens, slots, own, other, capacity):
    devices, served, rows = slots[0].shape
    local = own[0].shape[0]
    width = own[0].shape[2]
    pieces = [(column, places) for column, places, _ in tokens]
    def own_spec(x):
        return pl.BlockSpec((1,) + x.shape[1:], lambda g, e: (jnp.minimum(e, local - 1), 0, 0))

    def other_spec(x):
        return pl.BlockSpec((1,) + x.shape[1:], lambda g, e: (jnp.maximum(e - local, 0), 0, 0))

    column_spec = pl.BlockSpec((BLOCKS_STEP, rows, served), lambda g, e: (g, 0, 0))
    return pl.pallas_call(
        functools.partial(hidden_units_kernel, capacity, pieces),
        grid=(devices // BLOCKS_STEP, served),
        in_specs=[
            pl.BlockSpec((BLOCKS_STEP, served, rows), lambda g, e: (g, 0, 0)),
            column_spec,
            column_spec,
        ]
        + [own_spec(x) for x in own]
        + [other_spec(x) for x in other]
        + [pl.BlockSpec(memory_space=pl.ANY)] * len(tokens),
        out_specs=[
            pl.BlockSpec((1, BLOCKS_STEP * capacity, width), lambda g, e: (e, g, 0)),
            pl.BlockSpec((BLOCKS_STEP, rows, 2 * served * capacity), lambda g, e: (g, 0, 0)),
        ],
        out_shape=[
            jax.ShapeDtypeStruct((served, devices * capacity, width), BF16),
            jax.ShapeDtypeStruct((devices, rows, 2 * served * capacity), BF16),
        ],
        scratch_shapes=[
            pltpu.VMEM((BLOCKS_STEP, rows, D), BF16),
            pltpu.VMEM((served, BLOCKS_STEP * capacity, D), BF16),
            pltpu.SemaphoreType.DMA((BLOCKS_STEP, len(GROUPS))),
        ],
        compiler_params=pltpu.CompilerParams(vmem_limit_bytes=56 * MIB),
        name="hidden_units",
    )(
        *slots,
        *own,
        *other,
        *[array for _, _, array in tokens],
    )


def order_places(order):
    count = len(order)
    return [
        sum(((j >> (count - 1 - k)) & 1) << bit for k, bit in enumerate(order))
        for j in range(1 << count)
    ]


def down_kernel(capacity, order, inner_ref, spread_ref, own_ref, other_ref, keep_ref, send_ref, out_ref):
    served = inner_ref.shape[0]
    local = served // 2
    for e in range(served):
        down = own_ref[e] if e < local else other_ref[e - local]
        out_ref[e] = dot(inner_ref[e], down)
    places = order_places(order)
    half = len(places) // 2
    for j, place in enumerate(places):
        mine = [out_ref[e, place * capacity : (place + 1) * capacity] for e in range(served)]
        stacked = jnp.concatenate(mine, axis=0).astype(BF16)
        block = dot(spread_ref[place], jnp.concatenate([stacked, stacked], axis=0)).astype(BF16)
        if j < half:
            keep_ref[j] = block
        else:
            send_ref[j - half] = block


def down_strips(inner, spread, own, other, capacity, order, start, width):
    served, slots, units = inner.shape
    devices, rows, _ = spread.shape
    first = start // STRIP

    def whole(x):
        return pl.BlockSpec(x.shape, lambda i: (0, 0, 0), pipeline_mode=pl.Buffered(1))

    down_spec = pl.BlockSpec((own.shape[0], units, STRIP), lambda i: (0, 0, first + i))
    half_spec = pl.BlockSpec((devices // 2, rows, STRIP), lambda i: (0, 0, i))
    half_shape = jax.ShapeDtypeStruct((devices // 2, rows, width), BF16)
    return pl.pallas_call(
        functools.partial(down_kernel, capacity, order),
        grid=(width // STRIP,),
        in_specs=[whole(inner), whole(spread), down_spec, down_spec],
        out_specs=[half_spec, half_spec],
        out_shape=[half_shape, half_shape],
        scratch_shapes=[pltpu.VMEM((served, slots, STRIP), F32)],
        compiler_params=pltpu.CompilerParams(vmem_limit_bytes=48 * MIB),
        name="down_strips",
    )(inner, spread, own, other)


def sum_by_halving(keep, send, stages):
    for stage in stages[:-1]:
        total = (keep.astype(F32) + stage_flip(send, stage).astype(F32)).astype(BF16)
        half = total.shape[0] // 2
        keep, send = total[:half], total[half:]
    return keep[0].astype(F32) + stage_flip(send, stages[-1])[0].astype(F32)


def routing(expert_ids, gate_weights, local_experts):
    outer, cores, inner = (lax.axis_size(a) for a in (("outer", "mid"), "core", "inner"))
    experts = local_experts * outer * cores * inner
    chosen = expert_ids.T[None] == jnp.arange(experts, dtype=jnp.int32)[:, None, None]
    dense = jnp.sum(jnp.where(chosen, gate_weights.T[None], 0.0), axis=1)
    everyone = lax.all_gather(dense, SAME_CORE)
    device = lax.axis_index(AXES)
    return jnp.concatenate(
        [
            lax.dynamic_slice_in_dim(everyone, owner * local_experts, local_experts, axis=1)
            for owner in (device, device ^ inner)
        ],
        axis=1,
    )


def positions(weights):
    rows = weights.shape[2]
    bits = weights.shape[0].bit_length() - 1
    table = jnp.asarray([order_places(order[::-1]) for order in core_orders(bits)], jnp.int32)
    source = lax.axis_index(SAME_CORE) ^ table[lax.axis_index("core")]
    weights = jnp.take(weights, source, axis=0, mode="clip")
    named = weights > 0.0
    rank = jnp.einsum(
        "set,tu->seu",
        named.astype(BF16),
        jnp.triu(jnp.ones((rows, rows), BF16)),
        preferred_element_type=F32,
    )
    slots = jnp.where(named, rank - 1.0, -1.0)
    return slots, jnp.swapaxes(slots, 1, 2), jnp.swapaxes(weights, 1, 2)


def core_orders(bits):
    first = tuple(range(bits))[::-1]
    second = tuple(first[n ^ 1] if n ^ 1 < bits else first[n] for n in range(bits))
    return first, second


def flipped(array, bit):
    devices = lax.axis_size(AXES)
    return lax.ppermute(array, AXES, [(i, i ^ bit) for i in range(devices)])


def place_flip(array, bit):
    return flipped(array, 1 << (bit if 1 << bit < lax.axis_size("inner") else bit + 1))


def over_rest(array):
    pieces = [array]
    for bit in range(lax.axis_size(REST).bit_length() - 1):
        pieces = pieces + [place_flip(piece, bit) for piece in pieces]
    return pieces


def stage_flip(array, stage):
    inner, devices = lax.axis_size("inner"), lax.axis_size(AXES)
    bits = lax.axis_size(SAME_CORE).bit_length() - 1

    def partner(i):
        bit = core_orders(bits)[i // inner % 2][stage]
        return i ^ (1 << (bit if 1 << bit < inner else bit + 1))

    return lax.ppermute(array, AXES, [(i, partner(i)) for i in range(devices)])


def to_everyone(array, stages, plan):
    pieces = [((0,), array[None])]
    for step, stage in enumerate(stages):
        for chosen in plan[step] if step < len(plan) else [range(len(pieces))]:
            picked = [pieces[i] for i in chosen]
            places = sum((places for places, _ in picked), ())
            joined = jnp.concatenate([piece for _, piece in picked], axis=0)
            pieces.append(
                (tuple(place | (1 << stage) for place in places), stage_flip(joined, stage))
            )
    return pieces


def shards(
    split_core,
    residual_in,
    query_input,
    key_input,
    value_input,
    out_gate,
    write_strength,
    decay_rate,
    head_gain,
    out_proj,
    post_gain,
    expert_ids,
    gate_weights,
    expert_gate,
    expert_up,
    expert_down,
):
    tok_rows = residual_in.shape[0]
    devices = lax.axis_size(AXES)
    inner_size = lax.axis_size("inner")
    local_experts = expert_gate.shape[0]
    capacity = max(2, tok_rows * TOP * 8 // (5 * local_experts * devices))
    early = over_rest(out_proj[:EARLY_ROWS])[1:]
    late = lax.all_gather(out_proj[EARLY_ROWS:], REST)
    other_gate, other_up, other_down = (
        flipped(x, inner_size) for x in (expert_gate, expert_up, expert_down)
    )
    maps, mix = local_terms(query_input, key_input, value_input, write_strength, decay_rate)
    maps = after(maps, *early)
    served_weights = routing(after(expert_ids, maps), gate_weights, local_experts)
    others = (other_gate, other_up, other_down)
    if split_core:
        core_early = [flipped(first, inner_size) for first in [out_proj] + early]
        others += tuple(core_early)
    states, leaving = entering_states(maps, devices, others)
    slots = positions(served_weights)
    late = after(late, leaving)
    places = lax.axis_index(REST) ^ jnp.arange(late.shape[0], dtype=jnp.int32)
    late = [
        lax.dynamic_index_in_dim(late, places[q], keepdims=False) for q in range(1, late.shape[0])
    ]
    proj = [(out_proj,)] + list(zip(early, late))
    if split_core:
        core = lax.axis_index("core")
        core_late = [flipped(piece, inner_size) for piece in late]
        proj += [(core_early[0],)] + list(zip(core_early[1:], core_late))
        base = places // inner_size * (2 * inner_size) + places % inner_size
        places = jnp.concatenate([base + core * inner_size, base + (1 - core) * inner_size])
    hidden, *normed = finish(
        mix, states, out_gate, head_gain, proj, places, residual_in, post_gain
    )
    bits = slots[0].shape[0].bit_length() - 1
    plain, turned = tuple(range(bits)), tuple((n + bits - 2) % bits for n in range(bits))
    plans = (
        [[(0,)], [(0, 1)], [(0, 1), (2,)], [(0, 1), (2,), (3,), (4,)]],
        [[(0,)], [(0, 1)], [(0, 1, 2)], [(0, 1, 2), (3,)]],
    )
    tokens = []
    for column, (part, stages, plan) in enumerate(zip(normed, (plain, turned), plans)):
        tokens += [(column, places, piece) for places, piece in to_everyone(part, stages, plan)]
    inner, spread = hidden_units(
        tokens, slots, (expert_gate, expert_up), (other_gate, other_up), capacity
    )
    sums, start = [], 0
    for width, stages in ((512, plain), (512, plain), (512, turned), (512, plain)):
        keep, send = down_strips(
            inner, spread, expert_down, other_down, capacity, stages[::-1], start, width
        )
        sums.append(sum_by_halving(keep, send, stages[::-1]))
        start += width
    return (hidden.astype(F32) + jnp.concatenate(sums, axis=1)).astype(BF16)


def core_stride(devices):
    first = getattr(devices[0], "coords", None)
    for i in range(1, len(devices)):
        if first is not None and tuple(devices[i].coords) == tuple(first):
            return i
    return 1


def solution(mesh):
    devices = mesh.devices.reshape(-1)
    inner = core_stride(devices)
    columns = mesh.shape["exp"]
    if 2 * inner <= columns:
        shape, column_axes = (-1, columns // (2 * inner), 2, inner), AXES[1:]
    else:
        shape, column_axes = (-1, 1, 2, inner), ("inner",)
    split_core = "core" in column_axes
    view = Mesh(devices.reshape(shape), AXES)
    rows = P(AXES, None)
    placed = (
        (rows,) * 7 + (P(), P(None, column_axes), P(), rows, rows) + (P(AXES, None, None),) * 3
    )
    body = functools.partial(shards, split_core)
    return jax.shard_map(body, mesh=view, in_specs=placed, out_specs=rows, check_vma=False)
```

```python
import functools

import jax
import jax.numpy as jnp
from jax import lax
from jax.experimental import pallas as pl
from jax.experimental.pallas import tpu as pltpu
from jax.sharding import Mesh, PartitionSpec as P

D = 2048
HK = 8
GROUP_VALUE_HEADS = 16
DK = 128
DV = 128
TOP = 10
HEADS_STEP = 4
BLOCKS_STEP = 16
GROUPS = (1536, 512)
STRIP = 256

F32 = jnp.float32
BF16 = jnp.bfloat16
AXES = ("outer", "mid", "core", "inner")
SAME_CORE = ("outer", "mid", "inner")
REST = ("mid", "inner")
MIB = 1 << 20


def halves(x):
    high = x.astype(BF16)
    return high, (x - high.astype(F32)).astype(BF16)


def dot(a, b):
    return jnp.dot(a, b, preferred_element_type=F32)


def product(left, right):
    n = right[0].shape[1]
    lhs = jnp.concatenate(left, axis=1)
    top = jnp.concatenate(right, axis=1)
    bottom = jnp.concatenate([right[0], jnp.zeros_like(right[0])], axis=1)
    both = dot(lhs, jnp.concatenate([top, bottom], axis=0))
    return both[:, :n] + both[:, n:]


def local_kernel(q_ref, k_ref, v_ref, logs_ref, logs_row_ref, strength_row_ref, strength_ref, maps_ref, mix_ref):
    n = k_ref.shape[0]
    row = lax.broadcasted_iota(jnp.int32, (n, n), 0)
    column = lax.broadcasted_iota(jnp.int32, (n, n), 1)
    inclusive, strict, diagonal = row >= column, row > column, row == column
    heads = maps_ref.shape[0]
    group = GROUP_VALUE_HEADS // HK
    identity = diagonal.astype(F32)

    keys = []
    for i in range(heads // group):
        lanes = slice(i * DK, (i + 1) * DK)
        k_raw, q_raw = k_ref[:, lanes], q_ref[:, lanes]
        k_wide, q_wide = k_raw.astype(F32), q_raw.astype(F32)
        dims = (((1,), (1,)), ((), ()))
        gram = lax.dot_general(k_raw, k_raw, dims, preferred_element_type=F32)
        scores = lax.dot_general(q_raw, k_raw, dims, preferred_element_type=F32)
        inv_k = lax.rsqrt(jnp.sum(k_wide * k_wide, axis=1, keepdims=True) + 1e-06)
        inv_k_row = lax.rsqrt(jnp.sum(jnp.where(diagonal, gram, 0.0), axis=0, keepdims=True) + 1e-06)
        inv_q = lax.rsqrt(jnp.sum(q_wide * q_wide, axis=1, keepdims=True) + 1e-06) * DK ** (-0.5)
        keys.append(
            dict(
                k=k_raw,
                k_t=jnp.transpose(k_wide).astype(BF16),
                q=q_wide * inv_q,
                gram=gram * inv_k * inv_k_row,
                scores=scores * inv_q * inv_k_row,
                inv=inv_k,
                inv_row=inv_k_row,
            )
        )

    ratios, systems, inverses = [], [], []
    for j in range(heads):
        logs, logs_row = logs_ref[0][:, j : j + 1], logs_row_ref[0][j : j + 1, :]
        ratio = jnp.where(inclusive, jnp.exp(jnp.where(inclusive, logs - logs_row, 0.0)), 0.0)
        system = jnp.where(strict, ratio * keys[j // group]["gram"], 0.0) * strength_ref[0][:, j : j + 1]
        first = (row // 2 == column // 2) & strict
        ratios.append(ratio)
        systems.append(halves(system))
        inverses.append(identity - jnp.where(first, system, 0.0))
    size = 2
    while size < n:
        pairs = (row // (2 * size) == column // (2 * size)) & (row // size > column // size)
        inverse_halves = [halves(t) for t in inverses]
        cut = [
            tuple(jnp.where(pairs, part.astype(F32), 0.0).astype(BF16) for part in s) for s in systems
        ]
        left = [product(t, c) for t, c in zip(inverse_halves, cut)]
        inverses = [
            t - product(halves(x), th) for t, x, th in zip(inverses, left, inverse_halves)
        ]
        size *= 2

    for j in range(heads):
        key = keys[j // group]
        logs, logs_row = logs_ref[0][:, j : j + 1], logs_row_ref[0][j : j + 1, :]
        strength_row = strength_row_ref[0][j : j + 1, :]
        value = v_ref[:, j * DV : (j + 1) * DV]
        t = inverses[j]
        new_value = dot(
            jnp.concatenate(halves(t * strength_row), axis=1), jnp.concatenate([value, value], axis=0)
        )
        key_matrix = dot(
            jnp.concatenate(halves(t * (strength_row * jnp.exp(logs_row) * key["inv_row"])), axis=1),
            jnp.concatenate([key["k"], key["k"]], axis=0),
        )
        both = jnp.concatenate([key_matrix, new_value], axis=1)
        last = logs[n - 1 : n, :]
        faded = halves(both * (jnp.exp(last - logs) * key["inv"]))
        state = dot(
            jnp.concatenate([key["k_t"], key["k_t"]], axis=1), jnp.concatenate(faded, axis=0)
        )
        high, low = halves(jnp.exp(last) * identity - state[:, :DK])
        maps_ref[j, :, :DK] = high
        maps_ref[j, :, DK : 2 * DK] = low
        maps_ref[j, :, 2 * DK :] = state[:, DK:].astype(BF16)
        mixed = halves(ratios[j] * key["scores"])
        both_halves = halves(both)
        out = dot(
            jnp.concatenate(mixed, axis=1), jnp.concatenate([both_halves[0], both_halves[0]], axis=0)
        ) + dot(mixed[0], both_halves[1])
        mix_ref[j, :, :DK] = key["q"] * jnp.exp(logs) - out[:, :DK]
        mix_ref[j, :, DK:] = out[:, DK:]


def local_terms(query_input, key_input, value_input, write_strength, decay_rate):
    n = key_input.shape[0]
    groups, per_key = GROUP_VALUE_HEADS // HEADS_STEP, GROUP_VALUE_HEADS // HK
    lower = jnp.tril(jnp.ones((n, n), F32))
    logs = jnp.dot(lower, -decay_rate, precision=lax.Precision.HIGHEST)

    def columns(x):
        return jnp.swapaxes(x.reshape(n, groups, HEADS_STEP), 0, 1)

    def rows(x):
        return x.T.reshape(groups, HEADS_STEP, n)

    wide = HEADS_STEP // per_key * DK
    column_spec = pl.BlockSpec((1, n, HEADS_STEP), lambda i: (i, 0, 0))
    row_spec = pl.BlockSpec((1, HEADS_STEP, n), lambda i: (i, 0, 0))
    out_spec = pl.BlockSpec((HEADS_STEP, DK, 2 * DK + DV), lambda i: (i, 0, 0))
    mix_spec = pl.BlockSpec((HEADS_STEP, n, DK + DV), lambda i: (i, 0, 0))
    return pl.pallas_call(
        local_kernel,
        grid=(groups,),
        in_specs=[
            pl.BlockSpec((n, wide), lambda i: (0, i)),
            pl.BlockSpec((n, wide), lambda i: (0, i)),
            pl.BlockSpec((n, HEADS_STEP * DV), lambda i: (0, i)),
            column_spec,
            row_spec,
            row_spec,
            column_spec,
        ],
        out_specs=[out_spec, mix_spec],
        out_shape=[
            jax.ShapeDtypeStruct((GROUP_VALUE_HEADS, DK, 2 * DK + DV), BF16),
            jax.ShapeDtypeStruct((GROUP_VALUE_HEADS, n, DK + DV), F32),
        ],
        compiler_params=pltpu.CompilerParams(vmem_limit_bytes=40 * MIB),
        name="local_terms",
    )(
        query_input,
        key_input,
        value_input,
        columns(logs),
        rows(logs),
        rows(write_strength),
        columns(write_strength),
    )


def chain_kernel(maps_ref, *refs):
    *_, before_ref, whole_ref = refs
    row = lax.broadcasted_iota(jnp.int32, (DK, DK + DV), 0)
    column = lax.broadcasted_iota(jnp.int32, (DK, DK + DV), 1)
    passed = (row == column).astype(F32)
    for i in range(maps_ref.shape[0]):
        before_ref[i] = passed
        high, low = halves(passed)
        passed = dot(maps_ref[i, :, : 2 * DK], jnp.concatenate([high, high], axis=0)) + dot(
            maps_ref[i, :, :DK], low
        )
        passed = jnp.concatenate(
            [passed[:, :DK], passed[:, DK:] + maps_ref[i, :, 2 * DK :].astype(F32)], axis=1
        )
    whole_ref[...] = passed


def chain(maps, *others):
    count = maps.shape[0]
    return pl.pallas_call(
        chain_kernel,
        in_specs=[pl.BlockSpec(memory_space=pltpu.VMEM)]
        + [pl.BlockSpec(memory_space=pl.ANY)] * len(others),
        out_shape=[
            jax.ShapeDtypeStruct((count, DK, DK + DV), F32),
            jax.ShapeDtypeStruct((DK, DK + DV), F32),
        ],
        compiler_params=pltpu.CompilerParams(vmem_limit_bytes=40 * MIB),
        name="chain",
    )(maps, *others)


def tie_kernel(*refs):
    pass


def after(array, *others):
    anywhere = pl.BlockSpec(memory_space=pl.ANY)
    return pl.pallas_call(
        tie_kernel,
        in_specs=[anywhere] * (1 + len(others)),
        out_specs=anywhere,
        out_shape=jax.ShapeDtypeStruct(array.shape, array.dtype),
        input_output_aliases={0: 0},
        name="after",
    )(array, *others)


def entering_states(maps, devices, others):
    heads = maps.shape[0]
    segments = devices // heads
    groups = [[g * heads + h for h in range(heads)] for g in range(segments)]
    by_device = lax.all_to_all(
        maps, AXES, split_axis=0, concat_axis=0, axis_index_groups=groups, tiled=True
    )
    before, whole = chain(by_device, *others)
    if segments == 2:
        start = lax.ppermute(whole[:, DK:], AXES, [(h, heads + h) for h in range(heads)])
    else:
        across = [[g * heads + h for g in range(segments)] for h in range(heads)]
        adds = lax.all_gather(whole[:, DK:], AXES, axis_index_groups=across)
        steps = lax.all_gather(whole[:, :DK], AXES, axis_index_groups=across)
        segment = lax.axis_index(AXES) // heads
        carry = adds[0]
        start = jnp.where(segment == 1, carry, 0.0)
        for g in range(2, segments):
            carry = adds[g - 1] + jnp.dot(steps[g - 1], carry, precision=lax.Precision.HIGHEST)
            start = jnp.where(segment == g, carry, start)
    states = (
        jnp.dot(
            before[:, :, :DK].reshape(heads * DK, DK), start, precision=lax.Precision.HIGH
        ).reshape(heads, DK, DV)
        + before[:, :, DK:]
    ).astype(BF16)
    back = lax.all_to_all(
        states, AXES, split_axis=0, concat_axis=0, axis_index_groups=groups, tiled=True
    )
    return back


def finish_kernel(
    place_ref, mix_ref, state_ref, gate_ref, gain_ref, residual_ref, post_ref, *refs
):
    *proj_refs, hidden_ref, first_ref, second_ref, core_ref = refs
    for h in range(GROUP_VALUE_HEADS):
        lanes = slice(h * DV, (h + 1) * DV)
        state = state_ref[h]
        recurrent = (
            dot(
                jnp.concatenate(halves(mix_ref[h, :, :DK]), axis=1),
                jnp.concatenate([state, state], axis=0),
            )
            + mix_ref[h, :, DK:]
        )
        inv_rms = lax.rsqrt(jnp.mean(recurrent * recurrent, axis=1, keepdims=True) + 1e-06)
        gate = gate_ref[:, lanes].astype(F32)
        act = gate / (1.0 + jnp.exp(-gate))
        core_ref[:, lanes] = (recurrent * inv_rms * gain_ref[...] * act).astype(BF16)
    core = core_ref[...]
    squares = 0.0
    for i, proj_ref in enumerate(proj_refs):
        wide = proj_ref.shape[1]
        lanes = pl.ds(pl.multiple_of(place_ref[i] * wide, wide), wide)
        hidden = (residual_ref[:, lanes].astype(F32) + dot(core, proj_ref[...])).astype(BF16)
        hidden_ref[:, lanes] = hidden
        widened = hidden.astype(F32)
        squares += jnp.sum(widened * widened, axis=1, keepdims=True)
    inv_rms = lax.rsqrt(squares * (1.0 / D) + 1e-06)
    normed = (hidden_ref[...].astype(F32) * inv_rms * post_ref[...]).astype(BF16)
    start = 0
    for ref, width in zip((first_ref, second_ref), GROUPS):
        ref[...] = normed[:, start : start + width]
        start += width


def finish(mix, states, out_gate, head_gain, proj, places, residual_in, post_gain):
    shape = residual_in.shape
    vmem = pl.BlockSpec(memory_space=pltpu.VMEM)
    return pl.pallas_call(
        finish_kernel,
        in_specs=[pl.BlockSpec(memory_space=pltpu.SMEM)] + [vmem] * (6 + len(proj)),
        out_shape=[
            jax.ShapeDtypeStruct((shape[0], wide), BF16) for wide in (D,) + GROUPS
        ],
        scratch_shapes=[pltpu.VMEM(shape, BF16)],
        compiler_params=pltpu.CompilerParams(vmem_limit_bytes=48 * MIB),
        name="finish",
    )(
        places,
        mix,
        states,
        out_gate,
        head_gain.reshape(1, DV),
        residual_in,
        post_gain.reshape(1, D),
        *proj,
    )


def hidden_units_kernel(
    capacity,
    pieces,
    slot_row_ref,
    slot_ref,
    weight_ref,
    own_gate_ref,
    own_up_ref,
    other_gate_ref,
    other_up_ref,
    *refs,
):
    *token_refs, inner_ref, spread_ref, block_ref, taken_ref, sems = refs
    group, expert = pl.program_id(0), pl.program_id(1)
    blocks, rows, _ = block_ref.shape
    served = taken_ref.shape[0]
    joined = max(1, 16 // capacity)

    def copies(step, b):
        found = []
        start = 0
        for part, width in enumerate(GROUPS):
            for ref, (column, places) in zip(token_refs, pieces):
                place = step * blocks + b
                if column == part and place in places:
                    found.append(
                        pltpu.make_async_copy(
                            ref.at[places.index(place)],
                            block_ref.at[b, :, start : start + width],
                            sems.at[b, part],
                        )
                    )
            start += width
        return found

    def load(step):
        @pl.when((expert == 0) & (group == step))
        def _():
            for b in range(blocks):
                for copy in copies(step, b):
                    copy.start()

    for step in range(sum(len(places) for column, places in pieces if column == 0) // blocks):
        load(step)

    @pl.when(expert == 0)
    def _():
        slot_ids = lax.broadcasted_iota(jnp.int32, (capacity, rows), 0).astype(F32)
        for first in range(0, blocks, joined):
            picked = []
            for b in range(first, first + joined):
                chosen = jnp.concatenate(
                    [(slot_row_ref[b, e : e + 1, :] == slot_ids).astype(F32) for e in range(served)],
                    axis=0,
                ).astype(BF16)
                for copy in copies(0, b):
                    copy.wait()
                picked.append(dot(chosen, block_ref[b]))
            for e in range(served):
                part = [p[e * capacity : (e + 1) * capacity] for p in picked]
                taken_ref[e, first * capacity : (first + joined) * capacity] = jnp.concatenate(
                    part, axis=0
                ).astype(BF16)

    def serve(gate_ref, up_ref):
        received = taken_ref[expert]
        gate = dot(received, gate_ref[0])
        up = dot(received, up_ref[0])
        inner_ref[0] = (gate / (1.0 + jnp.exp(-gate)) * up).astype(BF16)

    @pl.when(expert < served // 2)
    def _():
        serve(own_gate_ref, own_up_ref)

    @pl.when(expert >= served // 2)
    def _():
        serve(other_gate_ref, other_up_ref)

    span = served * capacity
    lane = lax.broadcasted_iota(jnp.int32, (rows, 2 * span), 1)
    lane_expert, lane_slot = lane // capacity % served, (lane % capacity).astype(F32)
    share = blocks // served
    for i in range(share):
        b = expert * share + i
        slots, weights = slot_ref[b], weight_ref[b]
        slot = jnp.full((rows, 2 * span), -1.0, F32)
        weight = jnp.zeros((rows, 2 * span), F32)
        for e in range(served):
            slot = jnp.where(lane_expert == e, slots[:, e : e + 1], slot)
            weight = jnp.where(lane_expert == e, weights[:, e : e + 1], weight)
        high = weight.astype(BF16).astype(F32)
        spread_ref[b] = jnp.where(
            slot == lane_slot, jnp.where(lane < span, high, weight - high), 0.0
        ).astype(BF16)


def hidden_units(tokens, slots, own, other, capacity):
    devices, served, rows = slots[0].shape
    local = own[0].shape[0]
    width = own[0].shape[2]
    pieces = [(column, places) for column, places, _ in tokens]
    def own_spec(x):
        return pl.BlockSpec((1,) + x.shape[1:], lambda g, e: (jnp.minimum(e, local - 1), 0, 0))

    def other_spec(x):
        return pl.BlockSpec((1,) + x.shape[1:], lambda g, e: (jnp.maximum(e - local, 0), 0, 0))

    column_spec = pl.BlockSpec((BLOCKS_STEP, rows, served), lambda g, e: (g, 0, 0))
    return pl.pallas_call(
        functools.partial(hidden_units_kernel, capacity, pieces),
        grid=(devices // BLOCKS_STEP, served),
        in_specs=[
            pl.BlockSpec((BLOCKS_STEP, served, rows), lambda g, e: (g, 0, 0)),
            column_spec,
            column_spec,
        ]
        + [own_spec(x) for x in own]
        + [other_spec(x) for x in other]
        + [pl.BlockSpec(memory_space=pl.ANY)] * len(tokens),
        out_specs=[
            pl.BlockSpec((1, BLOCKS_STEP * capacity, width), lambda g, e: (e, g, 0)),
            pl.BlockSpec((BLOCKS_STEP, rows, 2 * served * capacity), lambda g, e: (g, 0, 0)),
        ],
        out_shape=[
            jax.ShapeDtypeStruct((served, devices * capacity, width), BF16),
            jax.ShapeDtypeStruct((devices, rows, 2 * served * capacity), BF16),
        ],
        scratch_shapes=[
            pltpu.VMEM((BLOCKS_STEP, rows, D), BF16),
            pltpu.VMEM((served, BLOCKS_STEP * capacity, D), BF16),
            pltpu.SemaphoreType.DMA((BLOCKS_STEP, len(GROUPS))),
        ],
        compiler_params=pltpu.CompilerParams(vmem_limit_bytes=56 * MIB),
        name="hidden_units",
    )(
        *slots,
        *own,
        *other,
        *[array for _, _, array in tokens],
    )


def order_places(order):
    count = len(order)
    return [
        sum(((j >> (count - 1 - k)) & 1) << bit for k, bit in enumerate(order))
        for j in range(1 << count)
    ]


def down_kernel(capacity, order, inner_ref, spread_ref, own_ref, other_ref, *refs):
    *_, keep_ref, send_ref, out_ref = refs
    served = inner_ref.shape[0]
    local = served // 2
    for e in range(served):
        down = own_ref[e] if e < local else other_ref[e - local]
        out_ref[e] = dot(inner_ref[e], down)
    places = order_places(order)
    half = len(places) // 2
    for j, place in enumerate(places):
        mine = [out_ref[e, place * capacity : (place + 1) * capacity] for e in range(served)]
        stacked = jnp.concatenate(mine, axis=0).astype(BF16)
        block = dot(spread_ref[place], jnp.concatenate([stacked, stacked], axis=0)).astype(BF16)
        if j < half:
            keep_ref[j] = block
        else:
            send_ref[j - half] = block


def down_strips(inner, spread, own, other, capacity, order, start, width, before):
    served, slots, units = inner.shape
    devices, rows, _ = spread.shape
    first = start // STRIP

    def whole(x):
        return pl.BlockSpec(x.shape, lambda i: (0, 0, 0), pipeline_mode=pl.Buffered(1))

    down_spec = pl.BlockSpec((own.shape[0], units, STRIP), lambda i: (0, 0, first + i))
    half_spec = pl.BlockSpec((devices // 2, rows, STRIP), lambda i: (0, 0, i))
    half_shape = jax.ShapeDtypeStruct((devices // 2, rows, width), BF16)
    return pl.pallas_call(
        functools.partial(down_kernel, capacity, order),
        grid=(width // STRIP,),
        in_specs=[whole(inner), whole(spread), down_spec, down_spec]
        + [pl.BlockSpec(memory_space=pl.ANY)] * len(before),
        out_specs=[half_spec, half_spec],
        out_shape=[half_shape, half_shape],
        scratch_shapes=[pltpu.VMEM((served, slots, STRIP), F32)],
        compiler_params=pltpu.CompilerParams(vmem_limit_bytes=48 * MIB),
        name="down_strips",
    )(inner, spread, own, other, *before)


def sum_by_halving(keep, send, stages):
    for stage in stages[:-1]:
        total = (keep.astype(F32) + stage_flip(send, stage).astype(F32)).astype(BF16)
        half = total.shape[0] // 2
        keep, send = total[:half], total[half:]
    return keep[0].astype(F32) + stage_flip(send, stages[-1])[0].astype(F32)


def routing(expert_ids, gate_weights, local_experts):
    outer, cores, inner = (lax.axis_size(a) for a in (("outer", "mid"), "core", "inner"))
    rows = expert_ids.shape[0]
    experts = local_experts * outer * cores * inner
    chosen = expert_ids.T[None] == jnp.arange(experts, dtype=jnp.int32)[:, None, None]
    dense = jnp.sum(jnp.where(chosen, gate_weights.T[None], 0.0), axis=1)
    by_chip = jnp.swapaxes(dense.reshape(outer, cores, inner, local_experts * rows), 1, 2)
    by_chip = by_chip.reshape(outer * inner, cores * local_experts, rows)
    return lax.all_to_all(by_chip, SAME_CORE, split_axis=0, concat_axis=0, tiled=True)


def positions(weights, local_experts):
    rows = weights.shape[2]
    turned = jnp.concatenate([weights[:, local_experts:], weights[:, :local_experts]], axis=1)
    weights = jnp.where(lax.axis_index("core") == 1, turned, weights)
    bits = weights.shape[0].bit_length() - 1
    table = jnp.asarray([order_places(order[::-1]) for order in core_orders(bits)], jnp.int32)
    source = lax.axis_index(SAME_CORE) ^ table[lax.axis_index("core")]
    weights = jnp.take(weights, source, axis=0, mode="clip")
    named = weights > 0.0
    rank = jnp.einsum(
        "set,tu->seu",
        named.astype(BF16),
        jnp.triu(jnp.ones((rows, rows), BF16)),
        preferred_element_type=F32,
    )
    slots = jnp.where(named, rank - 1.0, -1.0)
    return slots, jnp.swapaxes(slots, 1, 2), jnp.swapaxes(weights, 1, 2)


def core_orders(bits):
    first = tuple(range(bits))[::-1]
    second = tuple(first[n ^ 1] if n ^ 1 < bits else first[n] for n in range(bits))
    return first, second


def flipped(array, bit):
    devices = lax.axis_size(AXES)
    return lax.ppermute(array, AXES, [(i, i ^ bit) for i in range(devices)])


def place_flip(array, bit):
    return flipped(array, 1 << (bit if 1 << bit < lax.axis_size("inner") else bit + 1))


def over_rest(array):
    pieces = [array]
    for bit in range(lax.axis_size(REST).bit_length() - 1):
        pieces = pieces + [place_flip(piece, bit) for piece in pieces]
    return pieces


def stage_flip(array, stage):
    inner, devices = lax.axis_size("inner"), lax.axis_size(AXES)
    bits = lax.axis_size(SAME_CORE).bit_length() - 1

    def partner(i):
        bit = core_orders(bits)[i // inner % 2][stage]
        return i ^ (1 << (bit if 1 << bit < inner else bit + 1))

    return lax.ppermute(array, AXES, [(i, partner(i)) for i in range(devices)])


def to_everyone(array, stages, plan):
    pieces = [((0,), array[None])]
    for step, stage in enumerate(stages):
        for chosen in plan[step] if step < len(plan) else [range(len(pieces))]:
            picked = [pieces[i] for i in chosen]
            places = sum((places for places, _ in picked), ())
            joined = jnp.concatenate([piece for _, piece in picked], axis=0)
            pieces.append(
                (tuple(place | (1 << stage) for place in places), stage_flip(joined, stage))
            )
    return pieces


def shards(
    split_core,
    residual_in,
    query_input,
    key_input,
    value_input,
    out_gate,
    write_strength,
    decay_rate,
    head_gain,
    out_proj,
    post_gain,
    expert_ids,
    gate_weights,
    expert_gate,
    expert_up,
    expert_down,
):
    tok_rows = residual_in.shape[0]
    devices = lax.axis_size(AXES)
    inner_size = lax.axis_size("inner")
    local_experts = expert_gate.shape[0]
    capacity = max(2, tok_rows * TOP * 8 // (5 * local_experts * devices))
    proj = lax.all_gather(out_proj, REST)
    served_weights = routing(expert_ids, gate_weights, local_experts)
    other_gate, other_up, other_down = (
        flipped(x, inner_size) for x in (expert_gate, expert_up, expert_down)
    )
    maps, mix = local_terms(query_input, key_input, value_input, write_strength, decay_rate)
    others = (other_gate, other_up, other_down)
    if split_core:
        core_own = flipped(out_proj, inner_size)
        others += (core_own,)
    states = entering_states(maps, devices, others)
    slots = positions(served_weights, local_experts)
    proj = after(proj, states)
    places = lax.axis_index(REST) ^ jnp.arange(proj.shape[0], dtype=jnp.int32)
    proj = [out_proj] + [
        lax.dynamic_index_in_dim(proj, places[q], keepdims=False) for q in range(1, proj.shape[0])
    ]
    if split_core:
        core = lax.axis_index("core")
        proj += [core_own] + [flipped(piece, inner_size) for piece in proj[1:]]
        base = places // inner_size * (2 * inner_size) + places % inner_size
        places = jnp.concatenate([base + core * inner_size, base + (1 - core) * inner_size])
    hidden, *normed = finish(
        mix, states, out_gate, head_gain, proj, places, residual_in, post_gain
    )
    bits = slots[0].shape[0].bit_length() - 1
    plain, turned = tuple(range(bits)), tuple((n + bits - 2) % bits for n in range(bits))
    plans = (
        [[(0,)], [(0, 1)], [(0, 1), (2,)], [(0, 1), (2,), (3,), (4,)]],
        [[(0,)], [(0, 1)], [(0, 1, 2)], [(0, 1, 2), (3,)]],
    )
    tokens = []
    for column, (part, stages, plan) in enumerate(zip(normed, (plain, turned), plans)):
        tokens += [(column, places, piece) for places, piece in to_everyone(part, stages, plan)]
    inner, spread = hidden_units(
        tokens, slots, (expert_gate, expert_up), (other_gate, other_up), capacity
    )
    sums, start, before = [], 0, ()
    for width, stages in ((512, turned), (512, plain), (512, plain), (512, plain)):
        keep, send = down_strips(
            inner, spread, expert_down, other_down, capacity, stages[::-1], start, width, before
        )
        before = before or (keep,)
        sums.append(sum_by_halving(keep, send, stages[::-1]))
        start += width
    return (hidden.astype(F32) + jnp.concatenate(sums, axis=1)).astype(BF16)


def core_stride(devices):
    first = getattr(devices[0], "coords", None)
    for i in range(1, len(devices)):
        if first is not None and tuple(devices[i].coords) == tuple(first):
            return i
    return 1


def solution(mesh):
    devices = mesh.devices.reshape(-1)
    inner = core_stride(devices)
    columns = mesh.shape["exp"]
    if 2 * inner <= columns:
        shape, column_axes = (-1, columns // (2 * inner), 2, inner), AXES[1:]
    else:
        shape, column_axes = (-1, 1, 2, inner), ("inner",)
    split_core = "core" in column_axes
    view = Mesh(devices.reshape(shape), AXES)
    rows = P(AXES, None)
    placed = (
        (rows,) * 7 + (P(), P(None, column_axes), P(), rows, rows) + (P(AXES, None, None),) * 3
    )
    body = functools.partial(shards, split_core)
    return jax.shard_map(body, mesh=view, in_specs=placed, out_specs=rows, check_vma=False)
```

```python
import functools

import jax
import jax.numpy as jnp
from jax import lax
from jax.experimental import pallas as pl
from jax.experimental.pallas import tpu as pltpu
from jax.sharding import Mesh, PartitionSpec as P

D = 2048
HK = 8
GROUP_VALUE_HEADS = 16
DK = 128
DV = 128
TOP = 10
HEADS_STEP = 4
BLOCKS_STEP = 16
GROUPS = (1536, 512)
STRIP = 256
EARLY_ROWS = 896

F32 = jnp.float32
BF16 = jnp.bfloat16
AXES = ("outer", "mid", "core", "inner")
SAME_CORE = ("outer", "mid", "inner")
REST = ("mid", "inner")
MIB = 1 << 20


def halves(x):
    high = x.astype(BF16)
    return high, (x - high.astype(F32)).astype(BF16)


def dot(a, b):
    return jnp.dot(a, b, preferred_element_type=F32)


def product(left, right):
    n = right[0].shape[1]
    lhs = jnp.concatenate(left, axis=1)
    top = jnp.concatenate(right, axis=1)
    bottom = jnp.concatenate([right[0], jnp.zeros_like(right[0])], axis=1)
    both = dot(lhs, jnp.concatenate([top, bottom], axis=0))
    return both[:, :n] + both[:, n:]


def local_kernel(q_ref, k_ref, v_ref, logs_ref, logs_row_ref, strength_row_ref, strength_ref, maps_ref, mix_ref):
    n = k_ref.shape[0]
    row = lax.broadcasted_iota(jnp.int32, (n, n), 0)
    column = lax.broadcasted_iota(jnp.int32, (n, n), 1)
    inclusive, strict, diagonal = row >= column, row > column, row == column
    heads = maps_ref.shape[0]
    group = GROUP_VALUE_HEADS // HK
    identity = diagonal.astype(F32)

    keys = []
    for i in range(heads // group):
        lanes = slice(i * DK, (i + 1) * DK)
        k_raw, q_raw = k_ref[:, lanes], q_ref[:, lanes]
        k_wide, q_wide = k_raw.astype(F32), q_raw.astype(F32)
        dims = (((1,), (1,)), ((), ()))
        gram = lax.dot_general(k_raw, k_raw, dims, preferred_element_type=F32)
        scores = lax.dot_general(q_raw, k_raw, dims, preferred_element_type=F32)
        inv_k = lax.rsqrt(jnp.sum(k_wide * k_wide, axis=1, keepdims=True) + 1e-06)
        inv_k_row = lax.rsqrt(jnp.sum(jnp.where(diagonal, gram, 0.0), axis=0, keepdims=True) + 1e-06)
        inv_q = lax.rsqrt(jnp.sum(q_wide * q_wide, axis=1, keepdims=True) + 1e-06) * DK ** (-0.5)
        keys.append(
            dict(
                k=k_raw,
                k_t=jnp.transpose(k_wide).astype(BF16),
                q=q_wide * inv_q,
                gram=gram * inv_k * inv_k_row,
                scores=scores * inv_q * inv_k_row,
                inv=inv_k,
                inv_row=inv_k_row,
            )
        )

    ratios, systems, inverses = [], [], []
    for j in range(heads):
        logs, logs_row = logs_ref[0][:, j : j + 1], logs_row_ref[0][j : j + 1, :]
        ratio = jnp.where(inclusive, jnp.exp(jnp.where(inclusive, logs - logs_row, 0.0)), 0.0)
        system = jnp.where(strict, ratio * keys[j // group]["gram"], 0.0) * strength_ref[0][:, j : j + 1]
        first = (row // 2 == column // 2) & strict
        ratios.append(ratio)
        systems.append(halves(system))
        inverses.append(identity - jnp.where(first, system, 0.0))
    size = 2
    while size < n:
        pairs = (row // (2 * size) == column // (2 * size)) & (row // size > column // size)
        inverse_halves = [halves(t) for t in inverses]
        cut = [
            tuple(jnp.where(pairs, part.astype(F32), 0.0).astype(BF16) for part in s) for s in systems
        ]
        left = [product(t, c) for t, c in zip(inverse_halves, cut)]
        inverses = [
            t - product(halves(x), th) for t, x, th in zip(inverses, left, inverse_halves)
        ]
        size *= 2

    for j in range(heads):
        key = keys[j // group]
        logs, logs_row = logs_ref[0][:, j : j + 1], logs_row_ref[0][j : j + 1, :]
        strength_row = strength_row_ref[0][j : j + 1, :]
        value = v_ref[:, j * DV : (j + 1) * DV]
        t = inverses[j]
        new_value = dot(
            jnp.concatenate(halves(t * strength_row), axis=1), jnp.concatenate([value, value], axis=0)
        )
        key_matrix = dot(
            jnp.concatenate(halves(t * (strength_row * jnp.exp(logs_row) * key["inv_row"])), axis=1),
            jnp.concatenate([key["k"], key["k"]], axis=0),
        )
        both = jnp.concatenate([key_matrix, new_value], axis=1)
        last = logs[n - 1 : n, :]
        faded = halves(both * (jnp.exp(last - logs) * key["inv"]))
        state = dot(
            jnp.concatenate([key["k_t"], key["k_t"]], axis=1), jnp.concatenate(faded, axis=0)
        )
        high, low = halves(jnp.exp(last) * identity - state[:, :DK])
        maps_ref[j, :, :DK] = high
        maps_ref[j, :, DK : 2 * DK] = low
        maps_ref[j, :, 2 * DK :] = state[:, DK:].astype(BF16)
        mixed = halves(ratios[j] * key["scores"])
        both_halves = halves(both)
        out = dot(
            jnp.concatenate(mixed, axis=1), jnp.concatenate([both_halves[0], both_halves[0]], axis=0)
        ) + dot(mixed[0], both_halves[1])
        mix_ref[j, :, :DK] = key["q"] * jnp.exp(logs) - out[:, :DK]
        mix_ref[j, :, DK:] = out[:, DK:]


def local_terms(query_input, key_input, value_input, write_strength, decay_rate):
    n = key_input.shape[0]
    groups, per_key = GROUP_VALUE_HEADS // HEADS_STEP, GROUP_VALUE_HEADS // HK
    lower = jnp.tril(jnp.ones((n, n), F32))
    logs = jnp.dot(lower, -decay_rate, precision=lax.Precision.HIGHEST)

    def columns(x):
        return jnp.swapaxes(x.reshape(n, groups, HEADS_STEP), 0, 1)

    def rows(x):
        return x.T.reshape(groups, HEADS_STEP, n)

    wide = HEADS_STEP // per_key * DK
    column_spec = pl.BlockSpec((1, n, HEADS_STEP), lambda i: (i, 0, 0))
    row_spec = pl.BlockSpec((1, HEADS_STEP, n), lambda i: (i, 0, 0))
    out_spec = pl.BlockSpec((HEADS_STEP, DK, 2 * DK + DV), lambda i: (i, 0, 0))
    mix_spec = pl.BlockSpec((HEADS_STEP, n, DK + DV), lambda i: (i, 0, 0))
    return pl.pallas_call(
        local_kernel,
        grid=(groups,),
        in_specs=[
            pl.BlockSpec((n, wide), lambda i: (0, i)),
            pl.BlockSpec((n, wide), lambda i: (0, i)),
            pl.BlockSpec((n, HEADS_STEP * DV), lambda i: (0, i)),
            column_spec,
            row_spec,
            row_spec,
            column_spec,
        ],
        out_specs=[out_spec, mix_spec],
        out_shape=[
            jax.ShapeDtypeStruct((GROUP_VALUE_HEADS, DK, 2 * DK + DV), BF16),
            jax.ShapeDtypeStruct((GROUP_VALUE_HEADS, n, DK + DV), F32),
        ],
        compiler_params=pltpu.CompilerParams(vmem_limit_bytes=40 * MIB),
        name="local_terms",
    )(
        query_input,
        key_input,
        value_input,
        columns(logs),
        rows(logs),
        rows(write_strength),
        columns(write_strength),
    )


def chain_kernel(maps_ref, *refs):
    *_, before_ref, whole_ref = refs
    row = lax.broadcasted_iota(jnp.int32, (DK, DK + DV), 0)
    column = lax.broadcasted_iota(jnp.int32, (DK, DK + DV), 1)
    passed = (row == column).astype(F32)
    for i in range(maps_ref.shape[0]):
        before_ref[i] = passed
        high, low = halves(passed)
        passed = dot(maps_ref[i, :, : 2 * DK], jnp.concatenate([high, high], axis=0)) + dot(
            maps_ref[i, :, :DK], low
        )
        passed = jnp.concatenate(
            [passed[:, :DK], passed[:, DK:] + maps_ref[i, :, 2 * DK :].astype(F32)], axis=1
        )
    whole_ref[...] = passed


def chain(maps, *others):
    count = maps.shape[0]
    return pl.pallas_call(
        chain_kernel,
        in_specs=[pl.BlockSpec(memory_space=pltpu.VMEM)]
        + [pl.BlockSpec(memory_space=pl.ANY)] * len(others),
        out_shape=[
            jax.ShapeDtypeStruct((count, DK, DK + DV), F32),
            jax.ShapeDtypeStruct((DK, DK + DV), F32),
        ],
        compiler_params=pltpu.CompilerParams(vmem_limit_bytes=40 * MIB),
        name="chain",
    )(maps, *others)


def tie_kernel(*refs):
    pass


def after(array, *others):
    anywhere = pl.BlockSpec(memory_space=pl.ANY)
    return pl.pallas_call(
        tie_kernel,
        in_specs=[anywhere] * (1 + len(others)),
        out_specs=anywhere,
        out_shape=jax.ShapeDtypeStruct(array.shape, array.dtype),
        input_output_aliases={0: 0},
        name="after",
    )(array, *others)


def entering_states(maps, devices, others, late):
    heads = maps.shape[0]
    segments = devices // heads
    groups = [[g * heads + h for h in range(heads)] for g in range(segments)]
    by_device = lax.all_to_all(
        maps, AXES, split_axis=0, concat_axis=0, axis_index_groups=groups, tiled=True
    )
    before, whole = chain(by_device, *others)
    if segments == 2:
        start = lax.ppermute(whole[:, DK:], AXES, [(h, heads + h) for h in range(heads)])
    else:
        across = [[g * heads + h for g in range(segments)] for h in range(heads)]
        adds = lax.all_gather(whole[:, DK:], AXES, axis_index_groups=across)
        steps = lax.all_gather(whole[:, :DK], AXES, axis_index_groups=across)
        segment = lax.axis_index(AXES) // heads
        carry = adds[0]
        start = jnp.where(segment == 1, carry, 0.0)
        for g in range(2, segments):
            carry = adds[g - 1] + jnp.dot(steps[g - 1], carry, precision=lax.Precision.HIGHEST)
            start = jnp.where(segment == g, carry, start)
    start = after(start, *late)
    states = (
        jnp.dot(
            before[:, :, :DK].reshape(heads * DK, DK), start, precision=lax.Precision.HIGH
        ).reshape(heads, DK, DV)
        + before[:, :, DK:]
    ).astype(BF16)
    back = lax.all_to_all(
        states, AXES, split_axis=0, concat_axis=0, axis_index_groups=groups, tiled=True
    )
    return back


def finish_kernel(
    parts, place_ref, mix_ref, state_ref, gate_ref, gain_ref, residual_ref, post_ref, *refs
):
    *proj_refs, hidden_ref, first_ref, second_ref, core_ref = refs
    for h in range(GROUP_VALUE_HEADS):
        lanes = slice(h * DV, (h + 1) * DV)
        state = state_ref[h]
        recurrent = (
            dot(
                jnp.concatenate(halves(mix_ref[h, :, :DK]), axis=1),
                jnp.concatenate([state, state], axis=0),
            )
            + mix_ref[h, :, DK:]
        )
        inv_rms = lax.rsqrt(jnp.mean(recurrent * recurrent, axis=1, keepdims=True) + 1e-06)
        gate = gate_ref[:, lanes].astype(F32)
        act = gate / (1.0 + jnp.exp(-gate))
        core_ref[:, lanes] = (recurrent * inv_rms * gain_ref[...] * act).astype(BF16)
    core = core_ref[...]
    squares = 0.0
    proj_refs = list(proj_refs)
    for i, count in enumerate(parts):
        refs, proj_refs = proj_refs[:count], proj_refs[count:]
        wide = refs[0].shape[1]
        lanes = pl.ds(pl.multiple_of(place_ref[i] * wide, wide), wide)
        mixed, first = residual_ref[:, lanes].astype(F32), 0
        for ref in refs:
            mixed += dot(core[:, first : first + ref.shape[0]], ref[...])
            first += ref.shape[0]
        hidden = mixed.astype(BF16)
        hidden_ref[:, lanes] = hidden
        widened = hidden.astype(F32)
        squares += jnp.sum(widened * widened, axis=1, keepdims=True)
    inv_rms = lax.rsqrt(squares * (1.0 / D) + 1e-06)
    normed = (hidden_ref[...].astype(F32) * inv_rms * post_ref[...]).astype(BF16)
    start = 0
    for ref, width in zip((first_ref, second_ref), GROUPS):
        ref[...] = normed[:, start : start + width]
        start += width


def finish(mix, states, out_gate, head_gain, proj, places, residual_in, post_gain):
    shape = residual_in.shape
    vmem = pl.BlockSpec(memory_space=pltpu.VMEM)
    flat = [part for piece in proj for part in piece]
    return pl.pallas_call(
        functools.partial(finish_kernel, [len(piece) for piece in proj]),
        in_specs=[pl.BlockSpec(memory_space=pltpu.SMEM)] + [vmem] * (6 + len(flat)),
        out_shape=[
            jax.ShapeDtypeStruct((shape[0], wide), BF16) for wide in (D,) + GROUPS
        ],
        scratch_shapes=[pltpu.VMEM(shape, BF16)],
        compiler_params=pltpu.CompilerParams(vmem_limit_bytes=48 * MIB),
        name="finish",
    )(
        places,
        mix,
        states,
        out_gate,
        head_gain.reshape(1, DV),
        residual_in,
        post_gain.reshape(1, D),
        *flat,
    )


def hidden_units_kernel(
    capacity,
    pieces,
    slot_row_ref,
    slot_ref,
    weight_ref,
    own_gate_ref,
    own_up_ref,
    other_gate_ref,
    other_up_ref,
    *refs,
):
    *token_refs, inner_ref, spread_ref, block_ref, taken_ref, sems = refs
    group, expert = pl.program_id(0), pl.program_id(1)
    blocks, rows, _ = block_ref.shape
    served = taken_ref.shape[0]
    joined = max(1, 16 // capacity)

    def copies(step, b):
        found = []
        start = 0
        for part, width in enumerate(GROUPS):
            for ref, (column, places) in zip(token_refs, pieces):
                place = step * blocks + b
                if column == part and place in places:
                    found.append(
                        pltpu.make_async_copy(
                            ref.at[places.index(place)],
                            block_ref.at[b, :, start : start + width],
                            sems.at[b, part],
                        )
                    )
            start += width
        return found

    def load(step):
        @pl.when((expert == 0) & (group == step))
        def _():
            for b in range(blocks):
                for copy in copies(step, b):
                    copy.start()

    for step in range(sum(len(places) for column, places in pieces if column == 0) // blocks):
        load(step)

    @pl.when(expert == 0)
    def _():
        slot_ids = lax.broadcasted_iota(jnp.int32, (capacity, rows), 0).astype(F32)
        for first in range(0, blocks, joined):
            picked = []
            for b in range(first, first + joined):
                chosen = jnp.concatenate(
                    [(slot_row_ref[b, e : e + 1, :] == slot_ids).astype(F32) for e in range(served)],
                    axis=0,
                ).astype(BF16)
                for copy in copies(0, b):
                    copy.wait()
                picked.append(dot(chosen, block_ref[b]))
            for e in range(served):
                part = [p[e * capacity : (e + 1) * capacity] for p in picked]
                taken_ref[e, first * capacity : (first + joined) * capacity] = jnp.concatenate(
                    part, axis=0
                ).astype(BF16)

    def serve(gate_ref, up_ref):
        received = taken_ref[expert]
        gate = dot(received, gate_ref[0])
        up = dot(received, up_ref[0])
        inner_ref[0] = (gate / (1.0 + jnp.exp(-gate)) * up).astype(BF16)

    @pl.when(expert < served // 2)
    def _():
        serve(own_gate_ref, own_up_ref)

    @pl.when(expert >= served // 2)
    def _():
        serve(other_gate_ref, other_up_ref)

    span = served * capacity
    lane = lax.broadcasted_iota(jnp.int32, (rows, 2 * span), 1)
    lane_expert, lane_slot = lane // capacity % served, (lane % capacity).astype(F32)
    share = blocks // served
    for i in range(share):
        b = expert * share + i
        slots, weights = slot_ref[b], weight_ref[b]
        slot = jnp.full((rows, 2 * span), -1.0, F32)
        weight = jnp.zeros((rows, 2 * span), F32)
        for e in range(served):
            slot = jnp.where(lane_expert == e, slots[:, e : e + 1], slot)
            weight = jnp.where(lane_expert == e, weights[:, e : e + 1], weight)
        high = weight.astype(BF16).astype(F32)
        spread_ref[b] = jnp.where(
            slot == lane_slot, jnp.where(lane < span, high, weight - high), 0.0
        ).astype(BF16)


def hidden_units(tokens, slots, own, other, capacity):
    devices, served, rows = slots[0].shape
    local = own[0].shape[0]
    width = own[0].shape[2]
    pieces = [(column, places) for column, places, _ in tokens]
    def own_spec(x):
        return pl.BlockSpec((1,) + x.shape[1:], lambda g, e: (jnp.minimum(e, local - 1), 0, 0))

    def other_spec(x):
        return pl.BlockSpec((1,) + x.shape[1:], lambda g, e: (jnp.maximum(e - local, 0), 0, 0))

    column_spec = pl.BlockSpec((BLOCKS_STEP, rows, served), lambda g, e: (g, 0, 0))
    return pl.pallas_call(
        functools.partial(hidden_units_kernel, capacity, pieces),
        grid=(devices // BLOCKS_STEP, served),
        in_specs=[
            pl.BlockSpec((BLOCKS_STEP, served, rows), lambda g, e: (g, 0, 0)),
            column_spec,
            column_spec,
        ]
        + [own_spec(x) for x in own]
        + [other_spec(x) for x in other]
        + [pl.BlockSpec(memory_space=pl.ANY)] * len(tokens),
        out_specs=[
            pl.BlockSpec((1, BLOCKS_STEP * capacity, width), lambda g, e: (e, g, 0)),
            pl.BlockSpec((BLOCKS_STEP, rows, 2 * served * capacity), lambda g, e: (g, 0, 0)),
        ],
        out_shape=[
            jax.ShapeDtypeStruct((served, devices * capacity, width), BF16),
            jax.ShapeDtypeStruct((devices, rows, 2 * served * capacity), BF16),
        ],
        scratch_shapes=[
            pltpu.VMEM((BLOCKS_STEP, rows, D), BF16),
            pltpu.VMEM((served, BLOCKS_STEP * capacity, D), BF16),
            pltpu.SemaphoreType.DMA((BLOCKS_STEP, len(GROUPS))),
        ],
        compiler_params=pltpu.CompilerParams(vmem_limit_bytes=56 * MIB),
        name="hidden_units",
    )(
        *slots,
        *own,
        *other,
        *[array for _, _, array in tokens],
    )


def order_places(order):
    count = len(order)
    return [
        sum(((j >> (count - 1 - k)) & 1) << bit for k, bit in enumerate(order))
        for j in range(1 << count)
    ]


def down_kernel(capacity, order, inner_ref, spread_ref, own_ref, other_ref, *refs):
    *_, keep_ref, send_ref, out_ref = refs
    served = inner_ref.shape[0]
    local = served // 2
    for e in range(served):
        down = own_ref[e] if e < local else other_ref[e - local]
        out_ref[e] = dot(inner_ref[e], down)
    places = order_places(order)
    half = len(places) // 2
    for j, place in enumerate(places):
        mine = [out_ref[e, place * capacity : (place + 1) * capacity] for e in range(served)]
        stacked = jnp.concatenate(mine, axis=0).astype(BF16)
        block = dot(spread_ref[place], jnp.concatenate([stacked, stacked], axis=0)).astype(BF16)
        if j < half:
            keep_ref[j] = block
        else:
            send_ref[j - half] = block


def down_strips(inner, spread, own, other, capacity, order, start, width, before):
    served, slots, units = inner.shape
    devices, rows, _ = spread.shape
    first = start // STRIP

    def whole(x):
        return pl.BlockSpec(x.shape, lambda i: (0, 0, 0), pipeline_mode=pl.Buffered(1))

    down_spec = pl.BlockSpec((own.shape[0], units, STRIP), lambda i: (0, 0, first + i))
    half_spec = pl.BlockSpec((devices // 2, rows, STRIP), lambda i: (0, 0, i))
    half_shape = jax.ShapeDtypeStruct((devices // 2, rows, width), BF16)
    return pl.pallas_call(
        functools.partial(down_kernel, capacity, order),
        grid=(width // STRIP,),
        in_specs=[whole(inner), whole(spread), down_spec, down_spec]
        + [pl.BlockSpec(memory_space=pl.ANY)] * len(before),
        out_specs=[half_spec, half_spec],
        out_shape=[half_shape, half_shape],
        scratch_shapes=[pltpu.VMEM((served, slots, STRIP), F32)],
        compiler_params=pltpu.CompilerParams(vmem_limit_bytes=48 * MIB),
        name="down_strips",
    )(inner, spread, own, other, *before)


def sum_by_halving(keep, send, stages):
    for stage in stages[:-1]:
        total = (keep.astype(F32) + stage_flip(send, stage).astype(F32)).astype(BF16)
        half = total.shape[0] // 2
        keep, send = total[:half], total[half:]
    return keep[0].astype(F32) + stage_flip(send, stages[-1])[0].astype(F32)


def routing(expert_ids, gate_weights, local_experts):
    outer, cores, inner = (lax.axis_size(a) for a in (("outer", "mid"), "core", "inner"))
    rows = expert_ids.shape[0]
    experts = local_experts * outer * cores * inner
    chosen = expert_ids.T[None] == jnp.arange(experts, dtype=jnp.int32)[:, None, None]
    dense = jnp.sum(jnp.where(chosen, gate_weights.T[None], 0.0), axis=1)
    by_chip = jnp.swapaxes(dense.reshape(outer, cores, inner, local_experts * rows), 1, 2)
    by_chip = by_chip.reshape(outer * inner, cores * local_experts, rows)
    return lax.all_to_all(by_chip, SAME_CORE, split_axis=0, concat_axis=0, tiled=True)


def positions(weights, local_experts):
    rows = weights.shape[2]
    turned = jnp.concatenate([weights[:, local_experts:], weights[:, :local_experts]], axis=1)
    weights = jnp.where(lax.axis_index("core") == 1, turned, weights)
    bits = weights.shape[0].bit_length() - 1
    table = jnp.asarray([order_places(order[::-1]) for order in core_orders(bits)], jnp.int32)
    source = lax.axis_index(SAME_CORE) ^ table[lax.axis_index("core")]
    weights = jnp.take(weights, source, axis=0, mode="clip")
    named = weights > 0.0
    rank = jnp.einsum(
        "set,tu->seu",
        named.astype(BF16),
        jnp.triu(jnp.ones((rows, rows), BF16)),
        preferred_element_type=F32,
    )
    slots = jnp.where(named, rank - 1.0, -1.0)
    return slots, jnp.swapaxes(slots, 1, 2), jnp.swapaxes(weights, 1, 2)


def core_orders(bits):
    first = tuple(range(bits))[::-1]
    second = tuple(first[n ^ 1] if n ^ 1 < bits else first[n] for n in range(bits))
    return first, second


def flipped(array, bit):
    devices = lax.axis_size(AXES)
    return lax.ppermute(array, AXES, [(i, i ^ bit) for i in range(devices)])


def place_flip(array, bit):
    return flipped(array, 1 << (bit if 1 << bit < lax.axis_size("inner") else bit + 1))


def over_rest(array):
    pieces = [array]
    for bit in range(lax.axis_size(REST).bit_length() - 1):
        pieces = pieces + [place_flip(piece, bit) for piece in pieces]
    return pieces


def stage_flip(array, stage):
    inner, devices = lax.axis_size("inner"), lax.axis_size(AXES)
    bits = lax.axis_size(SAME_CORE).bit_length() - 1

    def partner(i):
        bit = core_orders(bits)[i // inner % 2][stage]
        return i ^ (1 << (bit if 1 << bit < inner else bit + 1))

    return lax.ppermute(array, AXES, [(i, partner(i)) for i in range(devices)])


def send_on(pieces, chosen, stage):
    picked = [pieces[i] for i in chosen]
    places = sum((places for places, _ in picked), ())
    joined = jnp.concatenate([piece for _, piece in picked], axis=0)
    return tuple(place | (1 << stage) for place in places), stage_flip(joined, stage)


def to_everyone(array, stages, plan):
    pieces = [((0,), array[None])]
    for step, stage in enumerate(stages):
        chosen = plan[step] if step < len(plan) else [range(len(pieces))]
        pieces = pieces + [send_on(pieces, group, stage) for group in chosen]
    return pieces


def to_everyone_early(array, stages):
    pieces = [((0,), array[None])]
    pieces += [send_on(pieces, (0,), stage) for stage in (stages[0], stages[2], stages[3])]
    joined = jnp.concatenate([pieces[0][1], pieces[1][1]], axis=0)
    joined = after(joined, pieces[2][1], pieces[3][1])
    both = [(pieces[0][0] + pieces[1][0], joined)]
    pieces.append(send_on(both, (0,), stages[1]))
    pieces += [send_on(pieces, (i,), stages[2]) for i in (1, 4)]
    pieces += [send_on(pieces, group, stages[3]) for group in ((1,), (4,), (2, 5), (6,))]
    for stage in stages[4:]:
        pieces = pieces + [send_on(pieces, range(len(pieces)), stage)]
    return pieces


def shards(
    split_core,
    residual_in,
    query_input,
    key_input,
    value_input,
    out_gate,
    write_strength,
    decay_rate,
    head_gain,
    out_proj,
    post_gain,
    expert_ids,
    gate_weights,
    expert_gate,
    expert_up,
    expert_down,
):
    tok_rows = residual_in.shape[0]
    devices = lax.axis_size(AXES)
    inner_size = lax.axis_size("inner")
    local_experts = expert_gate.shape[0]
    capacity = max(2, tok_rows * TOP * 8 // (5 * local_experts * devices))
    early, late = (
        over_rest(part)[1:] for part in (out_proj[:EARLY_ROWS], out_proj[EARLY_ROWS:])
    )
    served_weights = routing(expert_ids, gate_weights, local_experts)
    other_gate, other_up, other_down = (
        flipped(x, inner_size) for x in (expert_gate, expert_up, expert_down)
    )
    maps, mix = local_terms(query_input, key_input, value_input, write_strength, decay_rate)
    maps = after(maps, *early)
    others = (other_gate, other_up, other_down)
    if split_core:
        core_early = [flipped(piece, inner_size) for piece in [out_proj] + early]
        others += tuple(core_early)
    states = entering_states(maps, devices, others, late)
    slots = positions(served_weights, local_experts)
    proj = [(out_proj,)] + list(zip(early, late))
    places = lax.axis_index(REST) ^ jnp.arange(len(proj), dtype=jnp.int32)
    if split_core:
        core = lax.axis_index("core")
        core_late = [flipped(piece, inner_size) for piece in late]
        proj += [(core_early[0],)] + list(zip(core_early[1:], core_late))
        base = places // inner_size * (2 * inner_size) + places % inner_size
        places = jnp.concatenate([base + core * inner_size, base + (1 - core) * inner_size])
    hidden, *normed = finish(
        mix, states, out_gate, head_gain, proj, places, residual_in, post_gain
    )
    bits = slots[0].shape[0].bit_length() - 1
    plain, turned = tuple(range(bits)), tuple((n + bits - 2) % bits for n in range(bits))
    plan = [[(0,)], [(0, 1)], [(0, 1, 2)], [(0, 1, 2), (3,)]]
    tokens = [(0, *piece) for piece in to_everyone_early(normed[0], plain)]
    tokens += [(1, *piece) for piece in to_everyone(normed[1], turned, plan)]
    inner, spread = hidden_units(
        tokens, slots, (expert_gate, expert_up), (other_gate, other_up), capacity
    )
    sums, start, before = [], 0, ()
    for width, stages in ((512, plain), (512, plain), (512, turned), (512, plain)):
        keep, send = down_strips(
            inner, spread, expert_down, other_down, capacity, stages[::-1], start, width, before
        )
        before = before or (keep,)
        sums.append(sum_by_halving(keep, send, stages[::-1]))
        start += width
    return (hidden.astype(F32) + jnp.concatenate(sums, axis=1)).astype(BF16)


def core_stride(devices):
    first = getattr(devices[0], "coords", None)
    for i in range(1, len(devices)):
        if first is not None and tuple(devices[i].coords) == tuple(first):
            return i
    return 1


def solution(mesh):
    devices = mesh.devices.reshape(-1)
    inner = core_stride(devices)
    columns = mesh.shape["exp"]
    if 2 * inner <= columns:
        shape, column_axes = (-1, columns // (2 * inner), 2, inner), AXES[1:]
    else:
        shape, column_axes = (-1, 1, 2, inner), ("inner",)
    split_core = "core" in column_axes
    view = Mesh(devices.reshape(shape), AXES)
    rows = P(AXES, None)
    placed = (
        (rows,) * 7 + (P(), P(None, column_axes), P(), rows, rows) + (P(AXES, None, None),) * 3
    )
    body = functools.partial(shards, split_core)
    return jax.shard_map(body, mesh=view, in_specs=placed, out_specs=rows, check_vma=False)
```

```python
import functools

import jax
import jax.numpy as jnp
from jax import lax
from jax.experimental import pallas as pl
from jax.experimental.pallas import tpu as pltpu
from jax.sharding import Mesh, PartitionSpec as P

D = 2048
HK = 8
GROUP_VALUE_HEADS = 16
DK = 128
DV = 128
TOP = 10
HEADS_STEP = 4
BLOCKS_STEP = 16
GROUPS = (1536, 512)
STRIP = 256
EARLY_ROWS = 768

F32 = jnp.float32
BF16 = jnp.bfloat16
AXES = ("outer", "mid", "core", "inner")
SAME_CORE = ("outer", "mid", "inner")
REST = ("mid", "inner")
MIB = 1 << 20


def halves(x):
    high = x.astype(BF16)
    return high, (x - high.astype(F32)).astype(BF16)


def dot(a, b):
    return jnp.dot(a, b, preferred_element_type=F32)


def product(left, right):
    n = right[0].shape[1]
    lhs = jnp.concatenate(left, axis=1)
    top = jnp.concatenate(right, axis=1)
    bottom = jnp.concatenate([right[0], jnp.zeros_like(right[0])], axis=1)
    both = dot(lhs, jnp.concatenate([top, bottom], axis=0))
    return both[:, :n] + both[:, n:]


def local_kernel(q_ref, k_ref, v_ref, logs_ref, logs_row_ref, strength_row_ref, strength_ref, maps_ref, mix_ref):
    n = k_ref.shape[0]
    row = lax.broadcasted_iota(jnp.int32, (n, n), 0)
    column = lax.broadcasted_iota(jnp.int32, (n, n), 1)
    inclusive, strict, diagonal = row >= column, row > column, row == column
    heads = maps_ref.shape[0]
    group = GROUP_VALUE_HEADS // HK
    identity = diagonal.astype(F32)

    keys = []
    for i in range(heads // group):
        lanes = slice(i * DK, (i + 1) * DK)
        k_raw, q_raw = k_ref[:, lanes], q_ref[:, lanes]
        k_wide, q_wide = k_raw.astype(F32), q_raw.astype(F32)
        dims = (((1,), (1,)), ((), ()))
        gram = lax.dot_general(k_raw, k_raw, dims, preferred_element_type=F32)
        scores = lax.dot_general(q_raw, k_raw, dims, preferred_element_type=F32)
        inv_k = lax.rsqrt(jnp.sum(k_wide * k_wide, axis=1, keepdims=True) + 1e-06)
        inv_k_row = lax.rsqrt(jnp.sum(jnp.where(diagonal, gram, 0.0), axis=0, keepdims=True) + 1e-06)
        inv_q = lax.rsqrt(jnp.sum(q_wide * q_wide, axis=1, keepdims=True) + 1e-06) * DK ** (-0.5)
        keys.append(
            dict(
                k=k_raw,
                k_t=jnp.transpose(k_wide).astype(BF16),
                q=q_wide * inv_q,
                gram=gram * inv_k * inv_k_row,
                scores=scores * inv_q * inv_k_row,
                inv=inv_k,
                inv_row=inv_k_row,
            )
        )

    ratios, systems, inverses = [], [], []
    for j in range(heads):
        logs, logs_row = logs_ref[0][:, j : j + 1], logs_row_ref[0][j : j + 1, :]
        ratio = jnp.where(inclusive, jnp.exp(jnp.where(inclusive, logs - logs_row, 0.0)), 0.0)
        system = jnp.where(strict, ratio * keys[j // group]["gram"], 0.0) * strength_ref[0][:, j : j + 1]
        first = (row // 2 == column // 2) & strict
        ratios.append(ratio)
        systems.append(halves(system))
        inverses.append(identity - jnp.where(first, system, 0.0))
    size = 2
    while size < n:
        pairs = (row // (2 * size) == column // (2 * size)) & (row // size > column // size)
        inverse_halves = [halves(t) for t in inverses]
        cut = [
            tuple(jnp.where(pairs, part.astype(F32), 0.0).astype(BF16) for part in s) for s in systems
        ]
        left = [product(t, c) for t, c in zip(inverse_halves, cut)]
        inverses = [
            t - product(halves(x), th) for t, x, th in zip(inverses, left, inverse_halves)
        ]
        size *= 2

    for j in range(heads):
        key = keys[j // group]
        logs, logs_row = logs_ref[0][:, j : j + 1], logs_row_ref[0][j : j + 1, :]
        strength_row = strength_row_ref[0][j : j + 1, :]
        value = v_ref[:, j * DV : (j + 1) * DV]
        t = inverses[j]
        new_value = dot(
            jnp.concatenate(halves(t * strength_row), axis=1), jnp.concatenate([value, value], axis=0)
        )
        key_matrix = dot(
            jnp.concatenate(halves(t * (strength_row * jnp.exp(logs_row) * key["inv_row"])), axis=1),
            jnp.concatenate([key["k"], key["k"]], axis=0),
        )
        both = jnp.concatenate([key_matrix, new_value], axis=1)
        last = logs[n - 1 : n, :]
        faded = halves(both * (jnp.exp(last - logs) * key["inv"]))
        state = dot(
            jnp.concatenate([key["k_t"], key["k_t"]], axis=1), jnp.concatenate(faded, axis=0)
        )
        high, low = halves(jnp.exp(last) * identity - state[:, :DK])
        maps_ref[j, :, :DK] = high
        maps_ref[j, :, DK : 2 * DK] = low
        maps_ref[j, :, 2 * DK :] = state[:, DK:].astype(BF16)
        mixed = halves(ratios[j] * key["scores"])
        both_halves = halves(both)
        out = dot(
            jnp.concatenate(mixed, axis=1), jnp.concatenate([both_halves[0], both_halves[0]], axis=0)
        ) + dot(mixed[0], both_halves[1])
        mix_ref[j, :, :DK] = key["q"] * jnp.exp(logs) - out[:, :DK]
        mix_ref[j, :, DK:] = out[:, DK:]


def local_terms(query_input, key_input, value_input, write_strength, decay_rate):
    n = key_input.shape[0]
    groups, per_key = GROUP_VALUE_HEADS // HEADS_STEP, GROUP_VALUE_HEADS // HK
    lower = jnp.tril(jnp.ones((n, n), F32))
    logs = jnp.dot(lower, -decay_rate, precision=lax.Precision.HIGHEST)

    def columns(x):
        return jnp.swapaxes(x.reshape(n, groups, HEADS_STEP), 0, 1)

    def rows(x):
        return x.T.reshape(groups, HEADS_STEP, n)

    wide = HEADS_STEP // per_key * DK
    column_spec = pl.BlockSpec((1, n, HEADS_STEP), lambda i: (i, 0, 0))
    row_spec = pl.BlockSpec((1, HEADS_STEP, n), lambda i: (i, 0, 0))
    out_spec = pl.BlockSpec((HEADS_STEP, DK, 2 * DK + DV), lambda i: (i, 0, 0))
    mix_spec = pl.BlockSpec((HEADS_STEP, n, DK + DV), lambda i: (i, 0, 0))
    return pl.pallas_call(
        local_kernel,
        grid=(groups,),
        in_specs=[
            pl.BlockSpec((n, wide), lambda i: (0, i)),
            pl.BlockSpec((n, wide), lambda i: (0, i)),
            pl.BlockSpec((n, HEADS_STEP * DV), lambda i: (0, i)),
            column_spec,
            row_spec,
            row_spec,
            column_spec,
        ],
        out_specs=[out_spec, mix_spec],
        out_shape=[
            jax.ShapeDtypeStruct((GROUP_VALUE_HEADS, DK, 2 * DK + DV), BF16),
            jax.ShapeDtypeStruct((GROUP_VALUE_HEADS, n, DK + DV), F32),
        ],
        compiler_params=pltpu.CompilerParams(vmem_limit_bytes=40 * MIB),
        name="local_terms",
    )(
        query_input,
        key_input,
        value_input,
        columns(logs),
        rows(logs),
        rows(write_strength),
        columns(write_strength),
    )


def chain_kernel(maps_ref, *refs):
    *_, before_ref, whole_ref = refs
    row = lax.broadcasted_iota(jnp.int32, (DK, DK + DV), 0)
    column = lax.broadcasted_iota(jnp.int32, (DK, DK + DV), 1)
    passed = (row == column).astype(F32)
    for i in range(maps_ref.shape[0]):
        before_ref[i] = passed
        high, low = halves(passed)
        passed = dot(maps_ref[i, :, : 2 * DK], jnp.concatenate([high, high], axis=0)) + dot(
            maps_ref[i, :, :DK], low
        )
        passed = jnp.concatenate(
            [passed[:, :DK], passed[:, DK:] + maps_ref[i, :, 2 * DK :].astype(F32)], axis=1
        )
    whole_ref[...] = passed


def chain(maps, *others):
    count = maps.shape[0]
    return pl.pallas_call(
        chain_kernel,
        in_specs=[pl.BlockSpec(memory_space=pltpu.VMEM)]
        + [pl.BlockSpec(memory_space=pl.ANY)] * len(others),
        out_shape=[
            jax.ShapeDtypeStruct((count, DK, DK + DV), F32),
            jax.ShapeDtypeStruct((DK, DK + DV), F32),
        ],
        compiler_params=pltpu.CompilerParams(vmem_limit_bytes=40 * MIB),
        name="chain",
    )(maps, *others)


def tie_kernel(*refs):
    pass


def after(array, *others):
    anywhere = pl.BlockSpec(memory_space=pl.ANY)
    return pl.pallas_call(
        tie_kernel,
        in_specs=[anywhere] * (1 + len(others)),
        out_specs=anywhere,
        out_shape=jax.ShapeDtypeStruct(array.shape, array.dtype),
        input_output_aliases={0: 0},
        name="after",
    )(array, *others)


def entering_states(maps, devices, others, late, route):
    heads = maps.shape[0]
    segments = devices // heads
    groups = [[g * heads + h for h in range(heads)] for g in range(segments)]
    by_device = lax.all_to_all(
        maps, AXES, split_axis=0, concat_axis=0, axis_index_groups=groups, tiled=True
    )
    before, whole = chain(by_device, *others)
    if segments == 2:
        start = lax.ppermute(whole[:, DK:], AXES, [(h, heads + h) for h in range(heads)])
    else:
        across = [[g * heads + h for g in range(segments)] for h in range(heads)]
        adds = lax.all_gather(whole[:, DK:], AXES, axis_index_groups=across)
        steps = lax.all_gather(whole[:, :DK], AXES, axis_index_groups=across)
        segment = lax.axis_index(AXES) // heads
        carry = adds[0]
        start = jnp.where(segment == 1, carry, 0.0)
        for g in range(2, segments):
            carry = adds[g - 1] + jnp.dot(steps[g - 1], carry, precision=lax.Precision.HIGHEST)
            start = jnp.where(segment == g, carry, start)
    served = route(whole)
    start = after(start, *late, served)
    states = (
        jnp.dot(
            before[:, :, :DK].reshape(heads * DK, DK), start, precision=lax.Precision.HIGH
        ).reshape(heads, DK, DV)
        + before[:, :, DK:]
    ).astype(BF16)
    back = lax.all_to_all(
        states, AXES, split_axis=0, concat_axis=0, axis_index_groups=groups, tiled=True
    )
    return back, served


def finish_kernel(
    parts, place_ref, mix_ref, state_ref, gate_ref, gain_ref, residual_ref, post_ref, *refs
):
    *proj_refs, hidden_ref, first_ref, second_ref, core_ref = refs
    for h in range(GROUP_VALUE_HEADS):
        lanes = slice(h * DV, (h + 1) * DV)
        state = state_ref[h]
        recurrent = (
            dot(
                jnp.concatenate(halves(mix_ref[h, :, :DK]), axis=1),
                jnp.concatenate([state, state], axis=0),
            )
            + mix_ref[h, :, DK:]
        )
        inv_rms = lax.rsqrt(jnp.mean(recurrent * recurrent, axis=1, keepdims=True) + 1e-06)
        gate = gate_ref[:, lanes].astype(F32)
        act = gate / (1.0 + jnp.exp(-gate))
        core_ref[:, lanes] = (recurrent * inv_rms * gain_ref[...] * act).astype(BF16)
    core = core_ref[...]
    squares = 0.0
    proj_refs = list(proj_refs)
    for i, count in enumerate(parts):
        refs, proj_refs = proj_refs[:count], proj_refs[count:]
        wide = refs[0].shape[1]
        lanes = pl.ds(pl.multiple_of(place_ref[i] * wide, wide), wide)
        mixed, first = residual_ref[:, lanes].astype(F32), 0
        for ref in refs:
            mixed += dot(core[:, first : first + ref.shape[0]], ref[...])
            first += ref.shape[0]
        hidden = mixed.astype(BF16)
        hidden_ref[:, lanes] = hidden
        widened = hidden.astype(F32)
        squares += jnp.sum(widened * widened, axis=1, keepdims=True)
    inv_rms = lax.rsqrt(squares * (1.0 / D) + 1e-06)
    normed = (hidden_ref[...].astype(F32) * inv_rms * post_ref[...]).astype(BF16)
    start = 0
    for ref, width in zip((first_ref, second_ref), GROUPS):
        ref[...] = normed[:, start : start + width]
        start += width


def finish(mix, states, out_gate, head_gain, proj, places, residual_in, post_gain):
    shape = residual_in.shape
    vmem = pl.BlockSpec(memory_space=pltpu.VMEM)
    flat = [part for piece in proj for part in piece]
    return pl.pallas_call(
        functools.partial(finish_kernel, [len(piece) for piece in proj]),
        in_specs=[pl.BlockSpec(memory_space=pltpu.SMEM)] + [vmem] * (6 + len(flat)),
        out_shape=[
            jax.ShapeDtypeStruct((shape[0], wide), BF16) for wide in (D,) + GROUPS
        ],
        scratch_shapes=[pltpu.VMEM(shape, BF16)],
        compiler_params=pltpu.CompilerParams(vmem_limit_bytes=48 * MIB),
        name="finish",
    )(
        places,
        mix,
        states,
        out_gate,
        head_gain.reshape(1, DV),
        residual_in,
        post_gain.reshape(1, D),
        *flat,
    )


def hidden_units_kernel(
    capacity,
    pieces,
    slot_row_ref,
    slot_ref,
    weight_ref,
    own_gate_ref,
    own_up_ref,
    other_gate_ref,
    other_up_ref,
    *refs,
):
    *token_refs, inner_ref, spread_ref, block_ref, taken_ref, sems = refs
    group, expert = pl.program_id(0), pl.program_id(1)
    blocks, rows, _ = block_ref.shape
    served = taken_ref.shape[0]
    joined = max(1, 16 // capacity)

    def copies(step, b):
        found = []
        start = 0
        for part, width in enumerate(GROUPS):
            for ref, (column, places) in zip(token_refs, pieces):
                place = step * blocks + b
                if column == part and place in places:
                    found.append(
                        pltpu.make_async_copy(
                            ref.at[places.index(place)],
                            block_ref.at[b, :, start : start + width],
                            sems.at[b, part],
                        )
                    )
            start += width
        return found

    def load(step):
        @pl.when((expert == 0) & (group == step))
        def _():
            for b in range(blocks):
                for copy in copies(step, b):
                    copy.start()

    for step in range(sum(len(places) for column, places in pieces if column == 0) // blocks):
        load(step)

    @pl.when(expert == 0)
    def _():
        slot_ids = lax.broadcasted_iota(jnp.int32, (capacity, rows), 0).astype(F32)
        for first in range(0, blocks, joined):
            picked = []
            for b in range(first, first + joined):
                chosen = jnp.concatenate(
                    [(slot_row_ref[b, e : e + 1, :] == slot_ids).astype(F32) for e in range(served)],
                    axis=0,
                ).astype(BF16)
                for copy in copies(0, b):
                    copy.wait()
                picked.append(dot(chosen, block_ref[b]))
            for e in range(served):
                part = [p[e * capacity : (e + 1) * capacity] for p in picked]
                taken_ref[e, first * capacity : (first + joined) * capacity] = jnp.concatenate(
                    part, axis=0
                ).astype(BF16)

    def serve(gate_ref, up_ref):
        received = taken_ref[expert]
        gate = dot(received, gate_ref[0])
        up = dot(received, up_ref[0])
        inner_ref[0] = (gate / (1.0 + jnp.exp(-gate)) * up).astype(BF16)

    @pl.when(expert < served // 2)
    def _():
        serve(own_gate_ref, own_up_ref)

    @pl.when(expert >= served // 2)
    def _():
        serve(other_gate_ref, other_up_ref)

    span = served * capacity
    lane = lax.broadcasted_iota(jnp.int32, (rows, 2 * span), 1)
    lane_expert, lane_slot = lane // capacity % served, (lane % capacity).astype(F32)
    share = blocks // served
    for i in range(share):
        b = expert * share + i
        slots, weights = slot_ref[b], weight_ref[b]
        slot = jnp.full((rows, 2 * span), -1.0, F32)
        weight = jnp.zeros((rows, 2 * span), F32)
        for e in range(served):
            slot = jnp.where(lane_expert == e, slots[:, e : e + 1], slot)
            weight = jnp.where(lane_expert == e, weights[:, e : e + 1], weight)
        high = weight.astype(BF16).astype(F32)
        spread_ref[b] = jnp.where(
            slot == lane_slot, jnp.where(lane < span, high, weight - high), 0.0
        ).astype(BF16)


def hidden_units(tokens, slots, own, other, capacity):
    devices, served, rows = slots[0].shape
    local = own[0].shape[0]
    width = own[0].shape[2]
    pieces = [(column, places) for column, places, _ in tokens]
    def own_spec(x):
        return pl.BlockSpec((1,) + x.shape[1:], lambda g, e: (jnp.minimum(e, local - 1), 0, 0))

    def other_spec(x):
        return pl.BlockSpec((1,) + x.shape[1:], lambda g, e: (jnp.maximum(e - local, 0), 0, 0))

    column_spec = pl.BlockSpec((BLOCKS_STEP, rows, served), lambda g, e: (g, 0, 0))
    return pl.pallas_call(
        functools.partial(hidden_units_kernel, capacity, pieces),
        grid=(devices // BLOCKS_STEP, served),
        in_specs=[
            pl.BlockSpec((BLOCKS_STEP, served, rows), lambda g, e: (g, 0, 0)),
            column_spec,
            column_spec,
        ]
        + [own_spec(x) for x in own]
        + [other_spec(x) for x in other]
        + [pl.BlockSpec(memory_space=pl.ANY)] * len(tokens),
        out_specs=[
            pl.BlockSpec((1, BLOCKS_STEP * capacity, width), lambda g, e: (e, g, 0)),
            pl.BlockSpec((BLOCKS_STEP, rows, 2 * served * capacity), lambda g, e: (g, 0, 0)),
        ],
        out_shape=[
            jax.ShapeDtypeStruct((served, devices * capacity, width), BF16),
            jax.ShapeDtypeStruct((devices, rows, 2 * served * capacity), BF16),
        ],
        scratch_shapes=[
            pltpu.VMEM((BLOCKS_STEP, rows, D), BF16),
            pltpu.VMEM((served, BLOCKS_STEP * capacity, D), BF16),
            pltpu.SemaphoreType.DMA((BLOCKS_STEP, len(GROUPS))),
        ],
        compiler_params=pltpu.CompilerParams(vmem_limit_bytes=56 * MIB),
        name="hidden_units",
    )(
        *slots,
        *own,
        *other,
        *[array for _, _, array in tokens],
    )


def order_places(order):
    count = len(order)
    return [
        sum(((j >> (count - 1 - k)) & 1) << bit for k, bit in enumerate(order))
        for j in range(1 << count)
    ]


def down_kernel(capacity, order, inner_ref, spread_ref, own_ref, other_ref, *refs):
    *_, keep_ref, send_ref, out_ref = refs
    served = inner_ref.shape[0]
    local = served // 2
    for e in range(served):
        down = own_ref[e] if e < local else other_ref[e - local]
        out_ref[e] = dot(inner_ref[e], down)
    places = order_places(order)
    half = len(places) // 2
    for j, place in enumerate(places):
        mine = [out_ref[e, place * capacity : (place + 1) * capacity] for e in range(served)]
        stacked = jnp.concatenate(mine, axis=0).astype(BF16)
        block = dot(spread_ref[place], jnp.concatenate([stacked, stacked], axis=0)).astype(BF16)
        if j < half:
            keep_ref[j] = block
        else:
            send_ref[j - half] = block


def down_strips(inner, spread, own, other, capacity, order, start, width, before):
    served, slots, units = inner.shape
    devices, rows, _ = spread.shape
    first = start // STRIP

    def whole(x):
        return pl.BlockSpec(x.shape, lambda i: (0, 0, 0), pipeline_mode=pl.Buffered(1))

    down_spec = pl.BlockSpec((own.shape[0], units, STRIP), lambda i: (0, 0, first + i))
    half_spec = pl.BlockSpec((devices // 2, rows, STRIP), lambda i: (0, 0, i))
    half_shape = jax.ShapeDtypeStruct((devices // 2, rows, width), BF16)
    return pl.pallas_call(
        functools.partial(down_kernel, capacity, order),
        grid=(width // STRIP,),
        in_specs=[whole(inner), whole(spread), down_spec, down_spec]
        + [pl.BlockSpec(memory_space=pl.ANY)] * len(before),
        out_specs=[half_spec, half_spec],
        out_shape=[half_shape, half_shape],
        scratch_shapes=[pltpu.VMEM((served, slots, STRIP), F32)],
        compiler_params=pltpu.CompilerParams(vmem_limit_bytes=48 * MIB),
        name="down_strips",
    )(inner, spread, own, other, *before)


def sum_by_halving(keep, send, stages):
    for stage in stages[:-1]:
        total = (keep.astype(F32) + stage_flip(send, stage).astype(F32)).astype(BF16)
        half = total.shape[0] // 2
        keep, send = total[:half], total[half:]
    return keep[0].astype(F32) + stage_flip(send, stages[-1])[0].astype(F32)


def routing(expert_ids, gate_weights, local_experts):
    outer, cores, inner = (lax.axis_size(a) for a in (("outer", "mid"), "core", "inner"))
    rows = expert_ids.shape[0]
    experts = local_experts * outer * cores * inner
    chosen = expert_ids.T[None] == jnp.arange(experts, dtype=jnp.int32)[:, None, None]
    dense = jnp.sum(jnp.where(chosen, gate_weights.T[None], 0.0), axis=1)
    by_chip = jnp.swapaxes(dense.reshape(outer, cores, inner, local_experts * rows), 1, 2)
    by_chip = by_chip.reshape(outer * inner, cores * local_experts, rows)
    return lax.all_to_all(by_chip, SAME_CORE, split_axis=0, concat_axis=0, tiled=True)


def positions(weights, local_experts):
    rows = weights.shape[2]
    turned = jnp.concatenate([weights[:, local_experts:], weights[:, :local_experts]], axis=1)
    weights = jnp.where(lax.axis_index("core") == 1, turned, weights)
    bits = weights.shape[0].bit_length() - 1
    table = jnp.asarray([order_places(order[::-1]) for order in core_orders(bits)], jnp.int32)
    source = lax.axis_index(SAME_CORE) ^ table[lax.axis_index("core")]
    weights = jnp.take(weights, source, axis=0, mode="clip")
    named = weights > 0.0
    rank = jnp.einsum(
        "set,tu->seu",
        named.astype(BF16),
        jnp.triu(jnp.ones((rows, rows), BF16)),
        preferred_element_type=F32,
    )
    slots = jnp.where(named, rank - 1.0, -1.0)
    return slots, jnp.swapaxes(slots, 1, 2), jnp.swapaxes(weights, 1, 2)


def core_orders(bits):
    first = tuple(range(bits))[::-1]
    second = tuple(first[n ^ 1] if n ^ 1 < bits else first[n] for n in range(bits))
    return first, second


def flipped(array, bit):
    devices = lax.axis_size(AXES)
    return lax.ppermute(array, AXES, [(i, i ^ bit) for i in range(devices)])


def place_flip(array, bit):
    return flipped(array, 1 << (bit if 1 << bit < lax.axis_size("inner") else bit + 1))


def over_rest(array):
    pieces = [array]
    for bit in range(lax.axis_size(REST).bit_length() - 1):
        pieces = pieces + [place_flip(piece, bit) for piece in pieces]
    return pieces


def stage_flip(array, stage):
    inner, devices = lax.axis_size("inner"), lax.axis_size(AXES)
    bits = lax.axis_size(SAME_CORE).bit_length() - 1

    def partner(i):
        bit = core_orders(bits)[i // inner % 2][stage]
        return i ^ (1 << (bit if 1 << bit < inner else bit + 1))

    return lax.ppermute(array, AXES, [(i, partner(i)) for i in range(devices)])


def send_on(pieces, chosen, stage):
    picked = [pieces[i] for i in chosen]
    places = sum((places for places, _ in picked), ())
    joined = jnp.concatenate([piece for _, piece in picked], axis=0)
    return tuple(place | (1 << stage) for place in places), stage_flip(joined, stage)


def to_everyone(array, stages, plan):
    pieces = [((0,), array[None])]
    for step, stage in enumerate(stages):
        chosen = plan[step] if step < len(plan) else [range(len(pieces))]
        pieces = pieces + [send_on(pieces, group, stage) for group in chosen]
    return pieces


def to_everyone_early(array, stages, others):
    pieces = [((0,), array[None])]
    pieces += [send_on(pieces, (0,), stage) for stage in (stages[0], stages[2], stages[3])]
    joined = jnp.concatenate([pieces[0][1], pieces[1][1]], axis=0)
    joined = after(joined, pieces[2][1], pieces[3][1], *others)
    both = [(pieces[0][0] + pieces[1][0], joined)]
    pieces.append(send_on(both, (0,), stages[1]))
    pieces += [send_on(pieces, (i,), stages[2]) for i in (1, 4)]
    pieces += [send_on(pieces, group, stages[3]) for group in ((1,), (4,), (2, 5), (6,))]
    for stage in stages[4:]:
        pieces = pieces + [send_on(pieces, range(len(pieces)), stage)]
    return pieces


def shards(
    split_core,
    residual_in,
    query_input,
    key_input,
    value_input,
    out_gate,
    write_strength,
    decay_rate,
    head_gain,
    out_proj,
    post_gain,
    expert_ids,
    gate_weights,
    expert_gate,
    expert_up,
    expert_down,
):
    tok_rows = residual_in.shape[0]
    devices = lax.axis_size(AXES)
    inner_size = lax.axis_size("inner")
    local_experts = expert_gate.shape[0]
    capacity = max(2, tok_rows * TOP * 8 // (5 * local_experts * devices))
    late_rows = out_proj[EARLY_ROWS:]
    early = over_rest(out_proj[:EARLY_ROWS])[1:]
    other_gate, other_up, other_down = (
        flipped(x, inner_size) for x in (expert_gate, expert_up, expert_down)
    )
    maps, mix = local_terms(query_input, key_input, value_input, write_strength, decay_rate)
    ready = [*early, late_rows, other_gate, other_up, other_down]
    others = []
    if split_core:
        core_own = flipped(out_proj, inner_size)
        core_early = [flipped(piece, inner_size) for piece in early]
        ready, others = ready + [core_own], core_early
    maps = after(maps, *ready)
    late = over_rest(after(late_rows, maps))[1:]

    def route(whole):
        return routing(after(expert_ids, whole), gate_weights, local_experts)

    states, served_weights = entering_states(maps, devices, others, late, route)
    slots = positions(served_weights, local_experts)
    proj = [(out_proj,)] + list(zip(early, late))
    places = lax.axis_index(REST) ^ jnp.arange(len(proj), dtype=jnp.int32)
    if split_core:
        core = lax.axis_index("core")
        core_late = [flipped(after(piece, served_weights), inner_size) for piece in late]
        proj += [(core_own,)] + list(zip(core_early, core_late))
        base = places // inner_size * (2 * inner_size) + places % inner_size
        places = jnp.concatenate([base + core * inner_size, base + (1 - core) * inner_size])
    hidden, *normed = finish(
        mix, states, out_gate, head_gain, proj, places, residual_in, post_gain
    )
    bits = slots[0].shape[0].bit_length() - 1
    plain, turned = tuple(range(bits)), tuple((n + bits - 2) % bits for n in range(bits))
    plan = [[(0,)], [(0, 1)], [(0, 1, 2)], [(0, 1, 2), (3,)]]
    second = to_everyone(normed[1], turned, plan)
    first = to_everyone_early(normed[0], plain, [second[2][1]])
    tokens = [(0, *piece) for piece in first] + [(1, *piece) for piece in second]
    inner, spread = hidden_units(
        tokens, slots, (expert_gate, expert_up), (other_gate, other_up), capacity
    )
    sums, start, before = [], 0, ()
    for width, stages in ((512, plain), (512, plain), (512, turned), (512, plain)):
        keep, send = down_strips(
            inner, spread, expert_down, other_down, capacity, stages[::-1], start, width, before
        )
        before = before or (keep,)
        sums.append(sum_by_halving(keep, send, stages[::-1]))
        start += width
    return (hidden.astype(F32) + jnp.concatenate(sums, axis=1)).astype(BF16)


def core_stride(devices):
    first = getattr(devices[0], "coords", None)
    for i in range(1, len(devices)):
        if first is not None and tuple(devices[i].coords) == tuple(first):
            return i
    return 1


def solution(mesh):
    devices = mesh.devices.reshape(-1)
    inner = core_stride(devices)
    columns = mesh.shape["exp"]
    if 2 * inner <= columns:
        shape, column_axes = (-1, columns // (2 * inner), 2, inner), AXES[1:]
    else:
        shape, column_axes = (-1, 1, 2, inner), ("inner",)
    split_core = "core" in column_axes
    view = Mesh(devices.reshape(shape), AXES)
    rows = P(AXES, None)
    placed = (
        (rows,) * 7 + (P(), P(None, column_axes), P(), rows, rows) + (P(AXES, None, None),) * 3
    )
    body = functools.partial(shards, split_core)
    return jax.shard_map(body, mesh=view, in_specs=placed, out_specs=rows, check_vma=False)
```

```python
import functools

import jax
import jax.numpy as jnp
from jax import lax
from jax.experimental import pallas as pl
from jax.experimental.pallas import tpu as pltpu
from jax.sharding import Mesh, PartitionSpec as P

D = 2048
HK = 8
GROUP_VALUE_HEADS = 16
DK = 128
DV = 128
TOP = 10
HEADS_STEP = 4
BLOCKS_STEP = 16
GROUPS = (1536, 512)
STRIP = 256
EARLY_ROWS = 768

F32 = jnp.float32
BF16 = jnp.bfloat16
AXES = ("outer", "mid", "core", "inner")
SAME_CORE = ("outer", "mid", "inner")
REST = ("mid", "inner")
MIB = 1 << 20


def halves(x):
    high = x.astype(BF16)
    return high, (x - high.astype(F32)).astype(BF16)


def dot(a, b):
    return jnp.dot(a, b, preferred_element_type=F32)


def product(left, right):
    n = right[0].shape[1]
    lhs = jnp.concatenate(left, axis=1)
    top = jnp.concatenate(right, axis=1)
    bottom = jnp.concatenate([right[0], jnp.zeros_like(right[0])], axis=1)
    both = dot(lhs, jnp.concatenate([top, bottom], axis=0))
    return both[:, :n] + both[:, n:]


def local_kernel(q_ref, k_ref, v_ref, logs_ref, logs_row_ref, strength_row_ref, strength_ref, maps_ref, mix_ref):
    n = k_ref.shape[0]
    row = lax.broadcasted_iota(jnp.int32, (n, n), 0)
    column = lax.broadcasted_iota(jnp.int32, (n, n), 1)
    inclusive, strict, diagonal = row >= column, row > column, row == column
    heads = maps_ref.shape[0]
    group = GROUP_VALUE_HEADS // HK
    identity = diagonal.astype(F32)

    keys = []
    for i in range(heads // group):
        lanes = slice(i * DK, (i + 1) * DK)
        k_raw, q_raw = k_ref[:, lanes], q_ref[:, lanes]
        k_wide, q_wide = k_raw.astype(F32), q_raw.astype(F32)
        dims = (((1,), (1,)), ((), ()))
        gram = lax.dot_general(k_raw, k_raw, dims, preferred_element_type=F32)
        scores = lax.dot_general(q_raw, k_raw, dims, preferred_element_type=F32)
        inv_k = lax.rsqrt(jnp.sum(k_wide * k_wide, axis=1, keepdims=True) + 1e-06)
        inv_k_row = lax.rsqrt(jnp.sum(jnp.where(diagonal, gram, 0.0), axis=0, keepdims=True) + 1e-06)
        inv_q = lax.rsqrt(jnp.sum(q_wide * q_wide, axis=1, keepdims=True) + 1e-06) * DK ** (-0.5)
        keys.append(
            dict(
                k=k_raw,
                k_t=jnp.transpose(k_wide).astype(BF16),
                q=q_wide * inv_q,
                gram=gram * inv_k * inv_k_row,
                scores=scores * inv_q * inv_k_row,
                inv=inv_k,
                inv_row=inv_k_row,
            )
        )

    ratios, systems, inverses = [], [], []
    for j in range(heads):
        logs, logs_row = logs_ref[0][:, j : j + 1], logs_row_ref[0][j : j + 1, :]
        ratio = jnp.where(inclusive, jnp.exp(jnp.where(inclusive, logs - logs_row, 0.0)), 0.0)
        system = jnp.where(strict, ratio * keys[j // group]["gram"], 0.0) * strength_ref[0][:, j : j + 1]
        first = (row // 2 == column // 2) & strict
        ratios.append(ratio)
        systems.append(halves(system))
        inverses.append(identity - jnp.where(first, system, 0.0))
    size = 2
    while size < n:
        pairs = (row // (2 * size) == column // (2 * size)) & (row // size > column // size)
        inverse_halves = [halves(t) for t in inverses]
        cut = [
            tuple(jnp.where(pairs, part.astype(F32), 0.0).astype(BF16) for part in s) for s in systems
        ]
        left = [product(t, c) for t, c in zip(inverse_halves, cut)]
        inverses = [
            t - product(halves(x), th) for t, x, th in zip(inverses, left, inverse_halves)
        ]
        size *= 2

    for j in range(heads):
        key = keys[j // group]
        logs, logs_row = logs_ref[0][:, j : j + 1], logs_row_ref[0][j : j + 1, :]
        strength_row = strength_row_ref[0][j : j + 1, :]
        value = v_ref[:, j * DV : (j + 1) * DV]
        t = inverses[j]
        new_value = dot(
            jnp.concatenate(halves(t * strength_row), axis=1), jnp.concatenate([value, value], axis=0)
        )
        key_matrix = dot(
            jnp.concatenate(halves(t * (strength_row * jnp.exp(logs_row) * key["inv_row"])), axis=1),
            jnp.concatenate([key["k"], key["k"]], axis=0),
        )
        both = jnp.concatenate([key_matrix, new_value], axis=1)
        last = logs[n - 1 : n, :]
        faded = halves(both * (jnp.exp(last - logs) * key["inv"]))
        state = dot(
            jnp.concatenate([key["k_t"], key["k_t"]], axis=1), jnp.concatenate(faded, axis=0)
        )
        high, low = halves(jnp.exp(last) * identity - state[:, :DK])
        maps_ref[j, :, :DK] = high
        maps_ref[j, :, DK : 2 * DK] = low
        maps_ref[j, :, 2 * DK :] = state[:, DK:].astype(BF16)
        mixed = halves(ratios[j] * key["scores"])
        both_halves = halves(both)
        out = dot(
            jnp.concatenate(mixed, axis=1), jnp.concatenate([both_halves[0], both_halves[0]], axis=0)
        ) + dot(mixed[0], both_halves[1])
        mix_ref[j, :, :DK] = key["q"] * jnp.exp(logs) - out[:, :DK]
        mix_ref[j, :, DK:] = out[:, DK:]


def local_terms(query_input, key_input, value_input, write_strength, decay_rate):
    n = key_input.shape[0]
    groups, per_key = GROUP_VALUE_HEADS // HEADS_STEP, GROUP_VALUE_HEADS // HK
    lower = jnp.tril(jnp.ones((n, n), F32))
    logs = jnp.dot(lower, -decay_rate, precision=lax.Precision.HIGHEST)

    def columns(x):
        return jnp.swapaxes(x.reshape(n, groups, HEADS_STEP), 0, 1)

    def rows(x):
        return x.T.reshape(groups, HEADS_STEP, n)

    wide = HEADS_STEP // per_key * DK
    column_spec = pl.BlockSpec((1, n, HEADS_STEP), lambda i: (i, 0, 0))
    row_spec = pl.BlockSpec((1, HEADS_STEP, n), lambda i: (i, 0, 0))
    out_spec = pl.BlockSpec((HEADS_STEP, DK, 2 * DK + DV), lambda i: (i, 0, 0))
    mix_spec = pl.BlockSpec((HEADS_STEP, n, DK + DV), lambda i: (i, 0, 0))
    return pl.pallas_call(
        local_kernel,
        grid=(groups,),
        in_specs=[
            pl.BlockSpec((n, wide), lambda i: (0, i)),
            pl.BlockSpec((n, wide), lambda i: (0, i)),
            pl.BlockSpec((n, HEADS_STEP * DV), lambda i: (0, i)),
            column_spec,
            row_spec,
            row_spec,
            column_spec,
        ],
        out_specs=[out_spec, mix_spec],
        out_shape=[
            jax.ShapeDtypeStruct((GROUP_VALUE_HEADS, DK, 2 * DK + DV), BF16),
            jax.ShapeDtypeStruct((GROUP_VALUE_HEADS, n, DK + DV), F32),
        ],
        compiler_params=pltpu.CompilerParams(vmem_limit_bytes=40 * MIB),
        name="local_terms",
    )(
        query_input,
        key_input,
        value_input,
        columns(logs),
        rows(logs),
        rows(write_strength),
        columns(write_strength),
    )


def chain_kernel(maps_ref, *refs):
    *_, before_ref, whole_ref = refs
    row = lax.broadcasted_iota(jnp.int32, (DK, DK + DV), 0)
    column = lax.broadcasted_iota(jnp.int32, (DK, DK + DV), 1)
    passed = (row == column).astype(F32)
    for i in range(maps_ref.shape[0]):
        before_ref[i] = passed
        high, low = halves(passed)
        passed = dot(maps_ref[i, :, : 2 * DK], jnp.concatenate([high, high], axis=0)) + dot(
            maps_ref[i, :, :DK], low
        )
        passed = jnp.concatenate(
            [passed[:, :DK], passed[:, DK:] + maps_ref[i, :, 2 * DK :].astype(F32)], axis=1
        )
    whole_ref[...] = passed


def chain(maps, *others):
    count = maps.shape[0]
    return pl.pallas_call(
        chain_kernel,
        in_specs=[pl.BlockSpec(memory_space=pltpu.VMEM)]
        + [pl.BlockSpec(memory_space=pl.ANY)] * len(others),
        out_shape=[
            jax.ShapeDtypeStruct((count, DK, DK + DV), F32),
            jax.ShapeDtypeStruct((DK, DK + DV), F32),
        ],
        compiler_params=pltpu.CompilerParams(vmem_limit_bytes=40 * MIB),
        name="chain",
    )(maps, *others)


def tie_kernel(*refs):
    pass


def after(array, *others):
    anywhere = pl.BlockSpec(memory_space=pl.ANY)
    return pl.pallas_call(
        tie_kernel,
        in_specs=[anywhere] * (1 + len(others)),
        out_specs=anywhere,
        out_shape=jax.ShapeDtypeStruct(array.shape, array.dtype),
        input_output_aliases={0: 0},
        name="after",
    )(array, *others)


def entering_states(maps, devices, others, route):
    heads = maps.shape[0]
    segments = devices // heads
    groups = [[g * heads + h for h in range(heads)] for g in range(segments)]
    by_device = lax.all_to_all(
        maps, AXES, split_axis=0, concat_axis=0, axis_index_groups=groups, tiled=True
    )
    before, whole = chain(by_device, *others)
    if segments == 2:
        start = lax.ppermute(whole[:, DK:], AXES, [(h, heads + h) for h in range(heads)])
    else:
        across = [[g * heads + h for g in range(segments)] for h in range(heads)]
        adds = lax.all_gather(whole[:, DK:], AXES, axis_index_groups=across)
        steps = lax.all_gather(whole[:, :DK], AXES, axis_index_groups=across)
        segment = lax.axis_index(AXES) // heads
        carry = adds[0]
        start = jnp.where(segment == 1, carry, 0.0)
        for g in range(2, segments):
            carry = adds[g - 1] + jnp.dot(steps[g - 1], carry, precision=lax.Precision.HIGHEST)
            start = jnp.where(segment == g, carry, start)
    states = (
        jnp.dot(
            before[:, :, :DK].reshape(heads * DK, DK), start, precision=lax.Precision.HIGH
        ).reshape(heads, DK, DV)
        + before[:, :, DK:]
    ).astype(BF16)
    back = lax.all_to_all(
        states, AXES, split_axis=0, concat_axis=0, axis_index_groups=groups, tiled=True
    )
    return back, route(states)


def finish_kernel(
    parts, place_ref, mix_ref, state_ref, gate_ref, gain_ref, residual_ref, post_ref, *refs
):
    *proj_refs, hidden_ref, first_ref, second_ref, core_ref = refs
    for h in range(GROUP_VALUE_HEADS):
        lanes = slice(h * DV, (h + 1) * DV)
        state = state_ref[h]
        recurrent = (
            dot(
                jnp.concatenate(halves(mix_ref[h, :, :DK]), axis=1),
                jnp.concatenate([state, state], axis=0),
            )
            + mix_ref[h, :, DK:]
        )
        inv_rms = lax.rsqrt(jnp.mean(recurrent * recurrent, axis=1, keepdims=True) + 1e-06)
        gate = gate_ref[:, lanes].astype(F32)
        act = gate / (1.0 + jnp.exp(-gate))
        core_ref[:, lanes] = (recurrent * inv_rms * gain_ref[...] * act).astype(BF16)
    core = core_ref[...]
    squares = 0.0
    proj_refs = list(proj_refs)
    for i, count in enumerate(parts):
        refs, proj_refs = proj_refs[:count], proj_refs[count:]
        wide = refs[0].shape[1]
        lanes = pl.ds(pl.multiple_of(place_ref[i] * wide, wide), wide)
        mixed, first = residual_ref[:, lanes].astype(F32), 0
        for ref in refs:
            mixed += dot(core[:, first : first + ref.shape[0]], ref[...])
            first += ref.shape[0]
        hidden = mixed.astype(BF16)
        hidden_ref[:, lanes] = hidden
        widened = hidden.astype(F32)
        squares += jnp.sum(widened * widened, axis=1, keepdims=True)
    inv_rms = lax.rsqrt(squares * (1.0 / D) + 1e-06)
    normed = (hidden_ref[...].astype(F32) * inv_rms * post_ref[...]).astype(BF16)
    start = 0
    for ref, width in zip((first_ref, second_ref), GROUPS):
        ref[...] = normed[:, start : start + width]
        start += width


def finish(mix, states, out_gate, head_gain, proj, places, residual_in, post_gain):
    shape = residual_in.shape
    vmem = pl.BlockSpec(memory_space=pltpu.VMEM)
    flat = [part for piece in proj for part in piece]
    return pl.pallas_call(
        functools.partial(finish_kernel, [len(piece) for piece in proj]),
        in_specs=[pl.BlockSpec(memory_space=pltpu.SMEM)] + [vmem] * (6 + len(flat)),
        out_shape=[
            jax.ShapeDtypeStruct((shape[0], wide), BF16) for wide in (D,) + GROUPS
        ],
        scratch_shapes=[pltpu.VMEM(shape, BF16)],
        compiler_params=pltpu.CompilerParams(vmem_limit_bytes=48 * MIB),
        name="finish",
    )(
        places,
        mix,
        states,
        out_gate,
        head_gain.reshape(1, DV),
        residual_in,
        post_gain.reshape(1, D),
        *flat,
    )


def hidden_units_kernel(
    capacity,
    pieces,
    slot_row_ref,
    slot_ref,
    weight_ref,
    own_gate_ref,
    own_up_ref,
    other_gate_ref,
    other_up_ref,
    *refs,
):
    *token_refs, inner_ref, spread_ref, block_ref, taken_ref, sems = refs
    group, expert = pl.program_id(0), pl.program_id(1)
    blocks, rows, _ = block_ref.shape
    served = taken_ref.shape[0]
    joined = max(1, 16 // capacity)

    def copies(step, b):
        found = []
        start = 0
        for part, width in enumerate(GROUPS):
            for ref, (column, places) in zip(token_refs, pieces):
                place = step * blocks + b
                if column == part and place in places:
                    found.append(
                        pltpu.make_async_copy(
                            ref.at[places.index(place)],
                            block_ref.at[b, :, start : start + width],
                            sems.at[b, part],
                        )
                    )
            start += width
        return found

    def load(step):
        @pl.when((expert == 0) & (group == step))
        def _():
            for b in range(blocks):
                for copy in copies(step, b):
                    copy.start()

    for step in range(sum(len(places) for column, places in pieces if column == 0) // blocks):
        load(step)

    @pl.when(expert == 0)
    def _():
        slot_ids = lax.broadcasted_iota(jnp.int32, (capacity, rows), 0).astype(F32)
        for first in range(0, blocks, joined):
            picked = []
            for b in range(first, first + joined):
                chosen = jnp.concatenate(
                    [(slot_row_ref[b, e : e + 1, :] == slot_ids).astype(F32) for e in range(served)],
                    axis=0,
                ).astype(BF16)
                for copy in copies(0, b):
                    copy.wait()
                picked.append(dot(chosen, block_ref[b]))
            for e in range(served):
                part = [p[e * capacity : (e + 1) * capacity] for p in picked]
                taken_ref[e, first * capacity : (first + joined) * capacity] = jnp.concatenate(
                    part, axis=0
                ).astype(BF16)

    def serve(gate_ref, up_ref):
        received = taken_ref[expert]
        gate = dot(received, gate_ref[0])
        up = dot(received, up_ref[0])
        inner_ref[0] = (gate / (1.0 + jnp.exp(-gate)) * up).astype(BF16)

    @pl.when(expert < served // 2)
    def _():
        serve(own_gate_ref, own_up_ref)

    @pl.when(expert >= served // 2)
    def _():
        serve(other_gate_ref, other_up_ref)

    span = served * capacity
    lane = lax.broadcasted_iota(jnp.int32, (rows, 2 * span), 1)
    lane_expert, lane_slot = lane // capacity % served, (lane % capacity).astype(F32)
    share = blocks // served
    for i in range(share):
        b = expert * share + i
        slots, weights = slot_ref[b], weight_ref[b]
        slot = jnp.full((rows, 2 * span), -1.0, F32)
        weight = jnp.zeros((rows, 2 * span), F32)
        for e in range(served):
            slot = jnp.where(lane_expert == e, slots[:, e : e + 1], slot)
            weight = jnp.where(lane_expert == e, weights[:, e : e + 1], weight)
        high = weight.astype(BF16).astype(F32)
        spread_ref[b] = jnp.where(
            slot == lane_slot, jnp.where(lane < span, high, weight - high), 0.0
        ).astype(BF16)


def hidden_units(tokens, slots, own, other, capacity):
    devices, served, rows = slots[0].shape
    local = own[0].shape[0]
    width = own[0].shape[2]
    pieces = [(column, places) for column, places, _ in tokens]
    def own_spec(x):
        return pl.BlockSpec((1,) + x.shape[1:], lambda g, e: (jnp.minimum(e, local - 1), 0, 0))

    def other_spec(x):
        return pl.BlockSpec((1,) + x.shape[1:], lambda g, e: (jnp.maximum(e - local, 0), 0, 0))

    column_spec = pl.BlockSpec((BLOCKS_STEP, rows, served), lambda g, e: (g, 0, 0))
    return pl.pallas_call(
        functools.partial(hidden_units_kernel, capacity, pieces),
        grid=(devices // BLOCKS_STEP, served),
        in_specs=[
            pl.BlockSpec((BLOCKS_STEP, served, rows), lambda g, e: (g, 0, 0)),
            column_spec,
            column_spec,
        ]
        + [own_spec(x) for x in own]
        + [other_spec(x) for x in other]
        + [pl.BlockSpec(memory_space=pl.ANY)] * len(tokens),
        out_specs=[
            pl.BlockSpec((1, BLOCKS_STEP * capacity, width), lambda g, e: (e, g, 0)),
            pl.BlockSpec((BLOCKS_STEP, rows, 2 * served * capacity), lambda g, e: (g, 0, 0)),
        ],
        out_shape=[
            jax.ShapeDtypeStruct((served, devices * capacity, width), BF16),
            jax.ShapeDtypeStruct((devices, rows, 2 * served * capacity), BF16),
        ],
        scratch_shapes=[
            pltpu.VMEM((BLOCKS_STEP, rows, D), BF16),
            pltpu.VMEM((served, BLOCKS_STEP * capacity, D), BF16),
            pltpu.SemaphoreType.DMA((BLOCKS_STEP, len(GROUPS))),
        ],
        compiler_params=pltpu.CompilerParams(vmem_limit_bytes=56 * MIB),
        name="hidden_units",
    )(
        *slots,
        *own,
        *other,
        *[array for _, _, array in tokens],
    )


def order_places(order):
    count = len(order)
    return [
        sum(((j >> (count - 1 - k)) & 1) << bit for k, bit in enumerate(order))
        for j in range(1 << count)
    ]


def down_kernel(capacity, order, inner_ref, spread_ref, own_ref, other_ref, *refs):
    *_, keep_ref, send_ref, out_ref = refs
    served = inner_ref.shape[0]
    local = served // 2
    for e in range(served):
        down = own_ref[e] if e < local else other_ref[e - local]
        out_ref[e] = dot(inner_ref[e], down)
    places = order_places(order)
    half = len(places) // 2
    for j, place in enumerate(places):
        mine = [out_ref[e, place * capacity : (place + 1) * capacity] for e in range(served)]
        stacked = jnp.concatenate(mine, axis=0).astype(BF16)
        block = dot(spread_ref[place], jnp.concatenate([stacked, stacked], axis=0)).astype(BF16)
        if j < half:
            keep_ref[j] = block
        else:
            send_ref[j - half] = block


def down_strips(inner, spread, own, other, capacity, order, start, width, before):
    served, slots, units = inner.shape
    devices, rows, _ = spread.shape
    first = start // STRIP

    def whole(x):
        return pl.BlockSpec(x.shape, lambda i: (0, 0, 0), pipeline_mode=pl.Buffered(1))

    down_spec = pl.BlockSpec((own.shape[0], units, STRIP), lambda i: (0, 0, first + i))
    half_spec = pl.BlockSpec((devices // 2, rows, STRIP), lambda i: (0, 0, i))
    half_shape = jax.ShapeDtypeStruct((devices // 2, rows, width), BF16)
    return pl.pallas_call(
        functools.partial(down_kernel, capacity, order),
        grid=(width // STRIP,),
        in_specs=[whole(inner), whole(spread), down_spec, down_spec]
        + [pl.BlockSpec(memory_space=pl.ANY)] * len(before),
        out_specs=[half_spec, half_spec],
        out_shape=[half_shape, half_shape],
        scratch_shapes=[pltpu.VMEM((served, slots, STRIP), F32)],
        compiler_params=pltpu.CompilerParams(vmem_limit_bytes=48 * MIB),
        name="down_strips",
    )(inner, spread, own, other, *before)


def sum_by_halving(keep, send, stages):
    for stage in stages[:-1]:
        total = (keep.astype(F32) + stage_flip(send, stage).astype(F32)).astype(BF16)
        half = total.shape[0] // 2
        keep, send = total[:half], total[half:]
    return keep[0].astype(F32) + stage_flip(send, stages[-1])[0].astype(F32)


def routing(expert_ids, gate_weights, local_experts):
    outer, cores, inner = (lax.axis_size(a) for a in (("outer", "mid"), "core", "inner"))
    rows = expert_ids.shape[0]
    experts = local_experts * outer * cores * inner
    chosen = expert_ids.T[None] == jnp.arange(experts, dtype=jnp.int32)[:, None, None]
    dense = jnp.sum(jnp.where(chosen, gate_weights.T[None], 0.0), axis=1)
    by_chip = jnp.swapaxes(dense.reshape(outer, cores, inner, local_experts * rows), 1, 2)
    by_chip = by_chip.reshape(outer * inner, cores * local_experts, rows)
    return lax.all_to_all(by_chip, SAME_CORE, split_axis=0, concat_axis=0, tiled=True)


def positions(weights, local_experts):
    rows = weights.shape[2]
    turned = jnp.concatenate([weights[:, local_experts:], weights[:, :local_experts]], axis=1)
    weights = jnp.where(lax.axis_index("core") == 1, turned, weights)
    bits = weights.shape[0].bit_length() - 1
    table = jnp.asarray([order_places(order[::-1]) for order in core_orders(bits)], jnp.int32)
    source = lax.axis_index(SAME_CORE) ^ table[lax.axis_index("core")]
    weights = jnp.take(weights, source, axis=0, mode="clip")
    named = weights > 0.0
    rank = jnp.einsum(
        "set,tu->seu",
        named.astype(BF16),
        jnp.triu(jnp.ones((rows, rows), BF16)),
        preferred_element_type=F32,
    )
    slots = jnp.where(named, rank - 1.0, -1.0)
    return slots, jnp.swapaxes(slots, 1, 2), jnp.swapaxes(weights, 1, 2)


def core_orders(bits):
    first = tuple(range(bits))[::-1]
    second = tuple(first[n ^ 1] if n ^ 1 < bits else first[n] for n in range(bits))
    return first, second


def flipped(array, bit):
    devices = lax.axis_size(AXES)
    return lax.ppermute(array, AXES, [(i, i ^ bit) for i in range(devices)])


def place_flip(array, bit):
    return flipped(array, 1 << (bit if 1 << bit < lax.axis_size("inner") else bit + 1))


def over_rest(array):
    pieces = [array]
    for bit in range(lax.axis_size(REST).bit_length() - 1):
        pieces = pieces + [place_flip(piece, bit) for piece in pieces]
    return pieces


def stage_flip(array, stage):
    inner, devices = lax.axis_size("inner"), lax.axis_size(AXES)
    bits = lax.axis_size(SAME_CORE).bit_length() - 1

    def partner(i):
        bit = core_orders(bits)[i // inner % 2][stage]
        return i ^ (1 << (bit if 1 << bit < inner else bit + 1))

    return lax.ppermute(array, AXES, [(i, partner(i)) for i in range(devices)])


def send_on(pieces, chosen, stage):
    picked = [pieces[i] for i in chosen]
    places = sum((places for places, _ in picked), ())
    joined = jnp.concatenate([piece for _, piece in picked], axis=0)
    return tuple(place | (1 << stage) for place in places), stage_flip(joined, stage)


def to_everyone(array, stages, plan):
    pieces = [((0,), array[None])]
    for step, stage in enumerate(stages):
        chosen = plan[step] if step < len(plan) else [range(len(pieces))]
        pieces = pieces + [send_on(pieces, group, stage) for group in chosen]
    return pieces


def to_everyone_early(array, stages, others):
    pieces = [((0,), array[None])]
    pieces += [send_on(pieces, (0,), stage) for stage in (stages[0], stages[2], stages[3])]
    joined = jnp.concatenate([pieces[0][1], pieces[1][1]], axis=0)
    joined = after(joined, pieces[2][1], pieces[3][1], *others)
    both = [(pieces[0][0] + pieces[1][0], joined)]
    pieces.append(send_on(both, (0,), stages[1]))
    pieces += [send_on(pieces, (i,), stages[2]) for i in (1, 4)]
    pieces += [send_on(pieces, group, stages[3]) for group in ((1,), (4,), (2, 5), (6,))]
    for stage in stages[4:]:
        pieces = pieces + [send_on(pieces, range(len(pieces)), stage)]
    return pieces


def shards(
    split_core,
    residual_in,
    query_input,
    key_input,
    value_input,
    out_gate,
    write_strength,
    decay_rate,
    head_gain,
    out_proj,
    post_gain,
    expert_ids,
    gate_weights,
    expert_gate,
    expert_up,
    expert_down,
):
    tok_rows = residual_in.shape[0]
    devices = lax.axis_size(AXES)
    inner_size = lax.axis_size("inner")
    local_experts = expert_gate.shape[0]
    capacity = max(2, tok_rows * TOP * 8 // (5 * local_experts * devices))
    late_rows = out_proj[EARLY_ROWS:]
    early = over_rest(out_proj[:EARLY_ROWS])[1:]
    other_gate, other_up, other_down = (
        flipped(x, inner_size) for x in (expert_gate, expert_up, expert_down)
    )
    maps, mix = local_terms(query_input, key_input, value_input, write_strength, decay_rate)
    ready = [*early, late_rows, other_gate, other_up, other_down]
    others = []
    if split_core:
        core_own = flipped(out_proj, inner_size)
        core_early = [flipped(piece, inner_size) for piece in early]
        ready, others = ready + [core_own], core_early
    maps = after(maps, *ready)
    late = over_rest(after(late_rows, maps))[1:]

    def route(leaving):
        return routing(after(expert_ids, leaving), gate_weights, local_experts)

    states, served_weights = entering_states(maps, devices, others, route)
    slots = positions(served_weights, local_experts)
    proj = [(out_proj,)] + list(zip(early, late))
    places = lax.axis_index(REST) ^ jnp.arange(len(proj), dtype=jnp.int32)
    if split_core:
        core = lax.axis_index("core")
        core_late = [flipped(after(piece, states, served_weights), inner_size) for piece in late]
        proj += [(core_own,)] + list(zip(core_early, core_late))
        base = places // inner_size * (2 * inner_size) + places % inner_size
        places = jnp.concatenate([base + core * inner_size, base + (1 - core) * inner_size])
    hidden, *normed = finish(
        mix, states, out_gate, head_gain, proj, places, residual_in, post_gain
    )
    bits = slots[0].shape[0].bit_length() - 1
    plain, turned = tuple(range(bits)), tuple((n + bits - 2) % bits for n in range(bits))
    plan = [[(0,)], [(0, 1)], [(0, 1, 2)], [(0, 1, 2), (3,)]]
    second = to_everyone(normed[1], turned, plan)
    first = to_everyone_early(normed[0], plain, [second[2][1]])
    tokens = [(0, *piece) for piece in first] + [(1, *piece) for piece in second]
    inner, spread = hidden_units(
        tokens, slots, (expert_gate, expert_up), (other_gate, other_up), capacity
    )
    sums, start, before = [], 0, ()
    for width, stages in ((512, plain), (512, plain), (512, turned), (512, plain)):
        keep, send = down_strips(
            inner, spread, expert_down, other_down, capacity, stages[::-1], start, width, before
        )
        before = before or (keep,)
        sums.append(sum_by_halving(keep, send, stages[::-1]))
        start += width
    return (hidden.astype(F32) + jnp.concatenate(sums, axis=1)).astype(BF16)


def core_stride(devices):
    first = getattr(devices[0], "coords", None)
    for i in range(1, len(devices)):
        if first is not None and tuple(devices[i].coords) == tuple(first):
            return i
    return 1


def solution(mesh):
    devices = mesh.devices.reshape(-1)
    inner = core_stride(devices)
    columns = mesh.shape["exp"]
    if 2 * inner <= columns:
        shape, column_axes = (-1, columns // (2 * inner), 2, inner), AXES[1:]
    else:
        shape, column_axes = (-1, 1, 2, inner), ("inner",)
    split_core = "core" in column_axes
    view = Mesh(devices.reshape(shape), AXES)
    rows = P(AXES, None)
    placed = (
        (rows,) * 7 + (P(), P(None, column_axes), P(), rows, rows) + (P(AXES, None, None),) * 3
    )
    body = functools.partial(shards, split_core)
    return jax.shard_map(body, mesh=view, in_specs=placed, out_specs=rows, check_vma=False)
```

```python
import functools

import jax
import jax.numpy as jnp
from jax import lax
from jax.experimental import pallas as pl
from jax.experimental.pallas import tpu as pltpu
from jax.sharding import Mesh, PartitionSpec as P

D = 2048
HK = 8
GROUP_VALUE_HEADS = 16
DK = 128
DV = 128
TOP = 10
HEADS_STEP = 4
BLOCKS_STEP = 16
GROUPS = (1536, 512)
STRIP = 256
EARLY_ROWS = 768

F32 = jnp.float32
BF16 = jnp.bfloat16
AXES = ("outer", "mid", "core", "inner")
SAME_CORE = ("outer", "mid", "inner")
REST = ("mid", "inner")
MIB = 1 << 20


def halves(x):
    high = x.astype(BF16)
    return high, (x - high.astype(F32)).astype(BF16)


def dot(a, b):
    return jnp.dot(a, b, preferred_element_type=F32)


def product(left, right):
    n = right[0].shape[1]
    lhs = jnp.concatenate(left, axis=1)
    top = jnp.concatenate(right, axis=1)
    bottom = jnp.concatenate([right[0], jnp.zeros_like(right[0])], axis=1)
    both = dot(lhs, jnp.concatenate([top, bottom], axis=0))
    return both[:, :n] + both[:, n:]


def local_kernel(q_ref, k_ref, v_ref, logs_ref, logs_row_ref, strength_row_ref, strength_ref, maps_ref, mix_ref):
    n = k_ref.shape[0]
    row = lax.broadcasted_iota(jnp.int32, (n, n), 0)
    column = lax.broadcasted_iota(jnp.int32, (n, n), 1)
    inclusive, strict, diagonal = row >= column, row > column, row == column
    heads = maps_ref.shape[0]
    group = GROUP_VALUE_HEADS // HK
    identity = diagonal.astype(F32)

    keys = []
    for i in range(heads // group):
        lanes = slice(i * DK, (i + 1) * DK)
        k_raw, q_raw = k_ref[:, lanes], q_ref[:, lanes]
        k_wide, q_wide = k_raw.astype(F32), q_raw.astype(F32)
        dims = (((1,), (1,)), ((), ()))
        gram = lax.dot_general(k_raw, k_raw, dims, preferred_element_type=F32)
        scores = lax.dot_general(q_raw, k_raw, dims, preferred_element_type=F32)
        inv_k = lax.rsqrt(jnp.sum(k_wide * k_wide, axis=1, keepdims=True) + 1e-06)
        inv_k_row = lax.rsqrt(jnp.sum(jnp.where(diagonal, gram, 0.0), axis=0, keepdims=True) + 1e-06)
        inv_q = lax.rsqrt(jnp.sum(q_wide * q_wide, axis=1, keepdims=True) + 1e-06) * DK ** (-0.5)
        keys.append(
            dict(
                k=k_raw,
                k_t=jnp.transpose(k_wide).astype(BF16),
                q=q_wide * inv_q,
                gram=gram * inv_k * inv_k_row,
                scores=scores * inv_q * inv_k_row,
                inv=inv_k,
                inv_row=inv_k_row,
            )
        )

    ratios, systems, inverses = [], [], []
    for j in range(heads):
        logs, logs_row = logs_ref[0][:, j : j + 1], logs_row_ref[0][j : j + 1, :]
        ratio = jnp.where(inclusive, jnp.exp(jnp.where(inclusive, logs - logs_row, 0.0)), 0.0)
        system = jnp.where(strict, ratio * keys[j // group]["gram"], 0.0) * strength_ref[0][:, j : j + 1]
        first = (row // 2 == column // 2) & strict
        ratios.append(ratio)
        systems.append(halves(system))
        inverses.append(identity - jnp.where(first, system, 0.0))
    size = 2
    while size < n:
        pairs = (row // (2 * size) == column // (2 * size)) & (row // size > column // size)
        inverse_halves = [halves(t) for t in inverses]
        cut = [
            tuple(jnp.where(pairs, part.astype(F32), 0.0).astype(BF16) for part in s) for s in systems
        ]
        left = [product(t, c) for t, c in zip(inverse_halves, cut)]
        inverses = [
            t - product(halves(x), th) for t, x, th in zip(inverses, left, inverse_halves)
        ]
        size *= 2

    for j in range(heads):
        key = keys[j // group]
        logs, logs_row = logs_ref[0][:, j : j + 1], logs_row_ref[0][j : j + 1, :]
        strength_row = strength_row_ref[0][j : j + 1, :]
        value = v_ref[:, j * DV : (j + 1) * DV]
        t = inverses[j]
        new_value = dot(
            jnp.concatenate(halves(t * strength_row), axis=1), jnp.concatenate([value, value], axis=0)
        )
        key_matrix = dot(
            jnp.concatenate(halves(t * (strength_row * jnp.exp(logs_row) * key["inv_row"])), axis=1),
            jnp.concatenate([key["k"], key["k"]], axis=0),
        )
        both = jnp.concatenate([key_matrix, new_value], axis=1)
        last = logs[n - 1 : n, :]
        faded = halves(both * (jnp.exp(last - logs) * key["inv"]))
        state = dot(
            jnp.concatenate([key["k_t"], key["k_t"]], axis=1), jnp.concatenate(faded, axis=0)
        )
        high, low = halves(jnp.exp(last) * identity - state[:, :DK])
        maps_ref[j, :, :DK] = high
        maps_ref[j, :, DK : 2 * DK] = low
        maps_ref[j, :, 2 * DK :] = state[:, DK:].astype(BF16)
        mixed = halves(ratios[j] * key["scores"])
        both_halves = halves(both)
        out = dot(
            jnp.concatenate(mixed, axis=1), jnp.concatenate([both_halves[0], both_halves[0]], axis=0)
        ) + dot(mixed[0], both_halves[1])
        mix_ref[j, :, :DK] = key["q"] * jnp.exp(logs) - out[:, :DK]
        mix_ref[j, :, DK:] = out[:, DK:]


def local_terms(query_input, key_input, value_input, write_strength, decay_rate):
    n = key_input.shape[0]
    groups, per_key = GROUP_VALUE_HEADS // HEADS_STEP, GROUP_VALUE_HEADS // HK
    lower = jnp.tril(jnp.ones((n, n), F32))
    logs = jnp.dot(lower, -decay_rate, precision=lax.Precision.HIGHEST)

    def columns(x):
        return jnp.swapaxes(x.reshape(n, groups, HEADS_STEP), 0, 1)

    def rows(x):
        return x.T.reshape(groups, HEADS_STEP, n)

    wide = HEADS_STEP // per_key * DK
    column_spec = pl.BlockSpec((1, n, HEADS_STEP), lambda i: (i, 0, 0))
    row_spec = pl.BlockSpec((1, HEADS_STEP, n), lambda i: (i, 0, 0))
    out_spec = pl.BlockSpec((HEADS_STEP, DK, 2 * DK + DV), lambda i: (i, 0, 0))
    mix_spec = pl.BlockSpec((HEADS_STEP, n, DK + DV), lambda i: (i, 0, 0))
    return pl.pallas_call(
        local_kernel,
        grid=(groups,),
        in_specs=[
            pl.BlockSpec((n, wide), lambda i: (0, i)),
            pl.BlockSpec((n, wide), lambda i: (0, i)),
            pl.BlockSpec((n, HEADS_STEP * DV), lambda i: (0, i)),
            column_spec,
            row_spec,
            row_spec,
            column_spec,
        ],
        out_specs=[out_spec, mix_spec],
        out_shape=[
            jax.ShapeDtypeStruct((GROUP_VALUE_HEADS, DK, 2 * DK + DV), BF16),
            jax.ShapeDtypeStruct((GROUP_VALUE_HEADS, n, DK + DV), F32),
        ],
        compiler_params=pltpu.CompilerParams(vmem_limit_bytes=40 * MIB),
        name="local_terms",
    )(
        query_input,
        key_input,
        value_input,
        columns(logs),
        rows(logs),
        rows(write_strength),
        columns(write_strength),
    )


def chain_kernel(maps_ref, *refs):
    *_, before_ref, whole_ref = refs
    row = lax.broadcasted_iota(jnp.int32, (DK, DK + DV), 0)
    column = lax.broadcasted_iota(jnp.int32, (DK, DK + DV), 1)
    passed = (row == column).astype(F32)
    for i in range(maps_ref.shape[0]):
        before_ref[i] = passed
        high, low = halves(passed)
        passed = dot(maps_ref[i, :, : 2 * DK], jnp.concatenate([high, high], axis=0)) + dot(
            maps_ref[i, :, :DK], low
        )
        passed = jnp.concatenate(
            [passed[:, :DK], passed[:, DK:] + maps_ref[i, :, 2 * DK :].astype(F32)], axis=1
        )
    whole_ref[...] = passed


def chain(maps, *others):
    count = maps.shape[0]
    return pl.pallas_call(
        chain_kernel,
        in_specs=[pl.BlockSpec(memory_space=pltpu.VMEM)]
        + [pl.BlockSpec(memory_space=pl.ANY)] * len(others),
        out_shape=[
            jax.ShapeDtypeStruct((count, DK, DK + DV), F32),
            jax.ShapeDtypeStruct((DK, DK + DV), F32),
        ],
        compiler_params=pltpu.CompilerParams(vmem_limit_bytes=40 * MIB),
        name="chain",
    )(maps, *others)


def tie_kernel(*refs):
    pass


def after(array, *others):
    anywhere = pl.BlockSpec(memory_space=pl.ANY)
    return pl.pallas_call(
        tie_kernel,
        in_specs=[anywhere] * (1 + len(others)),
        out_specs=anywhere,
        out_shape=jax.ShapeDtypeStruct(array.shape, array.dtype),
        input_output_aliases={0: 0},
        name="after",
    )(array, *others)


def entering_states(maps, devices, others, late, route):
    heads = maps.shape[0]
    segments = devices // heads
    groups = [[g * heads + h for h in range(heads)] for g in range(segments)]
    by_device = lax.all_to_all(
        maps, AXES, split_axis=0, concat_axis=0, axis_index_groups=groups, tiled=True
    )
    before, whole = chain(by_device, *others)
    if segments == 2:
        start = lax.ppermute(whole[:, DK:], AXES, [(h, heads + h) for h in range(heads)])
    else:
        across = [[g * heads + h for g in range(segments)] for h in range(heads)]
        adds = lax.all_gather(whole[:, DK:], AXES, axis_index_groups=across)
        steps = lax.all_gather(whole[:, :DK], AXES, axis_index_groups=across)
        segment = lax.axis_index(AXES) // heads
        carry = adds[0]
        start = jnp.where(segment == 1, carry, 0.0)
        for g in range(2, segments):
            carry = adds[g - 1] + jnp.dot(steps[g - 1], carry, precision=lax.Precision.HIGHEST)
            start = jnp.where(segment == g, carry, start)
    served = route(whole)
    start = after(start, *late, served)
    states = (
        jnp.dot(
            before[:, :, :DK].reshape(heads * DK, DK), start, precision=lax.Precision.HIGH
        ).reshape(heads, DK, DV)
        + before[:, :, DK:]
    ).astype(BF16)
    back = lax.all_to_all(
        states, AXES, split_axis=0, concat_axis=0, axis_index_groups=groups, tiled=True
    )
    return back, served


def finish_kernel(
    parts, place_ref, mix_ref, state_ref, gate_ref, gain_ref, residual_ref, post_ref, *refs
):
    *proj_refs, hidden_ref, first_ref, second_ref, core_ref = refs
    for h in range(GROUP_VALUE_HEADS):
        lanes = slice(h * DV, (h + 1) * DV)
        state = state_ref[h]
        recurrent = (
            dot(
                jnp.concatenate(halves(mix_ref[h, :, :DK]), axis=1),
                jnp.concatenate([state, state], axis=0),
            )
            + mix_ref[h, :, DK:]
        )
        inv_rms = lax.rsqrt(jnp.mean(recurrent * recurrent, axis=1, keepdims=True) + 1e-06)
        gate = gate_ref[:, lanes].astype(F32)
        act = gate / (1.0 + jnp.exp(-gate))
        core_ref[:, lanes] = (recurrent * inv_rms * gain_ref[...] * act).astype(BF16)
    core = core_ref[...]
    squares = 0.0
    proj_refs = list(proj_refs)
    for i, count in enumerate(parts):
        refs, proj_refs = proj_refs[:count], proj_refs[count:]
        wide = refs[0].shape[1]
        lanes = pl.ds(pl.multiple_of(place_ref[i] * wide, wide), wide)
        mixed, first = residual_ref[:, lanes].astype(F32), 0
        for ref in refs:
            mixed += dot(core[:, first : first + ref.shape[0]], ref[...])
            first += ref.shape[0]
        hidden = mixed.astype(BF16)
        hidden_ref[:, lanes] = hidden
        widened = hidden.astype(F32)
        squares += jnp.sum(widened * widened, axis=1, keepdims=True)
    inv_rms = lax.rsqrt(squares * (1.0 / D) + 1e-06)
    normed = (hidden_ref[...].astype(F32) * inv_rms * post_ref[...]).astype(BF16)
    start = 0
    for ref, width in zip((first_ref, second_ref), GROUPS):
        ref[...] = normed[:, start : start + width]
        start += width


def finish(mix, states, out_gate, head_gain, proj, places, residual_in, post_gain):
    shape = residual_in.shape
    vmem = pl.BlockSpec(memory_space=pltpu.VMEM)
    flat = [part for piece in proj for part in piece]
    return pl.pallas_call(
        functools.partial(finish_kernel, [len(piece) for piece in proj]),
        in_specs=[pl.BlockSpec(memory_space=pltpu.SMEM)] + [vmem] * (6 + len(flat)),
        out_shape=[
            jax.ShapeDtypeStruct((shape[0], wide), BF16) for wide in (D,) + GROUPS
        ],
        scratch_shapes=[pltpu.VMEM(shape, BF16)],
        compiler_params=pltpu.CompilerParams(vmem_limit_bytes=48 * MIB),
        name="finish",
    )(
        places,
        mix,
        states,
        out_gate,
        head_gain.reshape(1, DV),
        residual_in,
        post_gain.reshape(1, D),
        *flat,
    )


def hidden_units_kernel(
    capacity,
    pieces,
    slot_row_ref,
    slot_ref,
    weight_ref,
    own_gate_ref,
    own_up_ref,
    other_gate_ref,
    other_up_ref,
    *refs,
):
    *token_refs, inner_ref, spread_ref, block_ref, taken_ref, sems = refs
    group, expert = pl.program_id(0), pl.program_id(1)
    blocks, rows, _ = block_ref.shape
    served = taken_ref.shape[0]
    joined = max(1, 16 // capacity)

    def copies(step, b):
        found = []
        start = 0
        for part, width in enumerate(GROUPS):
            for ref, (column, places) in zip(token_refs, pieces):
                place = step * blocks + b
                if column == part and place in places:
                    found.append(
                        pltpu.make_async_copy(
                            ref.at[places.index(place)],
                            block_ref.at[b, :, start : start + width],
                            sems.at[b, part],
                        )
                    )
            start += width
        return found

    def load(step):
        @pl.when((expert == 0) & (group == step))
        def _():
            for b in range(blocks):
                for copy in copies(step, b):
                    copy.start()

    for step in range(sum(len(places) for column, places in pieces if column == 0) // blocks):
        load(step)

    @pl.when(expert == 0)
    def _():
        slot_ids = lax.broadcasted_iota(jnp.int32, (capacity, rows), 0).astype(F32)
        for first in range(0, blocks, joined):
            picked = []
            for b in range(first, first + joined):
                chosen = jnp.concatenate(
                    [(slot_row_ref[b, e : e + 1, :] == slot_ids).astype(F32) for e in range(served)],
                    axis=0,
                ).astype(BF16)
                for copy in copies(0, b):
                    copy.wait()
                picked.append(dot(chosen, block_ref[b]))
            for e in range(served):
                part = [p[e * capacity : (e + 1) * capacity] for p in picked]
                taken_ref[e, first * capacity : (first + joined) * capacity] = jnp.concatenate(
                    part, axis=0
                ).astype(BF16)

    def serve(gate_ref, up_ref):
        received = taken_ref[expert]
        gate = dot(received, gate_ref[0])
        up = dot(received, up_ref[0])
        inner_ref[0] = (gate / (1.0 + jnp.exp(-gate)) * up).astype(BF16)

    @pl.when(expert < served // 2)
    def _():
        serve(own_gate_ref, own_up_ref)

    @pl.when(expert >= served // 2)
    def _():
        serve(other_gate_ref, other_up_ref)

    span = served * capacity
    lane = lax.broadcasted_iota(jnp.int32, (rows, 2 * span), 1)
    lane_expert, lane_slot = lane // capacity % served, (lane % capacity).astype(F32)
    share = blocks // served
    for i in range(share):
        b = expert * share + i
        slots, weights = slot_ref[b], weight_ref[b]
        slot = jnp.full((rows, 2 * span), -1.0, F32)
        weight = jnp.zeros((rows, 2 * span), F32)
        for e in range(served):
            slot = jnp.where(lane_expert == e, slots[:, e : e + 1], slot)
            weight = jnp.where(lane_expert == e, weights[:, e : e + 1], weight)
        high = weight.astype(BF16).astype(F32)
        spread_ref[b] = jnp.where(
            slot == lane_slot, jnp.where(lane < span, high, weight - high), 0.0
        ).astype(BF16)


def hidden_units(tokens, slots, own, other, capacity):
    devices, served, rows = slots[0].shape
    local = own[0].shape[0]
    width = own[0].shape[2]
    pieces = [(column, places) for column, places, _ in tokens]
    def own_spec(x):
        return pl.BlockSpec((1,) + x.shape[1:], lambda g, e: (jnp.minimum(e, local - 1), 0, 0))

    def other_spec(x):
        return pl.BlockSpec((1,) + x.shape[1:], lambda g, e: (jnp.maximum(e - local, 0), 0, 0))

    column_spec = pl.BlockSpec((BLOCKS_STEP, rows, served), lambda g, e: (g, 0, 0))
    return pl.pallas_call(
        functools.partial(hidden_units_kernel, capacity, pieces),
        grid=(devices // BLOCKS_STEP, served),
        in_specs=[
            pl.BlockSpec((BLOCKS_STEP, served, rows), lambda g, e: (g, 0, 0)),
            column_spec,
            column_spec,
        ]
        + [own_spec(x) for x in own]
        + [other_spec(x) for x in other]
        + [pl.BlockSpec(memory_space=pl.ANY)] * len(tokens),
        out_specs=[
            pl.BlockSpec((1, BLOCKS_STEP * capacity, width), lambda g, e: (e, g, 0)),
            pl.BlockSpec((BLOCKS_STEP, rows, 2 * served * capacity), lambda g, e: (g, 0, 0)),
        ],
        out_shape=[
            jax.ShapeDtypeStruct((served, devices * capacity, width), BF16),
            jax.ShapeDtypeStruct((devices, rows, 2 * served * capacity), BF16),
        ],
        scratch_shapes=[
            pltpu.VMEM((BLOCKS_STEP, rows, D), BF16),
            pltpu.VMEM((served, BLOCKS_STEP * capacity, D), BF16),
            pltpu.SemaphoreType.DMA((BLOCKS_STEP, len(GROUPS))),
        ],
        compiler_params=pltpu.CompilerParams(vmem_limit_bytes=56 * MIB),
        name="hidden_units",
    )(
        *slots,
        *own,
        *other,
        *[array for _, _, array in tokens],
    )


def order_places(order):
    count = len(order)
    return [
        sum(((j >> (count - 1 - k)) & 1) << bit for k, bit in enumerate(order))
        for j in range(1 << count)
    ]


def down_kernel(capacity, order, inner_ref, spread_ref, own_ref, other_ref, *refs):
    *_, keep_ref, send_ref, out_ref = refs
    served = inner_ref.shape[0]
    local = served // 2
    for e in range(served):
        down = own_ref[e] if e < local else other_ref[e - local]
        out_ref[e] = dot(inner_ref[e], down)
    places = order_places(order)
    half = len(places) // 2
    for j, place in enumerate(places):
        mine = [out_ref[e, place * capacity : (place + 1) * capacity] for e in range(served)]
        stacked = jnp.concatenate(mine, axis=0).astype(BF16)
        block = dot(spread_ref[place], jnp.concatenate([stacked, stacked], axis=0)).astype(BF16)
        if j < half:
            keep_ref[j] = block
        else:
            send_ref[j - half] = block


def down_strips(inner, spread, own, other, capacity, order, start, width, before):
    served, slots, units = inner.shape
    devices, rows, _ = spread.shape
    first = start // STRIP

    def whole(x):
        return pl.BlockSpec(x.shape, lambda i: (0, 0, 0), pipeline_mode=pl.Buffered(1))

    down_spec = pl.BlockSpec((own.shape[0], units, STRIP), lambda i: (0, 0, first + i))
    half_spec = pl.BlockSpec((devices // 2, rows, STRIP), lambda i: (0, 0, i))
    half_shape = jax.ShapeDtypeStruct((devices // 2, rows, width), BF16)
    return pl.pallas_call(
        functools.partial(down_kernel, capacity, order),
        grid=(width // STRIP,),
        in_specs=[whole(inner), whole(spread), down_spec, down_spec]
        + [pl.BlockSpec(memory_space=pl.ANY)] * len(before),
        out_specs=[half_spec, half_spec],
        out_shape=[half_shape, half_shape],
        scratch_shapes=[pltpu.VMEM((served, slots, STRIP), F32)],
        compiler_params=pltpu.CompilerParams(vmem_limit_bytes=48 * MIB),
        name="down_strips",
    )(inner, spread, own, other, *before)


def sum_by_halving(keep, send, stages):
    for stage in stages[:-1]:
        total = (keep.astype(F32) + stage_flip(send, stage).astype(F32)).astype(BF16)
        half = total.shape[0] // 2
        keep, send = total[:half], total[half:]
    return keep[0].astype(F32) + stage_flip(send, stages[-1])[0].astype(F32)


def routing(expert_ids, gate_weights, local_experts):
    outer, cores, inner = (lax.axis_size(a) for a in (("outer", "mid"), "core", "inner"))
    rows = expert_ids.shape[0]
    experts = local_experts * outer * cores * inner
    chosen = expert_ids.T[None] == jnp.arange(experts, dtype=jnp.int32)[:, None, None]
    dense = jnp.sum(jnp.where(chosen, gate_weights.T[None], 0.0), axis=1)
    by_chip = jnp.swapaxes(dense.reshape(outer, cores, inner, local_experts * rows), 1, 2)
    by_chip = by_chip.reshape(outer * inner, cores * local_experts, rows)
    return lax.all_to_all(by_chip, SAME_CORE, split_axis=0, concat_axis=0, tiled=True)


def positions(weights, local_experts):
    rows = weights.shape[2]
    turned = jnp.concatenate([weights[:, local_experts:], weights[:, :local_experts]], axis=1)
    weights = jnp.where(lax.axis_index("core") == 1, turned, weights)
    bits = weights.shape[0].bit_length() - 1
    table = jnp.asarray([order_places(order[::-1]) for order in core_orders(bits)], jnp.int32)
    source = lax.axis_index(SAME_CORE) ^ table[lax.axis_index("core")]
    weights = jnp.take(weights, source, axis=0, mode="clip")
    named = weights > 0.0
    rank = jnp.einsum(
        "set,tu->seu",
        named.astype(BF16),
        jnp.triu(jnp.ones((rows, rows), BF16)),
        preferred_element_type=F32,
    )
    slots = jnp.where(named, rank - 1.0, -1.0)
    return slots, jnp.swapaxes(slots, 1, 2), jnp.swapaxes(weights, 1, 2)


def core_orders(bits):
    first = tuple(range(bits))[::-1]
    second = tuple(first[n ^ 1] if n ^ 1 < bits else first[n] for n in range(bits))
    return first, second


def flipped(array, bit):
    devices = lax.axis_size(AXES)
    return lax.ppermute(array, AXES, [(i, i ^ bit) for i in range(devices)])


def place_flip(array, bit):
    return flipped(array, 1 << (bit if 1 << bit < lax.axis_size("inner") else bit + 1))


def over_rest(array):
    pieces = [array]
    for bit in range(lax.axis_size(REST).bit_length() - 1):
        pieces = pieces + [place_flip(piece, bit) for piece in pieces]
    return pieces


def stage_flip(array, stage):
    inner, devices = lax.axis_size("inner"), lax.axis_size(AXES)
    bits = lax.axis_size(SAME_CORE).bit_length() - 1

    def partner(i):
        bit = core_orders(bits)[i // inner % 2][stage]
        return i ^ (1 << (bit if 1 << bit < inner else bit + 1))

    return lax.ppermute(array, AXES, [(i, partner(i)) for i in range(devices)])


def send_on(pieces, chosen, stage):
    picked = [pieces[i] for i in chosen]
    places = sum((places for places, _ in picked), ())
    joined = jnp.concatenate([piece for _, piece in picked], axis=0)
    return tuple(place | (1 << stage) for place in places), stage_flip(joined, stage)


def to_everyone(array, stages, plan):
    pieces = [((0,), array[None])]
    for step, stage in enumerate(stages):
        chosen = plan[step] if step < len(plan) else [range(len(pieces))]
        pieces = pieces + [send_on(pieces, group, stage) for group in chosen]
    return pieces


def to_everyone_early(array, stages, others):
    pieces = [((0,), array[None])]
    pieces += [send_on(pieces, (0,), stage) for stage in (stages[0], stages[2], stages[3])]
    joined = jnp.concatenate([pieces[0][1], pieces[1][1]], axis=0)
    joined = after(joined, pieces[2][1], pieces[3][1], *others)
    both = [(pieces[0][0] + pieces[1][0], joined)]
    pieces.append(send_on(both, (0,), stages[1]))
    pieces += [send_on(pieces, (i,), stages[2]) for i in (1, 4)]
    pieces += [send_on(pieces, group, stages[3]) for group in ((1,), (4,), (2, 5), (6,))]
    for stage in stages[4:]:
        pieces = pieces + [send_on(pieces, range(len(pieces)), stage)]
    return pieces


def shards(
    split_core,
    residual_in,
    query_input,
    key_input,
    value_input,
    out_gate,
    write_strength,
    decay_rate,
    head_gain,
    out_proj,
    post_gain,
    expert_ids,
    gate_weights,
    expert_gate,
    expert_up,
    expert_down,
):
    tok_rows = residual_in.shape[0]
    devices = lax.axis_size(AXES)
    inner_size = lax.axis_size("inner")
    local_experts = expert_gate.shape[0]
    capacity = max(2, tok_rows * TOP * 8 // (5 * local_experts * devices))
    late_rows = out_proj[EARLY_ROWS:]
    early = over_rest(out_proj[:EARLY_ROWS])[1:]
    other_gate, other_up, other_down = (
        flipped(x, inner_size) for x in (expert_gate, expert_up, expert_down)
    )
    maps, mix = local_terms(query_input, key_input, value_input, write_strength, decay_rate)
    ready = [*early, late_rows, other_gate, other_up, other_down]
    others = []
    if split_core:
        core_own = flipped(out_proj, inner_size)
        core_early = [flipped(piece, inner_size) for piece in early]
        ready, others = ready + [core_own], core_early
    maps = after(maps, *ready)
    late = over_rest(after(late_rows, *early))[1:]

    def route(whole):
        return routing(after(expert_ids, whole), gate_weights, local_experts)

    states, served_weights = entering_states(maps, devices, others, late, route)
    slots = positions(served_weights, local_experts)
    proj = [(out_proj,)] + list(zip(early, late))
    places = lax.axis_index(REST) ^ jnp.arange(len(proj), dtype=jnp.int32)
    if split_core:
        core = lax.axis_index("core")
        core_late = [flipped(after(piece, served_weights), inner_size) for piece in late]
        proj += [(core_own,)] + list(zip(core_early, core_late))
        base = places // inner_size * (2 * inner_size) + places % inner_size
        places = jnp.concatenate([base + core * inner_size, base + (1 - core) * inner_size])
    hidden, *normed = finish(
        mix, states, out_gate, head_gain, proj, places, residual_in, post_gain
    )
    bits = slots[0].shape[0].bit_length() - 1
    plain, turned = tuple(range(bits)), tuple((n + bits - 2) % bits for n in range(bits))
    plan = [[(0,)], [(0, 1)], [(0, 1, 2)], [(0, 1, 2), (3,)]]
    second = to_everyone(normed[1], turned, plan)
    first = to_everyone_early(normed[0], plain, [second[2][1]])
    tokens = [(0, *piece) for piece in first] + [(1, *piece) for piece in second]
    inner, spread = hidden_units(
        tokens, slots, (expert_gate, expert_up), (other_gate, other_up), capacity
    )
    sums, start, before = [], 0, ()
    for width, stages in ((512, plain), (512, plain), (512, plain), (512, turned)):
        keep, send = down_strips(
            inner, spread, expert_down, other_down, capacity, stages[::-1], start, width, before
        )
        before = before or (keep,)
        sums.append(sum_by_halving(keep, send, stages[::-1]))
        start += width
    return (hidden.astype(F32) + jnp.concatenate(sums, axis=1)).astype(BF16)


def core_stride(devices):
    first = getattr(devices[0], "coords", None)
    for i in range(1, len(devices)):
        if first is not None and tuple(devices[i].coords) == tuple(first):
            return i
    return 1


def solution(mesh):
    devices = mesh.devices.reshape(-1)
    inner = core_stride(devices)
    columns = mesh.shape["exp"]
    if 2 * inner <= columns:
        shape, column_axes = (-1, columns // (2 * inner), 2, inner), AXES[1:]
    else:
        shape, column_axes = (-1, 1, 2, inner), ("inner",)
    split_core = "core" in column_axes
    view = Mesh(devices.reshape(shape), AXES)
    rows = P(AXES, None)
    placed = (
        (rows,) * 7 + (P(), P(None, column_axes), P(), rows, rows) + (P(AXES, None, None),) * 3
    )
    body = functools.partial(shards, split_core)
    return jax.shard_map(body, mesh=view, in_specs=placed, out_specs=rows, check_vma=False)
```
